256 devices in a mesh: bin: 16 (over z_lo, x), coil: 16 (over y, z_hi, core).
Axes of the slice: x: 4, y: 4, z: 8 (z_hi: 2, z_lo: 4; z = z_hi * 4 + z_lo), core: 2. Of those that a mesh axis runs over, the one named last changes fastest.
Arguments:
- kspace: float32 [32, 32, 4, 2, 96, 256], P('bin', 'coil'), may hold values from -6 to 6
- coil_maps: float32 [32, 4, 2, 96, 256], P('coil'), may hold values from -1 to 1
- sample_mask: int32 [32, 96, 256], P('bin'), may hold values from 0 to 1, as said below
Outputs:
- image: float32 [32, 4, 2, 96, 256], P('bin')
The draws below stay inside these ranges and needn't reach their ends.
Inputs may be any that keep to these rules, and one draw needn't show every extreme that they name: `sample_mask`: 0/1 entries; the share of sampled lines differs from bin to bin.
All inputs are finite; a program needn't handle non-finite values.
Results may differ from the reference program's by a relative error of at most 0.0015.
Values sent between devices are 32-bit elements; how exact they have to be, the bound alone decides.
A program may use at most 64 MiB of HBM per device.

```python
import jax
import jax.numpy as jnp
from jax import lax

NY = 256
NZ = 96
SL = 4
ITERS = 2
BINS = 32
COILS = 32


def draw_sample_mask(key, part):
    key = jax.random.fold_in(key, 11)
    key_level, key_ticket = jax.random.split(key)
    level = jax.random.randint(key_level, (BINS, 1, 1), 150, 700)
    ticket = jax.random.randint(key_ticket, (BINS, NZ, NY), 0, 1000)
    return (ticket < level).astype(jnp.int32)


def block_scale(stream_key, extent, shards, smallest, largest):
    level, own = 1.0, jax.random.fold_in(stream_key, 6)
    for position, blocks in shards:
        draws = jnp.exp(jax.random.uniform(jax.random.fold_in(own, position), (blocks,), jnp.float32, smallest / len(shards), largest / len(shards)))
        level = level * jnp.repeat(draws, extent[position] // blocks).reshape([-1 if axis == position else 1 for axis in range(len(extent))])
    return level


def noise(key, extent, spread, limit, cuts=(), dtype=jnp.bfloat16):
    factor_of = block_scale(key, extent, cuts, -0.22, 0.18) if cuts else 1.0
    array = jax.random.normal(key, extent, jnp.float32) * spread * factor_of
    return jnp.minimum(jnp.maximum(array, -limit), limit).astype(dtype)


def setup_inputs(seed: int = 0) -> dict:
    keys = jax.random.split(jax.random.key(seed), 4)
    return {
        "kspace": noise(keys[0], (BINS, COILS, SL, 2, NZ, NY), 1.0, 6.0, ((0, 16), (1, 16)), jnp.float32),
        "coil_maps": noise(keys[1], (COILS, SL, 2, NZ, NY), COILS ** -0.5, 1.0, ((0, 16),), jnp.float32),
        "sample_mask": draw_sample_mask(jax.random.fold_in(keys[3], 71), 0),
    }


def reference(kspace, coil_maps, sample_mask):
    sens = coil_maps[:, :, 0] + 1j * coil_maps[:, :, 1]
    masks = sample_mask.astype(jnp.float32)
    data = kspace[:, :, :, 0] + 1j * kspace[:, :, :, 1]

    def to_real(values):
        return jnp.stack([jnp.real(values), jnp.imag(values)], axis=1).astype(jnp.float32)

    def adjoint_bin(inputs):
        data_b, mask_b = inputs
        wave = jnp.fft.ifft2(data_b * mask_b, axes=(-2, -1), norm='ortho')
        return to_real(lax.optimization_barrier(jnp.sum(jnp.conj(sens) * wave, axis=0)))

    def normal_bin(inputs):
        field, mask_b = inputs
        values = field[:, 0] + 1j * field[:, 1]
        spectra = jnp.fft.fft2(sens * values[None], axes=(-2, -1), norm='ortho') * mask_b
        wave = jnp.fft.ifft2(spectra, axes=(-2, -1), norm='ortho')
        return to_real(lax.optimization_barrier(jnp.sum(jnp.conj(sens) * wave, axis=0))) + 0.1 * field
    rhs = lax.map(adjoint_bin, (data, masks))
    solution = jnp.zeros_like(rhs)
    resid = rhs
    direction = rhs
    norm_now = jnp.sum(resid * resid)
    for step in range(ITERS):
        image_dir = lax.map(normal_bin, (direction, masks))
        alpha = norm_now / jnp.sum(direction * image_dir)
        solution = solution + alpha * direction
        if step + 1 < ITERS:
            resid = resid - alpha * image_dir
            norm_next = jnp.sum(resid * resid)
            direction = resid + norm_next / norm_now * direction
            norm_now = norm_next
    zero_bin = jnp.zeros_like(solution[:1])
    diff = jnp.concatenate([solution[1:] - solution[:-1], zero_bin], axis=0)
    magnitude = jnp.sqrt(diff[:, :, 0] * diff[:, :, 0] + diff[:, :, 1] * diff[:, :, 1])
    count = (BINS - 1) * SL * NZ * NY
    lam = 1.0 * jnp.sum(magnitude) / count + 1e-06
    dual = diff * (lam / jnp.maximum(magnitude, lam))[:, :, None]
    prior = jnp.concatenate([zero_bin, dual[:-1]], axis=0)
    return solution + 0.25 * (dual - prior)
```

```python
import math

import jax
import jax.numpy as jnp
import numpy as np
from jax import lax
from jax.experimental import pallas as pl
from jax.experimental.pallas import tpu as pltpu
from jax.sharding import PartitionSpec as P

MESH = pl.DeviceIdType.MESH
F32 = jnp.float32
BF16 = jnp.bfloat16
NZ, NY, SL = 96, 256, 4
BIN_AXIS, COIL_AXIS = 16, 16
BINS = 32
COUNT = (BINS - 1) * SL * NZ * NY
PLANE = (2, NZ, NY)


def dft_tables(length):
    index = np.arange(length)
    angle = (index[:, None] * index[None, :] % length) * (2.0 * math.pi / length)
    factor = 1.0 / math.sqrt(length)
    return np.cos(angle) * factor, np.sin(angle) * factor


def halves(table):
    high = table.astype(np.float32).astype(jnp.bfloat16)
    low = (table - high.astype(np.float64)).astype(np.float32).astype(jnp.bfloat16)
    return np.stack([high, low])


def row_tables():
    cos, sin = dft_tables(NY)
    forward = np.block([[cos, -sin], [sin, cos]])
    return np.stack([halves(forward), halves(forward.T)])


def col_tables():
    cos, sin = dft_tables(NZ)
    forward = np.block([[cos, sin], [-sin, cos]])
    return np.stack([halves(forward), halves(forward.T)])


def split(values):
    high = values.astype(BF16)
    return high, (values - high.astype(F32)).astype(BF16)


def dot(left, right):
    return jnp.dot(left, right, preferred_element_type=F32)


def rows(high, low, table, which):
    return dot(high, table[which, 0]) + dot(low, table[which, 0]) + dot(high, table[which, 1])


def cols(values, table, which):
    high, low = split(values)
    return dot(table[which, 0], high) + dot(table[which, 0], low) + dot(table[which, 1], high)


def fold(values):
    part = jnp.sum(values.reshape(values.shape[0] // 8, 8, NY), axis=0)
    return part[:, :128] + part[:, 128:]


def total(values):
    return jnp.sum(values, keepdims=True)


def kernel(
    kspace, coil_maps, mask, row_table, col_table, out,
    maps, weight, high, low, mid, part, from_sib, to_y, from_y, to_z, from_z,
    rhs, quad, resid, image, near_rhs, near_resid, message, sums,
    map_send, map_recv, map_sib_send, map_sib_recv, map_local,
    sib_send, sib_recv, y_send, y_recv, z_send, z_recv,
    near_send, near_recv, sum_send, sum_recv,
    out_send, out_recv, out_sib_send, out_sib_recv, out_local,
):
    b = lax.axis_index("bin")
    j = lax.axis_index("coil")
    y, z, c = j // 4, (j // 2) % 2, j % 2

    def at_y(step):
        return (b, lax.rem(y + step, 4) * 4 + z * 2 + c)

    sibling = (b, j + 1 - 2 * c)
    opposite = (b, j + 2 - 4 * z)
    across = (lax.rem(b + 2 * c - 1 + BIN_AXIS, BIN_AXIS), j + 1 - 2 * c)

    def send(source, target, send_sem, recv_sem, device):
        copy = pltpu.make_async_remote_copy(
            src_ref=source, dst_ref=target, send_sem=send_sem, recv_sem=recv_sem,
            device_id=device, device_id_type=MESH,
        )
        copy.start()
        return copy

    barrier = pltpu.get_barrier_semaphore()
    for step in range(1, COIL_AXIS):
        pl.semaphore_signal(barrier, inc=1, device_id=(b, lax.rem(j + step, COIL_AXIS)), device_id_type=MESH)
    for step in range(1, BIN_AXIS):
        pl.semaphore_signal(barrier, inc=1, device_id=(lax.rem(b + step, BIN_AXIS), j), device_id_type=MESH)
    pl.semaphore_signal(barrier, inc=1, device_id=across, device_id_type=MESH)
    pl.semaphore_wait(barrier, COIL_AXIS + BIN_AXIS - 1)

    own_maps = pltpu.make_async_copy(coil_maps.at[:, y], maps.at[0, c], map_local)
    own_maps.start()
    map_copies = [
        send(coil_maps.at[:, lax.rem(y + step, 4)], maps.at[4 - step, c],
             map_send.at[step - 1], map_recv.at[4 - step - 1], at_y(step))
        for step in (1, 2, 3)
    ]
    sib_maps = [send(coil_maps.at[:, y], maps.at[0, c], map_sib_send.at[0], map_sib_recv.at[0], sibling)]

    weight[0] = mask[0].astype(F32)
    weight[1] = mask[1].astype(F32)

    def sib_copy(k):
        return pltpu.make_async_remote_copy(
            src_ref=part.at[k, 1 - c], dst_ref=from_sib.at[k],
            send_sem=sib_send.at[k], recv_sem=sib_recv.at[k],
            device_id=sibling, device_id_type=MESH,
        )

    def y_copy(k):
        return pltpu.make_async_remote_copy(
            src_ref=to_y.at[k], dst_ref=from_y.at[k],
            send_sem=y_send.at[k], recv_sem=y_recv.at[k],
            device_id=at_y(3 - k), device_id_type=MESH,
        )

    def adjoint(k, carry):
        s = lax.rem(y + 3 - k, 4)
        for t in range(4):
            w = weight[t // 2]
            values = jnp.concatenate(
                [kspace[t // 2, t % 2, s, 0] * w, kspace[t // 2, t % 2, s, 1] * w], axis=1
            )
            high[t * NZ:(t + 1) * NZ], low[t * NZ:(t + 1) * NZ] = split(values)
        mid[...] = rows(high[...], low[...], row_table, 1)
        for bin_ in range(2):
            sum_re, sum_im = 0.0, 0.0
            for coil in range(2):
                at = pl.ds((bin_ * 2 + coil) * NZ, NZ)
                wave = cols(jnp.concatenate([mid[at, :NY], mid[at, NY:]], axis=0), col_table, 1)
                sens_re, sens_im = coil_maps[coil, s, 0], coil_maps[coil, s, 1]
                sum_re += sens_re * wave[:NZ] + sens_im * wave[NZ:]
                sum_im += sens_re * wave[NZ:] - sens_im * wave[:NZ]
            part[k, bin_, 0] = sum_re
            part[k, bin_, 1] = sum_im
        sib_copy(k).start()

        @pl.when(k > 0)
        def _():
            sib_copy(k - 1).wait_recv()
            to_y[k - 1] = part[k - 1, c] + from_sib[k - 1]
            y_copy(k - 1).start()

        return carry

    lax.fori_loop(0, 4, adjoint, 0)
    sib_copy(3).wait_recv()
    own = part[3, c] + from_sib[3]
    for k in range(3):
        y_copy(k).wait_recv()
        own = own + from_y[k]
    to_z[0] = own
    z_copy = send(to_z.at[0], from_z.at[0], z_send.at[0], z_recv.at[0], opposite)
    own_maps.wait()
    for slot in (1, 2, 3):
        map_copies[3 - slot].wait_recv()
        sib_maps.append(
            send(maps.at[slot, c], maps.at[slot, c], map_sib_send.at[slot], map_sib_recv.at[slot], sibling)
        )
    z_copy.wait()
    rhs[...] = to_z[0] + from_z[0]
    near = [
        send(rhs, near_rhs.at[0], near_send.at[0], near_recv.at[0], sibling),
        send(rhs, near_rhs.at[1], near_send.at[1], near_recv.at[1], across),
    ]
    for copy in sib_maps:
        copy.wait_recv()

    def spectra(n, field, t):
        sens_re, sens_im = maps[n, t // 2, t % 2, 0], maps[n, t // 2, t % 2, 1]
        values = jnp.concatenate(
            [sens_re * field[0] - sens_im * field[1], sens_re * field[1] + sens_im * field[0]], axis=1
        )
        high[t * NZ:(t + 1) * NZ], low[t * NZ:(t + 1) * NZ] = split(values)

    def masked(t):
        at = pl.ds(t * NZ, NZ)
        values = cols(jnp.concatenate([mid[at, :NY], mid[at, NY:]], axis=0), col_table, 0)
        w = weight[c]
        return values * jnp.concatenate([w, w], axis=0)

    def normal(n, energy):
        for t in range(4):
            spectra(n, rhs, t)
        mid[...] = rows(high[...], low[...], row_table, 0)
        for t in range(4):
            values = masked(t)
            energy = energy + fold(values * values)
            wave = cols(values, col_table, 1)
            wave = jnp.concatenate([wave[:NZ], wave[NZ:]], axis=1)
            high[t * NZ:(t + 1) * NZ], low[t * NZ:(t + 1) * NZ] = split(wave)
        mid[...] = rows(high[...], low[...], row_table, 1)
        sum_re, sum_im = to_z[1, 0], to_z[1, 1]
        for t in range(4):
            at = pl.ds(t * NZ, NZ)
            sens_re, sens_im = maps[n, t // 2, t % 2, 0], maps[n, t // 2, t % 2, 1]
            sum_re += sens_re * mid[at, :NY] + sens_im * mid[at, NY:]
            sum_im += sens_re * mid[at, NY:] - sens_im * mid[at, :NY]
        to_z[1, 0] = sum_re
        to_z[1, 1] = sum_im
        return energy

    def forward(n, energy):
        for t in range(4):
            spectra(n, resid, t)
        mid[...] = rows(high[...], low[...], row_table, 0)
        for t in range(4):
            values = masked(t)
            energy = energy + fold(values * values)
        return energy

    def inner(left, right):
        return fold(left[0] * right[0] + left[1] * right[1])

    def reduce_all(which, parts):
        for n, value in enumerate(parts):
            message[which, 0, n] = value
        for stage in range(2):
            me, size = ((j, COIL_AXIS), (b, BIN_AXIS))[stage]
            used = pl.ds(0, len(parts))
            slots = sums.at[which, stage, :, used]
            copies = []
            for step in range(1, size):
                peer = lax.rem(me + step, size)
                copies.append(
                    send(message.at[which, stage, used], sums.at[which, stage, me, used],
                         sum_send.at[which, stage, step - 1], sum_recv.at[which, stage, step - 1],
                         ((b, peer), (peer, j))[stage])
                )
            sums[which, stage, me, used] = message[which, stage, used]
            for copy in copies:
                copy.wait()
            message[which, stage + 1, used] = jnp.sum(slots[...], axis=0)
        return [total(message[which, 2, n]) for n in range(len(parts))]

    zero = jnp.zeros((8, 128), F32)
    to_z[1] = jnp.zeros(PLANE, F32)
    energy = lax.fori_loop(0, 4, normal, zero)
    z_copy = send(to_z.at[1], from_z.at[1], z_send.at[1], z_recv.at[1], opposite)
    norm_0, energy_0 = reduce_all(0, [0.5 * inner(rhs, rhs), energy])
    curve_0 = energy_0 + 0.1 * norm_0
    alpha_0 = norm_0 / curve_0
    z_copy.wait()
    quad[...] = to_z[1] + from_z[1] + 0.1 * rhs[...]
    resid[...] = rhs[...] - alpha_0 * quad[...]
    near += [
        send(resid, near_resid.at[0], near_send.at[2], near_recv.at[2], sibling),
        send(resid, near_resid.at[1], near_send.at[3], near_recv.at[3], across),
    ]
    energy = lax.fori_loop(0, 4, forward, zero)
    norm_1, cross, energy_1 = reduce_all(
        1, [0.5 * inner(resid, resid), 0.5 * inner(resid, quad), energy]
    )
    beta = norm_1 / norm_0
    curve_1 = energy_1 + 0.1 * norm_1 + 2.0 * beta * cross + beta * beta * curve_0
    alpha_1 = norm_1 / curve_1
    on_rhs = alpha_0 + alpha_1 * beta
    for copy in near:
        copy.wait()
    here = on_rhs * rhs[...] + alpha_1 * resid[...]
    after = on_rhs * near_rhs[c] + alpha_1 * near_resid[c]
    before = on_rhs * near_rhs[1 - c] + alpha_1 * near_resid[1 - c]
    me = 2 * b + c
    diff = jnp.where(me < BINS - 1, after - here, 0.0)
    prior = jnp.where(me > 0, here - before, 0.0)
    size = jnp.sqrt(diff[0] * diff[0] + diff[1] * diff[1])
    prior_size = jnp.sqrt(prior[0] * prior[0] + prior[1] * prior[1])
    (size_sum,) = reduce_all(2, [0.5 * fold(size)])
    lam = size_sum / COUNT + 1e-06
    scale = lam / jnp.maximum(size, lam)
    prior_scale = lam / jnp.maximum(prior_size, lam)
    image[...] = here + 0.25 * (diff * scale[None] - prior * prior_scale[None])

    own_out = pltpu.make_async_copy(image, out.at[c, y], out_local)
    own_out.start()
    copies = [
        send(image, out.at[c, y], out_send.at[step - 1], out_recv.at[4 - step - 1], at_y(step))
        for step in (1, 2, 3)
    ]
    sib_copies = [send(image, out.at[c, y], out_sib_send.at[0], out_sib_recv.at[0], sibling)]
    for slot in (1, 3, 2):
        copies[3 - slot].wait_recv()
        there = out.at[c, lax.rem(y + slot, 4)]
        sib_copies.append(send(there, there, out_sib_send.at[slot], out_sib_recv.at[slot], sibling))
    own_out.wait()
    for k in range(4):
        sib_copy(k).wait_send()
    for k in range(3):
        y_copy(k).wait_send()
        map_copies[k].wait_send()
        copies[k].wait_send()
    for copy in sib_maps:
        copy.wait_send()
    for copy in sib_copies:
        copy.wait()


def on_device(kspace, coil_maps, sample_mask):
    dma = pltpu.SemaphoreType.DMA
    vmem = pl.BlockSpec(memory_space=pltpu.VMEM)
    return pl.pallas_call(
        kernel,
        out_shape=jax.ShapeDtypeStruct((2, SL) + PLANE, F32),
        in_specs=[vmem] * 5,
        out_specs=pl.BlockSpec(memory_space=pl.ANY),
        scratch_shapes=[
            pltpu.VMEM((4, 2, 2) + PLANE, F32),
            pltpu.VMEM(PLANE, F32),
            pltpu.VMEM((4 * NZ, 2 * NY), BF16),
            pltpu.VMEM((4 * NZ, 2 * NY), BF16),
            pltpu.VMEM((4 * NZ, 2 * NY), F32),
            pltpu.VMEM((4, 2) + PLANE, F32),
            pltpu.VMEM((4,) + PLANE, F32),
            pltpu.VMEM((3,) + PLANE, F32),
            pltpu.VMEM((3,) + PLANE, F32),
            pltpu.VMEM((2,) + PLANE, F32),
            pltpu.VMEM((2,) + PLANE, F32),
            pltpu.VMEM(PLANE, F32),
            pltpu.VMEM(PLANE, F32),
            pltpu.VMEM(PLANE, F32),
            pltpu.VMEM(PLANE, F32),
            pltpu.VMEM((2,) + PLANE, F32),
            pltpu.VMEM((2,) + PLANE, F32),
            pltpu.VMEM((3, 3, 3, 8, 128), F32),
            pltpu.VMEM((3, 2, 16, 3, 8, 128), F32),
            dma((3,)), dma((3,)), dma((4,)), dma((4,)), dma(()),
            dma((4,)), dma((4,)), dma((3,)), dma((3,)), dma((2,)), dma((2,)),
            dma((4,)), dma((4,)), dma((3, 2, 15)), dma((3, 2, 15)),
            dma((3,)), dma((3,)), dma((4,)), dma((4,)), dma(()),
        ],
        compiler_params=pltpu.CompilerParams(
            collective_id=0, has_side_effects=True, vmem_limit_bytes=48 * 1024 * 1024
        ),
        cost_estimate=pl.CostEstimate(flops=20_000_000_000, bytes_accessed=10_000_000, transcendentals=0),
    )(kspace, coil_maps, sample_mask, jnp.asarray(row_tables()), jnp.asarray(col_tables()))


def solution(mesh):
    return jax.shard_map(
        on_device,
        mesh=mesh,
        in_specs=(
            P("bin", "coil", None, None, None, None),
            P("coil", None, None, None, None),
            P("bin", None, None),
        ),
        out_specs=P("bin", None, None, None, None),
        check_vma=False,
    )
```

```python
import math

import jax
import jax.numpy as jnp
import numpy as np
from jax import lax
from jax.experimental import pallas as pl
from jax.experimental.pallas import tpu as pltpu
from jax.sharding import PartitionSpec as P

MESH = pl.DeviceIdType.MESH
F32 = jnp.float32
BF16 = jnp.bfloat16
NZ, NY, SL = 96, 256, 4
BIN_AXIS, COIL_AXIS = 16, 16
BINS = 32
COUNT = (BINS - 1) * SL * NZ * NY
PLANE = (2, NZ, NY)
HALF = NZ // 2


def dft_tables(length):
    index = np.arange(length)
    angle = (index[:, None] * index[None, :] % length) * (2.0 * math.pi / length)
    factor = 1.0 / math.sqrt(length)
    return np.cos(angle) * factor, np.sin(angle) * factor


def halves(table):
    high = table.astype(np.float32).astype(jnp.bfloat16)
    low = (table - high.astype(np.float64)).astype(np.float32).astype(jnp.bfloat16)
    return np.stack([high, low])


def row_tables():
    cos, sin = dft_tables(NY)
    forward = np.block([[cos, -sin], [sin, cos]])
    return np.stack([halves(forward), halves(forward.T)])


def col_tables():
    cos, sin = dft_tables(NZ)
    forward = np.block([[cos, sin], [-sin, cos]])
    return np.stack([halves(forward), halves(forward.T)])


def split(values):
    high = values.astype(BF16)
    return high, (values - high.astype(F32)).astype(BF16)


def dot(left, right):
    return jnp.dot(left, right, preferred_element_type=F32)


def rows(high, low, table, which):
    return dot(high, table[which, 0]) + dot(low, table[which, 0]) + dot(high, table[which, 1])


def cols(values, table, which):
    high, low = split(values)
    return dot(table[which, 0], high) + dot(table[which, 0], low) + dot(table[which, 1], high)


def fold(values):
    part = jnp.sum(values.reshape(values.shape[0] // 8, 8, NY), axis=0)
    return part[:, :128] + part[:, 128:]


def total(values):
    return jnp.sum(values, keepdims=True)


def kernel(
    kspace, coil_maps, mask, row_table, col_table, out,
    samples, own_maps, ticks, row, col, maps, weight, high, low, mid,
    part, from_sib, to_y, from_y, to_z, from_z,
    rhs, quad, resid, image, near_rhs, near_resid, message, sums,
    load_sem, sample_sem, slot_sem,
    map_send, map_recv, turn_send, turn_recv, map_sib_send, map_sib_recv,
    sib_send, sib_recv, y_send, y_recv, z_send, z_recv,
    near_send, near_recv, sum_send, sum_recv,
    out_send, out_recv, out_sib_send, out_sib_recv, out_local,
):
    b = lax.axis_index("bin")
    j = lax.axis_index("coil")
    y, z, c = j // 4, (j // 2) % 2, j % 2
    x = lax.rem(b, 4)
    ring = z * 4 + b // 4

    def at_y(step):
        return (b, lax.rem(y + step, 4) * 4 + z * 2 + c)

    def at_xz(step_x, step_z, core):
        place = lax.rem(ring + step_z + 8, 8)
        return (
            lax.rem(place, 4) * 4 + lax.rem(x + step_x + 4, 4),
            y * 4 + place // 4 * 2 + core,
        )

    sibling = (b, j + 1 - 2 * c)
    opposite = (b, j + 2 - 4 * z)
    wraps = jnp.where(c == 1, jnp.where(x == 3, 1, 0), jnp.where(x == 0, -1, 0))
    across = at_xz(2 * c - 1, wraps, 1 - c)
    coil_peers = [(b, lax.rem(j + step, COIL_AXIS)) for step in range(1, COIL_AXIS)]
    image_peers = [
        (b, lax.rem(y + step // 2, 4) * 4 + z * 2 + lax.rem(c + step, 2)) for step in range(1, 8)
    ]
    steps = [(dx, dz) for dz in (0, 1, 2, -1) for dx in range(4)][1:]
    bin_peers = [at_xz(dx, dz, c) for dx, dz in steps]

    def remote(source, target, send_sem, recv_sem, device):
        return pltpu.make_async_remote_copy(
            src_ref=source, dst_ref=target, send_sem=send_sem, recv_sem=recv_sem,
            device_id=device, device_id_type=MESH,
        )

    def send(*args):
        copy = remote(*args)
        copy.start()
        return copy

    def load(source, target, sem):
        copy = pltpu.make_async_copy(source, target, sem)
        copy.start()
        return copy

    def sample_copy(k):
        return pltpu.make_async_copy(
            kspace.at[:, :, lax.rem(y + 3 - k, 4)], samples.at[k], sample_sem.at[k]
        )

    barrier = pltpu.get_barrier_semaphore()
    greeted = coil_peers + [at_xz(-dx, -dz, c) for dx, dz in steps] + [across]
    for device in greeted:
        pl.semaphore_signal(barrier, inc=1, device_id=device, device_id_type=MESH)
    loads = [load(mask, ticks, load_sem.at[0]), load(row_table.at[1], row.at[1], load_sem.at[1])]
    sample_copy(0).start()
    loads += [load(col_table, col, load_sem.at[2]), load(coil_maps, own_maps, load_sem.at[3])]
    for k in (1, 2, 3):
        sample_copy(k).start()
    late_load = load(row_table.at[0], row.at[0], load_sem.at[4])
    slot_copy = load(coil_maps.at[:, y], maps.at[0, c], slot_sem)
    pl.semaphore_wait(barrier, len(greeted))

    quarter = pl.ds(pl.multiple_of(x * (NZ // 4), 8), NZ // 4)
    map_copies = [
        send(coil_maps.at[:, lax.rem(y + step, 4), :, quarter], maps.at[4 - step, c, :, :, quarter],
             map_send.at[step - 1], map_recv.at[4 - step - 1], at_y(step))
        for step in (1, 2, 3)
    ]
    sib_maps = [send(coil_maps.at[:, y], maps.at[0, c], map_sib_send.at[0], map_sib_recv.at[0], sibling)]
    loads[0].wait()
    weight[0] = ticks[0].astype(F32)
    weight[1] = ticks[1].astype(F32)
    for copy in loads[1:]:
        copy.wait()

    def half(h):
        return pl.ds(pl.multiple_of(h * HALF, 16), HALF)

    def sib_copy(k):
        return remote(part.at[k, 1 - c], from_sib.at[k], sib_send.at[k], sib_recv.at[k], sibling)

    def y_copy(k, h):
        return remote(
            to_y.at[k, :, half(h)], from_y.at[k, :, half(h)], y_send.at[k, h], y_recv.at[k, h], at_y(3 - k)
        )

    def z_copy(n, h):
        return remote(
            to_z.at[n, :, half(h)], from_z.at[n, :, half(h)], z_send.at[n, h], z_recv.at[n, h], opposite
        )

    def adjoint(k, carry):
        s = lax.rem(y + 3 - k, 4)
        sample_copy(k).wait()
        for t in range(4):
            w = weight[t // 2]
            values = jnp.concatenate(
                [samples[k, t // 2, t % 2, 0] * w, samples[k, t // 2, t % 2, 1] * w], axis=1
            )
            high[0, t * NZ:(t + 1) * NZ], low[0, t * NZ:(t + 1) * NZ] = split(values)
        used = pl.ds(0, 4 * NZ)
        mid[0, used] = rows(high[0, used], low[0, used], row, 1)
        for bin_ in range(2):
            sum_re, sum_im = 0.0, 0.0
            for coil in range(2):
                at = pl.ds((bin_ * 2 + coil) * NZ, NZ)
                wave = cols(jnp.concatenate([mid[0, at, :NY], mid[0, at, NY:]], axis=0), col, 1)
                sens_re, sens_im = own_maps[coil, s, 0], own_maps[coil, s, 1]
                sum_re += sens_re * wave[:NZ] + sens_im * wave[NZ:]
                sum_im += sens_re * wave[NZ:] - sens_im * wave[:NZ]
            part[k, bin_, 0] = sum_re
            part[k, bin_, 1] = sum_im
        sib_copy(k).start()

        @pl.when(k > 0)
        def _():
            sib_copy(k - 1).wait_recv()
            to_y[k - 1] = part[k - 1, c] + from_sib[k - 1]
            y_copy(k - 1, 0).start()

        return carry

    lax.fori_loop(0, 4, adjoint, 0)
    for k in range(3):
        y_copy(k, 1).start()
    for copy in map_copies:
        copy.wait_recv()
    slots = maps.at[pl.ds(1, 3), c, :, :, quarter]
    turns = [
        send(slots, slots, turn_send.at[step - 1], turn_recv.at[step - 1], at_xz(step, 0, c))
        for step in (1, 2, 3)
    ]
    sib_copy(3).wait_recv()
    for h in range(2):
        at = half(h)
        own = part[3, c, :, at] + from_sib[3, :, at]
        for k in range(3):
            y_copy(k, h).wait_recv()
            own = own + from_y[k, :, at]
        to_z[0, :, at] = own
        z_copy(0, h).start()
    for copy in turns:
        copy.wait_recv()
    slots = maps.at[pl.ds(1, 3), c]
    sib_maps.append(send(slots, slots, map_sib_send.at[1], map_sib_recv.at[1], sibling))
    slot_copy.wait()
    late_load.wait()

    def spread(field, h):
        at = half(h)
        field_re, field_im = field[0, at], field[1, at]

        def one(n, carry):
            for t in range(4):
                sens_re, sens_im = maps[n, t // 2, t % 2, 0, at], maps[n, t // 2, t % 2, 1, at]
                values = jnp.concatenate(
                    [sens_re * field_re - sens_im * field_im, sens_re * field_im + sens_im * field_re], axis=1
                )
                to = pl.ds(pl.multiple_of((n * 4 + t) * HALF, 16), HALF)
                high[h, to], low[h, to] = split(values)
            return carry

        lax.fori_loop(0, 4, one, 0)
        mid[h] = rows(high[h], low[h], row, 0)

    def masked(n):
        at = pl.ds(pl.multiple_of(n * HALF, 16), HALF)
        values = cols(
            jnp.concatenate([mid[0, at, :NY], mid[1, at, :NY], mid[0, at, NY:], mid[1, at, NY:]], axis=0), col, 0
        )
        w = weight[c]
        return values * jnp.concatenate([w, w], axis=0), at

    def normal(n, energy):
        for t in range(4):
            values, at = masked(n * 4 + t)
            energy = energy + fold(values * values)
            wave = cols(values, col, 1)
            for h in range(2):
                lines = jnp.concatenate(
                    [wave[h * HALF:(h + 1) * HALF], wave[NZ + h * HALF:NZ + (h + 1) * HALF]], axis=1
                )
                high[h, at], low[h, at] = split(lines)
        return energy

    def gather(h, carry):
        mid[h] = rows(high[h], low[h], row, 1)
        at = half(h)

        def one(n, sums_):
            sum_re, sum_im = sums_
            for t in range(4):
                lines = pl.ds(pl.multiple_of((n * 4 + t) * HALF, 16), HALF)
                sens_re, sens_im = maps[n, t // 2, t % 2, 0, at], maps[n, t // 2, t % 2, 1, at]
                sum_re += sens_re * mid[h, lines, :NY] + sens_im * mid[h, lines, NY:]
                sum_im += sens_re * mid[h, lines, NY:] - sens_im * mid[h, lines, :NY]
            return sum_re, sum_im

        none = jnp.zeros((HALF, NY), F32)
        to_z[1, 0, at], to_z[1, 1, at] = lax.fori_loop(0, 4, one, (none, none))
        z_copy(1, h).start()
        return carry

    def forward(n, energy):
        for t in range(4):
            values, _ = masked(n * 4 + t)
            energy = energy + fold(values * values)
        return energy

    def inner(left, right):
        return fold(left[0] * right[0] + left[1] * right[1])

    lane = lax.broadcasted_iota(jnp.int32, (1, 128), 1)

    def share(which, stage, peers, me):
        copies = [
            send(message.at[which, stage], sums.at[which, stage, me],
                 sum_send.at[which, stage, n], sum_recv.at[which, stage, n], peer)
            for n, peer in enumerate(peers)
        ]
        sums[which, stage, me] = message[which, stage]
        return copies

    def collect(which, stage, copies):
        for copy in copies:
            copy.wait()
        return jnp.sum(sums[which, stage, :len(copies) + 1], axis=0)

    def reduce_start(which, parts):
        line = jnp.zeros((1, 128), F32)
        for n, value in enumerate(parts):
            line = jnp.where(lane == n, total(value), line)
        message[which, 0] = line
        peers, me = (image_peers, y * 2 + c) if which == 2 else (coil_peers, j)
        return share(which, 0, peers, me)

    def reduce_end(which, copies, count):
        message[which, 1] = collect(which, 0, copies)
        line = collect(which, 1, share(which, 1, bin_peers, b))
        return [line[:, n:n + 1] for n in range(count)]

    zero = jnp.zeros((8, 128), F32)
    for copy in sib_maps:
        copy.wait_recv()
    for h in range(2):
        at = half(h)
        z_copy(0, h).wait_recv()
        rhs[:, at] = to_z[0, :, at] + from_z[0, :, at]
        spread(rhs, h)
    near = [
        send(rhs, near_rhs.at[0], near_send.at[0], near_recv.at[0], sibling),
        send(rhs, near_rhs.at[1], near_send.at[1], near_recv.at[1], across),
    ]
    energy = lax.fori_loop(0, 4, normal, zero)
    copies = reduce_start(0, [0.5 * inner(rhs, rhs), energy])
    lax.fori_loop(0, 2, gather, 0)
    norm_0, energy_0 = reduce_end(0, copies, 2)
    curve_0 = energy_0 + 0.1 * norm_0
    alpha_0 = norm_0 / curve_0
    for h in range(2):
        at = half(h)
        z_copy(1, h).wait_recv()
        quad[:, at] = to_z[1, :, at] + from_z[1, :, at] + 0.1 * rhs[:, at]
        resid[:, at] = rhs[:, at] - alpha_0 * quad[:, at]
        spread(resid, h)
    near += [
        send(resid, near_resid.at[0], near_send.at[2], near_recv.at[2], sibling),
        send(resid, near_resid.at[1], near_send.at[3], near_recv.at[3], across),
    ]
    energy = lax.fori_loop(0, 4, forward, zero)
    copies = reduce_start(1, [0.5 * inner(resid, resid), 0.5 * inner(resid, quad), energy])
    norm_1, cross, energy_1 = reduce_end(1, copies, 3)
    beta = norm_1 / norm_0
    curve_1 = energy_1 + 0.1 * norm_1 + 2.0 * beta * cross + beta * beta * curve_0
    alpha_1 = norm_1 / curve_1
    on_rhs = alpha_0 + alpha_1 * beta
    for copy in near:
        copy.wait()
    here = on_rhs * rhs[...] + alpha_1 * resid[...]
    after = on_rhs * near_rhs[c] + alpha_1 * near_resid[c]
    me = 2 * b + c
    diff = jnp.where(me < BINS - 1, after - here, 0.0)
    size = jnp.sqrt(diff[0] * diff[0] + diff[1] * diff[1])
    copies = reduce_start(2, [fold(size)])
    before = on_rhs * near_rhs[1 - c] + alpha_1 * near_resid[1 - c]
    prior = jnp.where(me > 0, here - before, 0.0)
    prior_size = jnp.sqrt(prior[0] * prior[0] + prior[1] * prior[1])
    (size_sum,) = reduce_end(2, copies, 1)
    lam = size_sum / COUNT + 1e-06
    scale = lam / jnp.maximum(size, lam)
    prior_scale = lam / jnp.maximum(prior_size, lam)
    image[...] = here + 0.25 * (diff * scale[None] - prior * prior_scale[None])

    own_out = pltpu.make_async_copy(image, out.at[c, y], out_local)
    own_out.start()
    copies = [
        send(image, out.at[c, y], out_send.at[step - 1], out_recv.at[4 - step - 1], at_y(step))
        for step in (1, 2, 3)
    ]
    sib_copies = [send(image, out.at[c, y], out_sib_send.at[0], out_sib_recv.at[0], sibling)]
    for slot in (1, 3, 2):
        copies[3 - slot].wait_recv()
        there = out.at[c, lax.rem(y + slot, 4)]
        sib_copies.append(send(there, there, out_sib_send.at[slot], out_sib_recv.at[slot], sibling))
    own_out.wait()
    for k in range(4):
        sib_copy(k).wait_send()
    for k in range(3):
        for h in range(2):
            y_copy(k, h).wait_send()
        map_copies[k].wait_send()
        turns[k].wait_send()
        copies[k].wait_send()
    for n in range(2):
        for h in range(2):
            z_copy(n, h).wait_send()
    for copy in sib_maps:
        copy.wait_send()
    for copy in sib_copies:
        copy.wait()


def on_device(kspace, coil_maps, sample_mask):
    dma = pltpu.SemaphoreType.DMA
    whole = pl.BlockSpec(memory_space=pl.ANY)
    return pl.pallas_call(
        kernel,
        out_shape=jax.ShapeDtypeStruct((2, SL) + PLANE, F32),
        in_specs=[whole] * 5,
        out_specs=whole,
        scratch_shapes=[
            pltpu.VMEM((4, 2, 2) + PLANE, F32),
            pltpu.VMEM((2, SL) + PLANE, F32),
            pltpu.VMEM(PLANE, jnp.int32),
            pltpu.VMEM((2, 2, 2 * NY, 2 * NY), BF16),
            pltpu.VMEM((2, 2, 2 * NZ, 2 * NZ), BF16),
            pltpu.VMEM((4, 2, 2) + PLANE, F32),
            pltpu.VMEM(PLANE, F32),
            pltpu.VMEM((2, 16 * HALF, 2 * NY), BF16),
            pltpu.VMEM((2, 16 * HALF, 2 * NY), BF16),
            pltpu.VMEM((2, 16 * HALF, 2 * NY), F32),
            pltpu.VMEM((4, 2) + PLANE, F32),
            pltpu.VMEM((4,) + PLANE, F32),
            pltpu.VMEM((3,) + PLANE, F32),
            pltpu.VMEM((3,) + PLANE, F32),
            pltpu.VMEM((2,) + PLANE, F32),
            pltpu.VMEM((2,) + PLANE, F32),
            pltpu.VMEM(PLANE, F32),
            pltpu.VMEM(PLANE, F32),
            pltpu.VMEM(PLANE, F32),
            pltpu.VMEM(PLANE, F32),
            pltpu.VMEM((2,) + PLANE, F32),
            pltpu.VMEM((2,) + PLANE, F32),
            pltpu.VMEM((3, 2, 1, 128), F32),
            pltpu.VMEM((3, 2, 16, 1, 128), F32),
            dma((5,)), dma((4,)), dma(()),
            dma((3,)), dma((3,)), dma((3,)), dma((3,)), dma((2,)), dma((2,)),
            dma((4,)), dma((4,)), dma((3, 2)), dma((3, 2)), dma((2, 2)), dma((2, 2)),
            dma((4,)), dma((4,)), dma((3, 2, 15)), dma((3, 2, 15)),
            dma((3,)), dma((3,)), dma((4,)), dma((4,)), dma(()),
        ],
        compiler_params=pltpu.CompilerParams(
            collective_id=0, has_side_effects=True, vmem_limit_bytes=60 * 1024 * 1024
        ),
        cost_estimate=pl.CostEstimate(flops=20_000_000_000, bytes_accessed=10_000_000, transcendentals=0),
    )(kspace, coil_maps, sample_mask, jnp.asarray(row_tables()), jnp.asarray(col_tables()))


def solution(mesh):
    return jax.shard_map(
        on_device,
        mesh=mesh,
        in_specs=(
            P("bin", "coil", None, None, None, None),
            P("coil", None, None, None, None),
            P("bin", None, None),
        ),
        out_specs=P("bin", None, None, None, None),
        check_vma=False,
    )
```

```python
import math

import jax
import jax.numpy as jnp
import numpy as np
from jax import lax
from jax.experimental import pallas as pl
from jax.experimental.pallas import tpu as pltpu
from jax.sharding import PartitionSpec as P

MESH = pl.DeviceIdType.MESH
F32 = jnp.float32
BF16 = jnp.bfloat16
NZ, NY, SL = 96, 256, 4
BIN_AXIS, COIL_AXIS = 16, 16
BINS = 32
COUNT = (BINS - 1) * SL * NZ * NY
PLANE = (2, NZ, NY)
HALF = NZ // 2


def dft_tables(length):
    index = np.arange(length)
    angle = (index[:, None] * index[None, :] % length) * (2.0 * math.pi / length)
    factor = 1.0 / math.sqrt(length)
    return np.cos(angle) * factor, np.sin(angle) * factor


def halves(table):
    high = table.astype(np.float32).astype(jnp.bfloat16)
    low = (table - high.astype(np.float64)).astype(np.float32).astype(jnp.bfloat16)
    return np.stack([high, low])


def row_tables():
    cos, sin = dft_tables(NY)
    forward = np.block([[cos, -sin], [sin, cos]])
    return np.stack([halves(forward), halves(forward.T)])


def col_tables():
    cos, sin = dft_tables(NZ)
    forward = np.block([[cos, sin], [-sin, cos]])
    return np.stack([halves(forward), halves(forward.T)])


def split(values):
    high = values.astype(BF16)
    return high, (values - high.astype(F32)).astype(BF16)


def dot(left, right):
    return jnp.dot(left, right, preferred_element_type=F32)


def rows(high, low, table, which):
    return dot(high, table[which, 0]) + dot(low, table[which, 0]) + dot(high, table[which, 1])


def cols(values, table, which):
    high, low = split(values)
    return dot(table[which, 0], high) + dot(table[which, 0], low) + dot(table[which, 1], high)


def fold(values):
    part = jnp.sum(values.reshape(values.shape[0] // 8, 8, NY), axis=0)
    return part[:, :128] + part[:, 128:]


def total(values):
    return jnp.sum(values, keepdims=True)


def kernel(
    kspace, coil_maps, mask, row_table, col_table, out,
    samples, own_maps, ticks, row, col, maps, weight, high, low, mid,
    part, from_sib, to_y, from_y, to_z, from_z,
    fields, quad, gaps, sizes, result, message, sums,
    load_sem, sample_sem, slot_sem,
    map_send, map_recv, turn_send, turn_recv, map_sib_send, map_sib_recv,
    sib_send, sib_recv, y_send, y_recv, z_send, z_recv,
    near_send, near_recv, along_send, along_recv, pass_send, pass_recv, far_send, far_recv,
    sum_send, sum_recv, out_sem,
):
    b = lax.axis_index("bin")
    j = lax.axis_index("coil")
    y, z, c = j // 4, (j // 2) % 2, j % 2
    x = lax.rem(b, 4)
    ring = z * 4 + b // 4

    def at_y(step):
        return (b, lax.rem(y + step, 4) * 4 + z * 2 + c)

    def at_xz(step_x, step_z, core):
        place = lax.rem(ring + step_z + 8, 8)
        return (
            lax.rem(place, 4) * 4 + lax.rem(x + step_x + 4, 4),
            y * 4 + place // 4 * 2 + core,
        )

    rhs = fields.at[0, 1 + c, y]
    resid = fields.at[1, 1 + c, y]
    sibling = (b, j + 1 - 2 * c)
    opposite = (b, j + 2 - 4 * z)
    wraps = jnp.where(c == 1, jnp.where(x == 3, 1, 0), jnp.where(x == 0, -1, 0))
    across = at_xz(2 * c - 1, wraps, 1 - c)
    coil_peers = [(b, lax.rem(j + step, COIL_AXIS)) for step in range(1, COIL_AXIS)]
    image_peers = [
        (b, lax.rem(y + step // 2, 4) * 4 + z * 2 + lax.rem(c + step, 2)) for step in range(1, 8)
    ]
    steps = [(dx, dz) for dz in (0, 1, 2, -1) for dx in range(4)][1:]
    bin_peers = [at_xz(dx, dz, c) for dx, dz in steps]

    def remote(source, target, send_sem, recv_sem, device):
        return pltpu.make_async_remote_copy(
            src_ref=source, dst_ref=target, send_sem=send_sem, recv_sem=recv_sem,
            device_id=device, device_id_type=MESH,
        )

    def send(*args):
        copy = remote(*args)
        copy.start()
        return copy

    def load(source, target, sem):
        copy = pltpu.make_async_copy(source, target, sem)
        copy.start()
        return copy

    def sample_copy(k):
        return pltpu.make_async_copy(
            kspace.at[:, :, lax.rem(y + 3 - k, 4)], samples.at[k], sample_sem.at[k]
        )

    barrier = pltpu.get_barrier_semaphore()
    greeted = coil_peers + [at_xz(-dx, -dz, c) for dx, dz in steps] + [across]
    for device in greeted:
        pl.semaphore_signal(barrier, inc=1, device_id=device, device_id_type=MESH)
    loads = [load(mask, ticks, load_sem.at[0]), load(row_table.at[1], row.at[1], load_sem.at[1])]
    sample_copy(0).start()
    loads += [load(col_table, col, load_sem.at[2]), load(coil_maps, own_maps, load_sem.at[3])]
    for k in (1, 2, 3):
        sample_copy(k).start()
    late_load = load(row_table.at[0], row.at[0], load_sem.at[4])
    slot_copy = load(coil_maps.at[:, y], maps.at[0, c], slot_sem)
    pl.semaphore_wait(barrier, len(greeted))

    quarter = pl.ds(pl.multiple_of(x * (NZ // 4), 8), NZ // 4)
    map_copies = [
        send(coil_maps.at[:, lax.rem(y + step, 4), :, quarter], maps.at[4 - step, c, :, :, quarter],
             map_send.at[step - 1], map_recv.at[4 - step - 1], at_y(step))
        for step in (1, 2, 3)
    ]
    sib_maps = [send(coil_maps.at[:, y], maps.at[0, c], map_sib_send.at[0], map_sib_recv.at[0], sibling)]
    loads[0].wait()
    weight[0] = ticks[0].astype(F32)
    weight[1] = ticks[1].astype(F32)
    for copy in loads[1:]:
        copy.wait()

    def half(h):
        return pl.ds(pl.multiple_of(h * HALF, 16), HALF)

    def sib_copy(k):
        return remote(part.at[k, 1 - c], from_sib.at[k], sib_send.at[k], sib_recv.at[k], sibling)

    def y_copy(k, h):
        return remote(
            to_y.at[k, :, half(h)], from_y.at[k, :, half(h)], y_send.at[k, h], y_recv.at[k, h], at_y(3 - k)
        )

    def z_copy(n, h):
        return remote(
            to_z.at[n, :, half(h)], from_z.at[n, :, half(h)], z_send.at[n, h], z_recv.at[n, h], opposite
        )

    def adjoint(k, carry):
        s = lax.rem(y + 3 - k, 4)
        sample_copy(k).wait()
        for t in range(4):
            w = weight[t // 2]
            values = jnp.concatenate(
                [samples[k, t // 2, t % 2, 0] * w, samples[k, t // 2, t % 2, 1] * w], axis=1
            )
            high[0, t * NZ:(t + 1) * NZ], low[0, t * NZ:(t + 1) * NZ] = split(values)
        used = pl.ds(0, 4 * NZ)
        mid[0, used] = rows(high[0, used], low[0, used], row, 1)
        for bin_ in range(2):
            sum_re, sum_im = 0.0, 0.0
            for coil in range(2):
                at = pl.ds((bin_ * 2 + coil) * NZ, NZ)
                wave = cols(jnp.concatenate([mid[0, at, :NY], mid[0, at, NY:]], axis=0), col, 1)
                sens_re, sens_im = own_maps[coil, s, 0], own_maps[coil, s, 1]
                sum_re += sens_re * wave[:NZ] + sens_im * wave[NZ:]
                sum_im += sens_re * wave[NZ:] - sens_im * wave[:NZ]
            part[k, bin_, 0] = sum_re
            part[k, bin_, 1] = sum_im
        sib_copy(k).start()

        @pl.when(k > 0)
        def _():
            sib_copy(k - 1).wait_recv()
            to_y[k - 1] = part[k - 1, c] + from_sib[k - 1]
            y_copy(k - 1, 0).start()

        return carry

    lax.fori_loop(0, 4, adjoint, 0)
    for k in range(3):
        y_copy(k, 1).start()
    for copy in map_copies:
        copy.wait_recv()
    slots = maps.at[pl.ds(1, 3), c, :, :, quarter]
    turns = [
        send(slots, slots, turn_send.at[step - 1], turn_recv.at[step - 1], at_xz(step, 0, c))
        for step in (1, 2, 3)
    ]
    sib_copy(3).wait_recv()
    for h in range(2):
        at = half(h)
        own = part[3, c, :, at] + from_sib[3, :, at]
        for k in range(3):
            y_copy(k, h).wait_recv()
            own = own + from_y[k, :, at]
        to_z[0, :, at] = own
        z_copy(0, h).start()
    for copy in turns:
        copy.wait_recv()
    slots = maps.at[pl.ds(1, 3), c]
    sib_maps.append(send(slots, slots, map_sib_send.at[1], map_sib_recv.at[1], sibling))
    slot_copy.wait()
    late_load.wait()

    def spread(field, h):
        at = half(h)
        field_re, field_im = field[0, at], field[1, at]

        def one(n, carry):
            for t in range(4):
                sens_re, sens_im = maps[n, t // 2, t % 2, 0, at], maps[n, t // 2, t % 2, 1, at]
                values = jnp.concatenate(
                    [sens_re * field_re - sens_im * field_im, sens_re * field_im + sens_im * field_re], axis=1
                )
                to = pl.ds(pl.multiple_of((n * 4 + t) * HALF, 16), HALF)
                high[h, to], low[h, to] = split(values)
            return carry

        lax.fori_loop(0, 4, one, 0)
        mid[h] = rows(high[h], low[h], row, 0)

    def masked(n):
        at = pl.ds(pl.multiple_of(n * HALF, 16), HALF)
        values = cols(
            jnp.concatenate([mid[0, at, :NY], mid[1, at, :NY], mid[0, at, NY:], mid[1, at, NY:]], axis=0), col, 0
        )
        w = weight[c]
        return values * jnp.concatenate([w, w], axis=0), at

    def normal(n, energy):
        for t in range(4):
            values, at = masked(n * 4 + t)
            energy = energy + fold(values * values)
            wave = cols(values, col, 1)
            for h in range(2):
                lines = jnp.concatenate(
                    [wave[h * HALF:(h + 1) * HALF], wave[NZ + h * HALF:NZ + (h + 1) * HALF]], axis=1
                )
                high[h, at], low[h, at] = split(lines)
        return energy

    def gather(h, carry):
        mid[h] = rows(high[h], low[h], row, 1)
        at = half(h)

        def one(n, sums_):
            sum_re, sum_im = sums_
            for t in range(4):
                lines = pl.ds(pl.multiple_of((n * 4 + t) * HALF, 16), HALF)
                sens_re, sens_im = maps[n, t // 2, t % 2, 0, at], maps[n, t // 2, t % 2, 1, at]
                sum_re += sens_re * mid[h, lines, :NY] + sens_im * mid[h, lines, NY:]
                sum_im += sens_re * mid[h, lines, NY:] - sens_im * mid[h, lines, :NY]
            return sum_re, sum_im

        none = jnp.zeros((HALF, NY), F32)
        to_z[1, 0, at], to_z[1, 1, at] = lax.fori_loop(0, 4, one, (none, none))
        z_copy(1, h).start()
        return carry

    def forward(n, energy):
        for t in range(4):
            values, _ = masked(n * 4 + t)
            energy = energy + fold(values * values)
        return energy

    def inner(left, right):
        return fold(left[0] * right[0] + left[1] * right[1])

    lane = lax.broadcasted_iota(jnp.int32, (1, 128), 1)

    def share(which, stage, peers, me):
        copies = [
            send(message.at[which, stage], sums.at[which, stage, me],
                 sum_send.at[which, stage, n], sum_recv.at[which, stage, n], peer)
            for n, peer in enumerate(peers)
        ]
        sums[which, stage, me] = message[which, stage]
        return copies

    def collect(which, stage, copies):
        for copy in copies:
            copy.wait()
        return jnp.sum(sums[which, stage, :len(copies) + 1], axis=0)

    def reduce_start(which, parts):
        line = jnp.zeros((1, 128), F32)
        for n, value in enumerate(parts):
            line = jnp.where(lane == n, total(value), line)
        message[which, 0] = line
        peers, me = (image_peers, y * 2 + c) if which == 2 else (coil_peers, j)
        return share(which, 0, peers, me)

    def reduce_end(which, copies, count, meanwhile):
        message[which, 1] = collect(which, 0, copies)
        copies = share(which, 1, bin_peers, b)
        meanwhile()
        line = collect(which, 1, copies)
        return [line[:, n:n + 1] for n in range(count)]

    near, along, onward, far = [], [], [], []

    def publish(n):
        mine = fields.at[n, 1 + c, y]
        near.append([
            send(mine, mine, near_send.at[n, 0], near_recv.at[n, 0], sibling),
            send(mine, fields.at[n, 3 - 3 * c, y], near_send.at[n, 1], near_recv.at[n, 1], across),
        ])
        along.append([
            send(mine, mine, along_send.at[n, step - 1], along_recv.at[n, 4 - step - 1], at_y(step))
            for step in (1, 2, 3)
        ])

    def pass_on(n):
        onward.append([])
        for slot in (1, 3, 2):
            along[n][3 - slot].wait_recv()
            line = lax.rem(y + slot, 4)
            plane = fields.at[n, 1 + c, line]
            onward[n] += [
                send(plane, plane, pass_send.at[n, 0, slot - 1], pass_recv.at[n, 0, slot - 1], sibling),
                send(plane, fields.at[n, 3 - 3 * c, line],
                     pass_send.at[n, 1, slot - 1], pass_recv.at[n, 1, slot - 1], across),
            ]

    def greet(n):
        for copy in near[n]:
            copy.wait_recv()

    def hand_over(n):
        for copy in onward[n][1::2]:
            copy.wait_recv()
        planes = fields.at[n, 3 * c]
        far.append(send(planes, planes, far_send.at[n], far_recv.at[n], sibling))

    def settle(n):
        for copy in onward[n][::2]:
            copy.wait_recv()
        far[n].wait_recv()

    zero = jnp.zeros((8, 128), F32)
    for copy in sib_maps:
        copy.wait_recv()
    for h in range(2):
        at = half(h)
        z_copy(0, h).wait_recv()
        rhs[:, at] = to_z[0, :, at] + from_z[0, :, at]
        spread(rhs, h)
    publish(0)
    energy = lax.fori_loop(0, 4, normal, zero)
    copies = reduce_start(0, [0.5 * inner(rhs, rhs), energy])
    lax.fori_loop(0, 2, gather, 0)
    norm_0, energy_0 = reduce_end(0, copies, 2, lambda: pass_on(0))
    curve_0 = energy_0 + 0.1 * norm_0
    alpha_0 = norm_0 / curve_0
    for h in range(2):
        at = half(h)
        z_copy(1, h).wait_recv()
        quad[:, at] = to_z[1, :, at] + from_z[1, :, at] + 0.1 * rhs[:, at]
        resid[:, at] = rhs[:, at] - alpha_0 * quad[:, at]
        spread(resid, h)
    publish(1)
    greet(0)
    hand_over(0)
    energy = lax.fori_loop(0, 4, forward, zero)
    copies = reduce_start(1, [0.5 * inner(resid, resid), 0.5 * inner(resid, quad), energy])
    norm_1, cross, energy_1 = reduce_end(1, copies, 3, lambda: pass_on(1))
    beta = norm_1 / norm_0
    curve_1 = energy_1 + 0.1 * norm_1 + 2.0 * beta * cross + beta * beta * curve_0
    alpha_1 = norm_1 / curve_1
    on_rhs = alpha_0 + alpha_1 * beta
    greet(1)

    def iterate(place, line):
        return on_rhs * fields[0, place, line] + alpha_1 * fields[1, place, line]

    def length(gap):
        return jnp.sqrt(gap[0] * gap[0] + gap[1] * gap[1])

    gap = jnp.where(2 * b + c < BINS - 1, iterate(2 + c, y) - iterate(1 + c, y), 0.0)
    copies = reduce_start(2, [fold(length(gap))])

    def differences(line, carry):
        values = [iterate(place, line) for place in range(4)]
        result[line, 0] = values[1]
        result[line, 1] = values[2]
        for n, keep in enumerate((b > 0, None, b < BIN_AXIS - 1)):
            gap = values[n + 1] - values[n]
            if keep is not None:
                gap = jnp.where(keep, gap, 0.0)
            gaps[line, n] = gap
            sizes[line, n] = length(gap)
        return carry

    def prepare():
        hand_over(1)
        settle(0)
        settle(1)
        lax.fori_loop(0, SL, differences, 0)

    (size_sum,) = reduce_end(2, copies, 1, prepare)
    lam = size_sum / COUNT + 1e-06

    def out_copy(line):
        return pltpu.make_async_copy(result.at[line], out.at[:, line], out_sem.at[line])

    def finish(line, carry):
        dual = [
            gaps[line, n] * (lam / jnp.maximum(sizes[line, n], lam))[None] for n in range(3)
        ]
        for n in range(2):
            result[line, n] = result[line, n] + 0.25 * (dual[n + 1] - dual[n])
        out_copy(line).start()
        return carry

    lax.fori_loop(0, SL, finish, 0)
    for k in range(4):
        sib_copy(k).wait_send()
    for k in range(3):
        for h in range(2):
            y_copy(k, h).wait_send()
        map_copies[k].wait_send()
        turns[k].wait_send()
    for n in range(2):
        for h in range(2):
            z_copy(n, h).wait_send()
        for copy in near[n] + along[n] + onward[n] + [far[n]]:
            copy.wait_send()
    for copy in sib_maps:
        copy.wait_send()
    for line in range(SL):
        out_copy(line).wait()


def on_device(kspace, coil_maps, sample_mask):
    dma = pltpu.SemaphoreType.DMA
    whole = pl.BlockSpec(memory_space=pl.ANY)
    return pl.pallas_call(
        kernel,
        out_shape=jax.ShapeDtypeStruct((2, SL) + PLANE, F32),
        in_specs=[whole] * 5,
        out_specs=whole,
        scratch_shapes=[
            pltpu.VMEM((4, 2, 2) + PLANE, F32),
            pltpu.VMEM((2, SL) + PLANE, F32),
            pltpu.VMEM(PLANE, jnp.int32),
            pltpu.VMEM((2, 2, 2 * NY, 2 * NY), BF16),
            pltpu.VMEM((2, 2, 2 * NZ, 2 * NZ), BF16),
            pltpu.VMEM((4, 2, 2) + PLANE, F32),
            pltpu.VMEM(PLANE, F32),
            pltpu.VMEM((2, 16 * HALF, 2 * NY), BF16),
            pltpu.VMEM((2, 16 * HALF, 2 * NY), BF16),
            pltpu.VMEM((2, 16 * HALF, 2 * NY), F32),
            pltpu.VMEM((4, 2) + PLANE, F32),
            pltpu.VMEM((4,) + PLANE, F32),
            pltpu.VMEM((3,) + PLANE, F32),
            pltpu.VMEM((3,) + PLANE, F32),
            pltpu.VMEM((2,) + PLANE, F32),
            pltpu.VMEM((2,) + PLANE, F32),
            pltpu.VMEM((2, 4, SL) + PLANE, F32),
            pltpu.VMEM(PLANE, F32),
            pltpu.VMEM((SL, 3) + PLANE, F32),
            pltpu.VMEM((SL, 3, NZ, NY), F32),
            pltpu.VMEM((SL, 2) + PLANE, F32),
            pltpu.VMEM((3, 2, 1, 128), F32),
            pltpu.VMEM((3, 2, 16, 1, 128), F32),
            dma((5,)), dma((4,)), dma(()),
            dma((3,)), dma((3,)), dma((3,)), dma((3,)), dma((2,)), dma((2,)),
            dma((4,)), dma((4,)), dma((3, 2)), dma((3, 2)), dma((2, 2)), dma((2, 2)),
            dma((2, 2)), dma((2, 2)), dma((2, 3)), dma((2, 3)),
            dma((2, 2, 3)), dma((2, 2, 3)), dma((2,)), dma((2,)),
            dma((3, 2, 15)), dma((3, 2, 15)), dma((SL,)),
        ],
        compiler_params=pltpu.CompilerParams(
            collective_id=0, has_side_effects=True, vmem_limit_bytes=60 * 1024 * 1024
        ),
        cost_estimate=pl.CostEstimate(flops=20_000_000_000, bytes_accessed=10_000_000, transcendentals=0),
    )(kspace, coil_maps, sample_mask, jnp.asarray(row_tables()), jnp.asarray(col_tables()))


def solution(mesh):
    return jax.shard_map(
        on_device,
        mesh=mesh,
        in_specs=(
            P("bin", "coil", None, None, None, None),
            P("coil", None, None, None, None),
            P("bin", None, None),
        ),
        out_specs=P("bin", None, None, None, None),
        check_vma=False,
    )
```

```python
import math

import jax
import jax.numpy as jnp
import numpy as np
from jax import lax
from jax.experimental import pallas as pl
from jax.experimental.pallas import tpu as pltpu
from jax.sharding import PartitionSpec as P

MESH = pl.DeviceIdType.MESH
F32 = jnp.float32
BF16 = jnp.bfloat16
NZ, NY, SL = 96, 256, 4
BIN_AXIS, COIL_AXIS = 16, 16
BINS = 32
COUNT = (BINS - 1) * SL * NZ * NY
PLANE = (2, NZ, NY)
HALF = NZ // 2


def dft_tables(length):
    index = np.arange(length)
    angle = (index[:, None] * index[None, :] % length) * (2.0 * math.pi / length)
    factor = 1.0 / math.sqrt(length)
    return np.cos(angle) * factor, np.sin(angle) * factor


def halves(table):
    high = table.astype(np.float32).astype(jnp.bfloat16)
    low = (table - high.astype(np.float64)).astype(np.float32).astype(jnp.bfloat16)
    return np.stack([high, low])


def row_tables():
    cos, sin = dft_tables(NY)
    forward = np.block([[cos, -sin], [sin, cos]])
    return np.stack([halves(forward), halves(forward.T)])


def col_tables():
    cos, sin = dft_tables(NZ)
    forward = np.block([[cos, sin], [-sin, cos]])
    return np.stack([halves(forward), halves(forward.T)])


def split(values):
    high = values.astype(BF16)
    return high, (values - high.astype(F32)).astype(BF16)


def dot(left, right):
    return jnp.dot(left, right, preferred_element_type=F32)


def rows(high, low, table, which):
    return dot(high, table[which, 0]) + dot(low, table[which, 0]) + dot(high, table[which, 1])


def cols(values, table, which):
    high, low = split(values)
    return dot(table[which, 0], high) + dot(table[which, 0], low) + dot(table[which, 1], high)


def fold(values):
    part = jnp.sum(values.reshape(values.shape[0] // 8, 8, NY), axis=0)
    return part[:, :128] + part[:, 128:]


def total(values):
    return jnp.sum(values, keepdims=True)


def kernel(
    kspace, coil_maps, mask, row_table, col_table, out,
    samples, own_maps, ticks, row, col, maps, weight, high, low, mid,
    part, from_sib, to_y, from_y, to_z, from_z,
    fields, quad, gaps, sizes, result, message, sums,
    load_sem, sample_sem, slot_sem,
    map_send, map_recv, turn_send, turn_recv, map_sib_send, map_sib_recv,
    sib_send, sib_recv, y_send, y_recv, z_send, z_recv,
    near_send, near_recv, along_send, along_recv, pass_send, pass_recv, far_send, far_recv,
    sum_send, sum_recv, out_sem,
):
    b = lax.axis_index("bin")
    j = lax.axis_index("coil")
    y, z, c = j // 4, (j // 2) % 2, j % 2
    x = lax.rem(b, 4)
    ring = z * 4 + b // 4

    def at_y(step):
        return (b, lax.rem(y + step, 4) * 4 + z * 2 + c)

    def at_xz(step_x, step_z, core):
        place = lax.rem(ring + step_z + 8, 8)
        return (
            lax.rem(place, 4) * 4 + lax.rem(x + step_x + 4, 4),
            y * 4 + place // 4 * 2 + core,
        )

    rhs = fields.at[0, 1 + c, y]
    resid = fields.at[1, 1 + c, y]
    sibling = (b, j + 1 - 2 * c)
    opposite = (b, j + 2 - 4 * z)
    wraps = jnp.where(c == 1, jnp.where(x == 3, 1, 0), jnp.where(x == 0, -1, 0))
    across = at_xz(2 * c - 1, wraps, 1 - c)
    column_peers = [at_xz(0, step // 2, lax.rem(c + step, 2)) for step in range(1, 16)]
    near_peers = [
        at_xz(0, dz, core) for dz in (0, 1, 2, -1) for core in (c, 1 - c)
    ][1:]
    plane_peers = [
        (b - x + lax.rem(x + step % 4, 4), lax.rem(y + step // 4, 4) * 4 + z * 2 + c) for step in range(1, 16)
    ]

    def remote(source, target, send_sem, recv_sem, device):
        return pltpu.make_async_remote_copy(
            src_ref=source, dst_ref=target, send_sem=send_sem, recv_sem=recv_sem,
            device_id=device, device_id_type=MESH,
        )

    def send(*args):
        copy = remote(*args)
        copy.start()
        return copy

    def arrived(ref, sem):
        remote(ref, ref, sem, sem, sibling).wait_recv()

    def departed(ref, sem):
        remote(ref, ref, sem, sem, sibling).wait_send()

    def load(source, target, sem):
        copy = pltpu.make_async_copy(source, target, sem)
        copy.start()
        return copy

    def sample_copy(k):
        return pltpu.make_async_copy(
            kspace.at[:, :, lax.rem(y + 3 - k, 4)], samples.at[k], sample_sem.at[k]
        )

    barrier = pltpu.get_barrier_semaphore()
    greeted = column_peers + plane_peers + [across]
    for device in greeted:
        pl.semaphore_signal(barrier, inc=1, device_id=device, device_id_type=MESH)
    loads = [load(mask, ticks, load_sem.at[0]), load(row_table.at[1], row.at[1], load_sem.at[1])]
    sample_copy(0).start()
    loads += [load(col_table, col, load_sem.at[2]), load(coil_maps, own_maps, load_sem.at[3])]
    for k in (1, 2, 3):
        sample_copy(k).start()
    late_load = load(row_table.at[0], row.at[0], load_sem.at[4])
    slot_copy = load(coil_maps.at[:, y], maps.at[0, c], slot_sem)
    loads[0].wait()
    weight[0] = ticks[0].astype(F32)
    weight[1] = ticks[1].astype(F32)
    for copy in loads[1:]:
        copy.wait()

    def half(h):
        return pl.ds(pl.multiple_of(h * HALF, 16), HALF)

    def sib_copy(k):
        return remote(part.at[k, 1 - c], from_sib.at[k], sib_send.at[k], sib_recv.at[k], sibling)

    def y_copy(k, h):
        return remote(
            to_y.at[k, :, half(h)], from_y.at[k, :, half(h)], y_send, y_recv.at[h], at_y(3 - k)
        )

    def z_copy(n, h):
        return remote(
            to_z.at[n, :, half(h)], from_z.at[n, :, half(h)], z_send.at[n, h], z_recv.at[n, h], opposite
        )

    def adjoint(k, carry):
        s = lax.rem(y + 3 - k, 4)
        sample_copy(k).wait()
        for t in range(4):
            w = weight[t // 2]
            values = jnp.concatenate(
                [samples[k, t // 2, t % 2, 0] * w, samples[k, t // 2, t % 2, 1] * w], axis=1
            )
            high[0, t * NZ:(t + 1) * NZ], low[0, t * NZ:(t + 1) * NZ] = split(values)
        used = pl.ds(0, 4 * NZ)
        mid[0, used] = rows(high[0, used], low[0, used], row, 1)
        for bin_ in range(2):
            sum_re, sum_im = 0.0, 0.0
            for coil in range(2):
                at = pl.ds((bin_ * 2 + coil) * NZ, NZ)
                wave = cols(jnp.concatenate([mid[0, at, :NY], mid[0, at, NY:]], axis=0), col, 1)
                sens_re, sens_im = own_maps[coil, s, 0], own_maps[coil, s, 1]
                sum_re += sens_re * wave[:NZ] + sens_im * wave[NZ:]
                sum_im += sens_re * wave[NZ:] - sens_im * wave[:NZ]
            part[k, bin_, 0] = sum_re
            part[k, bin_, 1] = sum_im
        return carry

    lax.fori_loop(0, 4, adjoint, 0)
    pl.semaphore_wait(barrier, len(greeted))
    for k in range(4):
        sib_copy(k).start()
    quarter = pl.ds(pl.multiple_of(x * (NZ // 4), 8), NZ // 4)
    for step in (1, 2, 3):
        send(coil_maps.at[:, lax.rem(y + step, 4), :, quarter], maps.at[4 - step, c, :, :, quarter],
             map_send, map_recv, at_y(step))
    for k in range(3):
        sib_copy(k).wait_recv()
        to_y[k] = part[k, c] + from_sib[k]
        y_copy(k, 0).start()
    for k in range(3):
        y_copy(k, 1).start()
    send(own_maps.at[:, y], maps.at[0, c], map_sib_send.at[0], map_sib_recv.at[0], sibling)
    slots = maps.at[pl.ds(1, 3), c, :, :, quarter]
    arrived(slots, map_recv)
    for step in (1, 2, 3):
        send(slots, slots, turn_send, turn_recv, at_xz(step, 0, c))
    sib_copy(3).wait_recv()
    part[3, c] = part[3, c] + from_sib[3]
    for h in range(2):
        at = half(h)
        arrived(from_y.at[:, :, at], y_recv.at[h])
        to_z[0, :, at] = part[3, c, :, at] + from_y[0, :, at] + from_y[1, :, at] + from_y[2, :, at]
        z_copy(0, h).start()
    turned = maps.at[pl.ds(1, 3), c, :, :, pl.ds(0, 3 * (NZ // 4))]
    arrived(turned, turn_recv)
    rest = maps.at[pl.ds(1, 3), c]
    send(rest, rest, map_sib_send.at[1], map_sib_recv.at[1], sibling)
    slot_copy.wait()
    late_load.wait()

    def spread(field, h):
        at = half(h)
        field_re, field_im = field[0, at], field[1, at]

        def one(n, carry):
            for t in range(4):
                sens_re, sens_im = maps[n, t // 2, t % 2, 0, at], maps[n, t // 2, t % 2, 1, at]
                values = jnp.concatenate(
                    [sens_re * field_re - sens_im * field_im, sens_re * field_im + sens_im * field_re], axis=1
                )
                to = pl.ds(pl.multiple_of((n * 4 + t) * HALF, 16), HALF)
                high[h, to], low[h, to] = split(values)
            return carry

        lax.fori_loop(0, 4, one, 0)
        mid[h] = rows(high[h], low[h], row, 0)

    def masked(n):
        at = pl.ds(pl.multiple_of(n * HALF, 16), HALF)
        values = cols(
            jnp.concatenate([mid[0, at, :NY], mid[1, at, :NY], mid[0, at, NY:], mid[1, at, NY:]], axis=0), col, 0
        )
        w = weight[c]
        return values * jnp.concatenate([w, w], axis=0), at

    def normal(n, energy):
        for t in range(4):
            values, at = masked(n * 4 + t)
            energy = energy + fold(values * values)
            wave = cols(values, col, 1)
            for h in range(2):
                lines = jnp.concatenate(
                    [wave[h * HALF:(h + 1) * HALF], wave[NZ + h * HALF:NZ + (h + 1) * HALF]], axis=1
                )
                high[h, at], low[h, at] = split(lines)
        return energy

    def gather(h, carry):
        mid[h] = rows(high[h], low[h], row, 1)
        at = half(h)

        def one(n, sums_):
            sum_re, sum_im = sums_
            for t in range(4):
                lines = pl.ds(pl.multiple_of((n * 4 + t) * HALF, 16), HALF)
                sens_re, sens_im = maps[n, t // 2, t % 2, 0, at], maps[n, t // 2, t % 2, 1, at]
                sum_re += sens_re * mid[h, lines, :NY] + sens_im * mid[h, lines, NY:]
                sum_im += sens_re * mid[h, lines, NY:] - sens_im * mid[h, lines, :NY]
            return sum_re, sum_im

        none = jnp.zeros((HALF, NY), F32)
        to_z[1, 0, at], to_z[1, 1, at] = lax.fori_loop(0, 4, one, (none, none))
        z_copy(1, h).start()
        return carry

    def forward(n, energy):
        for t in range(4):
            values, _ = masked(n * 4 + t)
            energy = energy + fold(values * values)
        return energy

    def inner(left, right):
        return fold(left[0] * right[0] + left[1] * right[1])

    lane = lax.broadcasted_iota(jnp.int32, (1, 128), 1)

    def share(which, stage, peers, me):
        for peer in peers:
            send(message.at[which, stage], sums.at[which, stage, me],
                 sum_send.at[which, stage], sum_recv.at[which, stage], peer)
        sums[which, stage, me] = message[which, stage]

    def collect(which, stage, peers):
        lines = sums.at[which, stage, pl.ds(0, len(peers))]
        arrived(lines, sum_recv.at[which, stage])
        departed(lines, sum_send.at[which, stage])
        return jnp.sum(sums[which, stage, :len(peers) + 1], axis=0)

    def first_group(which):
        if which == 2:
            return near_peers, lax.rem(ring, 4) * 2 + c
        return column_peers, ring * 2 + c

    def reduce_start(which, parts):
        line = jnp.zeros((1, 128), F32)
        for n, value in enumerate(parts):
            line = jnp.where(lane == n, total(value), line)
        message[which, 0] = line
        share(which, 0, *first_group(which))

    def reduce_end(which, count, meanwhile):
        message[which, 1] = collect(which, 0, first_group(which)[0])
        share(which, 1, plane_peers, y * 4 + x)
        meanwhile()
        line = collect(which, 1, plane_peers)
        return [line[:, n:n + 1] for n in range(count)]

    def publish(n, h):
        lines = fields.at[n, 1 + c, y, :, half(h)]
        for step in (1, 2, 3):
            send(lines, lines, along_send.at[n], along_recv.at[n], at_y(step))

    def near_copy(n, which):
        mine = fields.at[n, 1 + c, y]
        target, device = ((mine, sibling), (fields.at[n, 3 - 3 * c, y], across))[which]
        return remote(mine, target, near_send.at[n, which], near_recv.at[n, which], device)

    def announce(n):
        near_copy(n, 0).start()
        near_copy(n, 1).start()

    def greet(n):
        near_copy(n, 0).wait_recv()
        near_copy(n, 1).wait_recv()

    def pass_on(n):
        arrived(fields.at[n, 1 + c, pl.ds(0, 3)], along_recv.at[n])
        for slot in (1, 2, 3):
            line = lax.rem(y + slot, 4)
            plane = fields.at[n, 1 + c, line]
            send(plane, fields.at[n, 3 - 3 * c, line], pass_send.at[n, 1], pass_recv.at[n, 1], across)
            send(plane, plane, pass_send.at[n, 0], pass_recv.at[n, 0], sibling)

    def far_copy(n):
        planes = fields.at[n, 3 * c]
        return remote(planes, planes, far_send.at[n], far_recv.at[n], sibling)

    def hand_over(n):
        arrived(fields.at[n, 3 * c, pl.ds(0, 3)], pass_recv.at[n, 1])
        far_copy(n).start()

    def settle(n):
        arrived(fields.at[n, 2 - c, pl.ds(0, 3)], pass_recv.at[n, 0])
        far_copy(n).wait_recv()

    zero = jnp.zeros((8, 128), F32)
    arrived(maps.at[0, c], map_sib_recv.at[0])
    arrived(rest, map_sib_recv.at[1])
    for h in range(2):
        at = half(h)
        z_copy(0, h).wait_recv()
        rhs[:, at] = to_z[0, :, at] + from_z[0, :, at]
        publish(0, h)
        spread(rhs, h)
    announce(0)
    energy = lax.fori_loop(0, 4, normal, zero)
    reduce_start(0, [0.5 * inner(rhs, rhs), energy])
    lax.fori_loop(0, 2, gather, 0)
    norm_0, energy_0 = reduce_end(0, 2, lambda: pass_on(0))
    curve_0 = energy_0 + 0.1 * norm_0
    alpha_0 = norm_0 / curve_0
    for h in range(2):
        at = half(h)
        z_copy(1, h).wait_recv()
        quad[:, at] = to_z[1, :, at] + from_z[1, :, at] + 0.1 * rhs[:, at]
        resid[:, at] = rhs[:, at] - alpha_0 * quad[:, at]
        publish(1, h)
        if h == 1:
            announce(1)
        spread(resid, h)
    greet(0)
    hand_over(0)
    energy = lax.fori_loop(0, 4, forward, zero)
    reduce_start(1, [0.5 * inner(resid, resid), 0.5 * inner(resid, quad), energy])
    norm_1, cross, energy_1 = reduce_end(1, 3, lambda: pass_on(1))
    beta = norm_1 / norm_0
    curve_1 = energy_1 + 0.1 * norm_1 + 2.0 * beta * cross + beta * beta * curve_0
    alpha_1 = norm_1 / curve_1
    on_rhs = alpha_0 + alpha_1 * beta
    greet(1)

    def iterate(place, line):
        return on_rhs * fields[0, place, line] + alpha_1 * fields[1, place, line]

    def length(gap):
        return jnp.sqrt(gap[0] * gap[0] + gap[1] * gap[1])

    gap = jnp.where(2 * b + c < BINS - 1, iterate(2 + c, y) - iterate(1 + c, y), 0.0)
    reduce_start(2, [fold(length(gap))])

    def differences(line, carry):
        values = [iterate(place, line) for place in range(4)]
        result[line, 0] = values[1]
        result[line, 1] = values[2]
        for n, keep in enumerate((b > 0, None, b < BIN_AXIS - 1)):
            gap = values[n + 1] - values[n]
            if keep is not None:
                gap = jnp.where(keep, gap, 0.0)
            gaps[line, n] = gap
            sizes[line, n] = 1.0 / length(gap)
        return carry

    def prepare():
        hand_over(1)
        settle(0)
        settle(1)
        lax.fori_loop(0, SL, differences, 0)

    (size_sum,) = reduce_end(2, 1, prepare)
    lam = size_sum / COUNT + 1e-06

    def out_copy(line):
        return pltpu.make_async_copy(result.at[line], out.at[:, line], out_sem.at[line])

    def finish(line, carry):
        dual = [
            gaps[line, n] * jnp.minimum(lam * sizes[line, n], 1.0)[None] for n in range(3)
        ]
        for n in range(2):
            result[line, n] = result[line, n] + 0.25 * (dual[n + 1] - dual[n])
        out_copy(line).start()
        return carry

    lax.fori_loop(0, SL, finish, 0)
    for k in range(4):
        sib_copy(k).wait_send()
    departed(slots, map_send)
    departed(turned, turn_send)
    departed(maps.at[0, c], map_sib_send.at[0])
    departed(rest, map_sib_send.at[1])
    departed(to_y, y_send)
    for n in range(2):
        for h in range(2):
            z_copy(n, h).wait_send()
        near_copy(n, 0).wait_send()
        near_copy(n, 1).wait_send()
        departed(fields.at[n, 1 + c, pl.ds(0, 3)], along_send.at[n])
        for which in range(2):
            departed(fields.at[n, 1 + c, pl.ds(0, 3)], pass_send.at[n, which])
        far_copy(n).wait_send()
    for line in range(SL):
        out_copy(line).wait()


def on_device(kspace, coil_maps, sample_mask):
    dma = pltpu.SemaphoreType.DMA
    whole = pl.BlockSpec(memory_space=pl.ANY)
    return pl.pallas_call(
        kernel,
        out_shape=jax.ShapeDtypeStruct((2, SL) + PLANE, F32),
        in_specs=[whole] * 5,
        out_specs=whole,
        scratch_shapes=[
            pltpu.VMEM((4, 2, 2) + PLANE, F32),
            pltpu.VMEM((2, SL) + PLANE, F32),
            pltpu.VMEM(PLANE, jnp.int32),
            pltpu.VMEM((2, 2, 2 * NY, 2 * NY), BF16),
            pltpu.VMEM((2, 2, 2 * NZ, 2 * NZ), BF16),
            pltpu.VMEM((4, 2, 2) + PLANE, F32),
            pltpu.VMEM(PLANE, F32),
            pltpu.VMEM((2, 16 * HALF, 2 * NY), BF16),
            pltpu.VMEM((2, 16 * HALF, 2 * NY), BF16),
            pltpu.VMEM((2, 16 * HALF, 2 * NY), F32),
            pltpu.VMEM((4, 2) + PLANE, F32),
            pltpu.VMEM((4,) + PLANE, F32),
            pltpu.VMEM((3,) + PLANE, F32),
            pltpu.VMEM((3,) + PLANE, F32),
            pltpu.VMEM((2,) + PLANE, F32),
            pltpu.VMEM((2,) + PLANE, F32),
            pltpu.VMEM((2, 4, SL) + PLANE, F32),
            pltpu.VMEM(PLANE, F32),
            pltpu.VMEM((SL, 3) + PLANE, F32),
            pltpu.VMEM((SL, 3, NZ, NY), F32),
            pltpu.VMEM((SL, 2) + PLANE, F32),
            pltpu.VMEM((3, 2, 1, 128), F32),
            pltpu.VMEM((3, 2, 16, 1, 128), F32),
            dma((5,)), dma((4,)), dma(()),
            dma(()), dma(()), dma(()), dma(()), dma((2,)), dma((2,)),
            dma((4,)), dma((4,)), dma(()), dma((2,)), dma((2, 2)), dma((2, 2)),
            dma((2, 2)), dma((2, 2)), dma((2,)), dma((2,)),
            dma((2, 2)), dma((2, 2)), dma((2,)), dma((2,)),
            dma((3, 2)), dma((3, 2)), dma((SL,)),
        ],
        compiler_params=pltpu.CompilerParams(
            collective_id=0, has_side_effects=True, vmem_limit_bytes=60 * 1024 * 1024
        ),
        cost_estimate=pl.CostEstimate(flops=20_000_000_000, bytes_accessed=10_000_000, transcendentals=0),
    )(kspace, coil_maps, sample_mask, jnp.asarray(row_tables()), jnp.asarray(col_tables()))


def solution(mesh):
    return jax.shard_map(
        on_device,
        mesh=mesh,
        in_specs=(
            P("bin", "coil", None, None, None, None),
            P("coil", None, None, None, None),
            P("bin", None, None),
        ),
        out_specs=P("bin", None, None, None, None),
        check_vma=False,
    )
```

```python
import math

import jax
import jax.numpy as jnp
import numpy as np
from jax import lax
from jax.experimental import pallas as pl
from jax.experimental.pallas import tpu as pltpu
from jax.sharding import PartitionSpec as P

MESH = pl.DeviceIdType.MESH
F32 = jnp.float32
BF16 = jnp.bfloat16
NZ, NY, SL = 96, 256, 4
BIN_AXIS, COIL_AXIS = 16, 16
BINS = 32
COUNT = (BINS - 1) * SL * NZ * NY
PLANE = (2, NZ, NY)
HALF = NZ // 2
CHUNK = NZ // 4


def dft_tables(length):
    index = np.arange(length)
    angle = (index[:, None] * index[None, :] % length) * (2.0 * math.pi / length)
    factor = 1.0 / math.sqrt(length)
    return np.cos(angle) * factor, np.sin(angle) * factor


def halves(table):
    high = table.astype(np.float32).astype(jnp.bfloat16)
    low = (table - high.astype(np.float64)).astype(np.float32).astype(jnp.bfloat16)
    return np.stack([high, low])


def row_tables():
    cos, sin = dft_tables(NY)
    forward = np.block([[cos, -sin], [sin, cos]])
    return np.stack([halves(forward), halves(forward.T)])


def col_tables():
    cos, sin = dft_tables(NZ)
    forward = np.block([[cos, sin], [-sin, cos]])
    return np.stack([halves(forward), halves(forward.T)])


def split(values):
    high = values.astype(BF16)
    return high, (values - high.astype(F32)).astype(BF16)


def dot(left, right):
    return jnp.dot(left, right, preferred_element_type=F32)


def rows(high, low, table, which):
    return dot(high, table[which, 0]) + dot(low, table[which, 0]) + dot(high, table[which, 1])


def cols(values, table, which):
    high, low = split(values)
    return dot(table[which, 0], high) + dot(table[which, 0], low) + dot(table[which, 1], high)


def fold(values):
    part = jnp.sum(values.reshape(values.shape[0] // 8, 8, NY), axis=0)
    return part[:, :128] + part[:, 128:]


def total(values):
    return jnp.sum(values, keepdims=True)


def kernel(
    kspace, coil_maps, mask, row_table, col_table, out,
    samples, own_maps, ticks, row, col, maps, weight, high, low, lines_high, lines_low, mid,
    part, from_sib, to_y, from_y, to_z, from_z,
    fields, quad, gaps, sizes, result, message, sums,
    load_sem, sample_sem, slot_sem,
    map_send, map_recv, turn_send, turn_recv, map_sib_send, map_sib_recv,
    sib_send, sib_recv, y_send, y_recv, z_send, z_recv,
    near_send, near_recv, along_send, along_recv, pass_send, pass_recv, far_send, far_recv, core_send, core_recv,
    sum_send, sum_recv, out_sem,
):
    b = lax.axis_index("bin")
    j = lax.axis_index("coil")
    y, z, c = j // 4, (j // 2) % 2, j % 2
    x = lax.rem(b, 4)
    ring = z * 4 + b // 4

    def at_y(step):
        return (b, lax.rem(y + step, 4) * 4 + z * 2 + c)

    def at_xz(step_x, step_z, core):
        place = lax.rem(ring + step_z + 8, 8)
        return (
            lax.rem(place, 4) * 4 + lax.rem(x + step_x + 4, 4),
            y * 4 + place // 4 * 2 + core,
        )

    rhs = fields.at[0, 1 + c, y]
    resid = fields.at[1, 1 + c, y]
    sibling = (b, j + 1 - 2 * c)
    opposite = (b, j + 2 - 4 * z)
    wraps = jnp.where(c == 1, jnp.where(x == 3, 1, 0), jnp.where(x == 0, -1, 0))
    across = at_xz(2 * c - 1, wraps, 1 - c)
    column_peers = [at_xz(0, step // 2, lax.rem(c + step, 2)) for step in range(1, 16)]
    near_peers = [
        at_xz(0, dz, core) for dz in (0, 1, 2, -1) for core in (c, 1 - c)
    ][1:]
    plane_peers = [
        (b - x + lax.rem(x + step % 4, 4), lax.rem(y + step // 4, 4) * 4 + z * 2 + c) for step in range(1, 16)
    ]

    def remote(source, target, send_sem, recv_sem, device):
        return pltpu.make_async_remote_copy(
            src_ref=source, dst_ref=target, send_sem=send_sem, recv_sem=recv_sem,
            device_id=device, device_id_type=MESH,
        )

    def send(*args):
        copy = remote(*args)
        copy.start()
        return copy

    def arrived(ref, sem):
        remote(ref, ref, sem, sem, sibling).wait_recv()

    def departed(ref, sem):
        remote(ref, ref, sem, sem, sibling).wait_send()

    def load(source, target, sem):
        copy = pltpu.make_async_copy(source, target, sem)
        copy.start()
        return copy

    def sample_copy(k):
        return pltpu.make_async_copy(
            kspace.at[:, :, lax.rem(y + 3 - k, 4)], samples.at[k], sample_sem.at[k]
        )

    barrier = pltpu.get_barrier_semaphore()
    greeted = column_peers + plane_peers + [across]
    for device in greeted:
        pl.semaphore_signal(barrier, inc=1, device_id=device, device_id_type=MESH)
    loads = [load(mask, ticks, load_sem.at[0]), load(row_table.at[1], row.at[1], load_sem.at[1])]
    sample_copy(0).start()
    loads += [load(col_table, col, load_sem.at[2]), load(coil_maps, own_maps, load_sem.at[3])]
    for k in (1, 2, 3):
        sample_copy(k).start()
    late_load = load(row_table.at[0], row.at[0], load_sem.at[4])
    slot_copy = load(coil_maps.at[:, y], maps.at[0, c], slot_sem)
    loads[0].wait()
    weight[0] = ticks[0].astype(F32)
    weight[1] = ticks[1].astype(F32)
    for copy in loads[1:]:
        copy.wait()

    def half(h):
        return pl.ds(pl.multiple_of(h * HALF, 16), HALF)

    def sib_copy(k):
        return remote(part.at[k, 1 - c], from_sib.at[k], sib_send.at[k], sib_recv.at[k], sibling)

    def chunk(r):
        return pl.ds(r * CHUNK, CHUNK)

    def y_start(r):
        for k in range(3):
            send(to_y.at[k, :, chunk(r)], from_y.at[k, :, chunk(r)], y_send, y_recv.at[r], at_y(3 - k))

    def first_z(r):
        return remote(
            to_z.at[0, :, chunk(r)], from_z.at[0, :, chunk(r)], z_send.at[0], z_recv.at[r], opposite
        )

    def second_z(h):
        return remote(
            to_z.at[1, :, half(h)], from_z.at[1, :, half(h)], z_send.at[1], z_recv.at[4 + h], opposite
        )

    def adjoint(k, carry):
        s = lax.rem(y + 3 - k, 4)
        sample_copy(k).wait()
        for t in range(4):
            w = weight[t // 2]
            values = jnp.concatenate(
                [samples[k, t // 2, t % 2, 0] * w, samples[k, t // 2, t % 2, 1] * w], axis=1
            )
            lines_high[t * NZ:(t + 1) * NZ], lines_low[t * NZ:(t + 1) * NZ] = split(values)
        mid[:4 * NZ] = rows(lines_high[...], lines_low[...], row, 1)
        for bin_ in range(2):
            sum_re, sum_im = 0.0, 0.0
            for coil in range(2):
                at = pl.ds((bin_ * 2 + coil) * NZ, NZ)
                wave = cols(jnp.concatenate([mid[at, :NY], mid[at, NY:]], axis=0), col, 1)
                sens_re, sens_im = own_maps[coil, s, 0], own_maps[coil, s, 1]
                sum_re += sens_re * wave[:NZ] + sens_im * wave[NZ:]
                sum_im += sens_re * wave[NZ:] - sens_im * wave[:NZ]
            part[k, bin_, 0] = sum_re
            part[k, bin_, 1] = sum_im
        return carry

    lax.fori_loop(0, 4, adjoint, 0)
    pl.semaphore_wait(barrier, len(greeted))
    for k in range(4):
        sib_copy(k).start()
    quarter = pl.ds(pl.multiple_of(x * (NZ // 4), 8), NZ // 4)
    for step in (1, 2, 3):
        send(coil_maps.at[:, lax.rem(y + step, 4), :, quarter], maps.at[4 - step, c, :, :, quarter],
             map_send, map_recv, at_y(step))
    for k in range(3):
        sib_copy(k).wait_recv()
        to_y[k] = part[k, c] + from_sib[k]
    y_start(0)
    y_start(1)
    send(own_maps.at[:, y], maps.at[0, c], map_sib_send.at[0], map_sib_recv.at[0], sibling)
    slots = maps.at[pl.ds(1, 3), c, :, :, quarter]
    sib_copy(3).wait_recv()
    part[3, c] = part[3, c] + from_sib[3]
    arrived(slots, map_recv)
    for step in (1, 2, 3):
        send(slots, slots, turn_send, turn_recv, at_xz(step, 0, c))
    for r in range(4):
        at = chunk(r)
        arrived(from_y.at[:, :, at], y_recv.at[r])
        if r < 2:
            y_start(r + 2)
        to_z[0, :, at] = part[3, c, :, at] + from_y[0, :, at] + from_y[1, :, at] + from_y[2, :, at]
        first_z(r).start()
    turned = maps.at[pl.ds(1, 3), c, :, :, pl.ds(0, 3 * (NZ // 4))]
    rest = maps.at[pl.ds(1, 3), c]
    slot_copy.wait()
    late_load.wait()

    def pair(n):
        late = n - 2
        slot = jnp.where(n < 2, 0, 1 + lax.rem(late + 3, 3))
        flip = jnp.where(n < 2, n, jnp.where(late < 3, 0, 1))
        return slot, lax.rem(c + flip, 2)

    def spread(field, n):
        for t in range(4):
            slot, core = pair(2 * n + t // 2)
            sens_re, sens_im = maps[slot, core, t % 2, 0], maps[slot, core, t % 2, 1]
            values = jnp.concatenate(
                [sens_re * field[0] - sens_im * field[1], sens_re * field[1] + sens_im * field[0]], axis=1
            )
            lines_high[t * NZ:(t + 1) * NZ], lines_low[t * NZ:(t + 1) * NZ] = split(values)
        mid[:4 * NZ] = rows(lines_high[...], lines_low[...], row, 0)

    def masked(t):
        at = pl.ds(t * NZ, NZ)
        values = cols(jnp.concatenate([mid[at, :NY], mid[at, NY:]], axis=0), col, 0)
        w = weight[c]
        return values * jnp.concatenate([w, w], axis=0)

    def normal(n, energy):
        @pl.when(n == 1)
        def _():
            arrived(turned, turn_recv)
            send(rest, rest, map_sib_send.at[1], map_sib_recv.at[1], sibling)

        @pl.when(n == 2)
        def _():
            arrived(rest, map_sib_recv.at[1])

        spread(rhs, n)
        for t in range(4):
            values = masked(t)
            energy = energy + fold(values * values)
            wave = cols(values, col, 1)
            at = pl.ds(pl.multiple_of((n * 4 + t) * HALF, 16), HALF)
            for h in range(2):
                lines = jnp.concatenate(
                    [wave[h * HALF:(h + 1) * HALF], wave[NZ + h * HALF:NZ + (h + 1) * HALF]], axis=1
                )
                high[h, at], low[h, at] = split(lines)
        return energy

    def gather(h, carry):
        mid[...] = rows(high[h], low[h], row, 1)
        at = half(h)

        def one(n, sums_):
            sum_re, sum_im = sums_
            for t in range(4):
                lines = pl.ds(pl.multiple_of((n * 4 + t) * HALF, 16), HALF)
                slot, core = pair(2 * n + t // 2)
                sens_re, sens_im = maps[slot, core, t % 2, 0, at], maps[slot, core, t % 2, 1, at]
                sum_re += sens_re * mid[lines, :NY] + sens_im * mid[lines, NY:]
                sum_im += sens_re * mid[lines, NY:] - sens_im * mid[lines, :NY]
            return sum_re, sum_im

        none = jnp.zeros((HALF, NY), F32)
        to_z[1, 0, at], to_z[1, 1, at] = lax.fori_loop(0, 4, one, (none, none))
        second_z(h).start()
        return carry

    def forward(n, energy):
        spread(resid, n)
        for t in range(4):
            values = masked(t)
            energy = energy + fold(values * values)
        return energy

    def inner(left, right):
        return fold(left[0] * right[0] + left[1] * right[1])

    lane = lax.broadcasted_iota(jnp.int32, (1, 128), 1)

    def share(which, stage, peers, me):
        for peer in peers:
            send(message.at[which, stage], sums.at[which, stage, me],
                 sum_send.at[which, stage], sum_recv.at[which, stage], peer)
        sums[which, stage, me] = message[which, stage]

    def collect(which, stage, peers):
        lines = sums.at[which, stage, pl.ds(0, len(peers))]
        arrived(lines, sum_recv.at[which, stage])
        departed(lines, sum_send.at[which, stage])
        return jnp.sum(sums[which, stage, :len(peers) + 1], axis=0)

    def first_group(which):
        if which == 2:
            return near_peers, lax.rem(ring, 4) * 2 + c
        return column_peers, ring * 2 + c

    def reduce_start(which, parts):
        line = jnp.zeros((1, 128), F32)
        for n, value in enumerate(parts):
            line = jnp.where(lane == n, total(value), line)
        message[which, 0] = line
        share(which, 0, *first_group(which))

    def reduce_end(which, count, meanwhile):
        message[which, 1] = collect(which, 0, first_group(which)[0])
        share(which, 1, plane_peers, y * 4 + x)
        meanwhile()
        line = collect(which, 1, plane_peers)
        return [line[:, n:n + 1] for n in range(count)]

    def publish(n, h):
        lines = fields.at[n, 1 + c, y, :, half(h)]
        for step in (1, 2, 3):
            send(lines, lines, along_send.at[n], along_recv.at[n], at_y(step))

    def near_copy(n, which):
        mine = fields.at[n, 1 + c, y]
        target, device = ((mine, sibling), (fields.at[n, 3 - 3 * c, y], across))[which]
        return remote(mine, target, near_send.at[n, which], near_recv.at[n, which], device)

    def announce(n):
        near_copy(n, 0).start()
        near_copy(n, 1).start()

    def extend(n):
        near_copy(n, 1).wait_recv()
        plane = fields.at[n, 3 * c, y]
        for step in (1, 3):
            send(plane, plane, far_send.at[n], far_recv.at[n], at_y(step))

    def pass_on(n):
        arrived(fields.at[n, 1 + c, pl.ds(0, 3)], along_recv.at[n])
        facing = lax.rem(y + 2, 4)
        plane = fields.at[n, 1 + c, facing]
        send(plane, fields.at[n, 3 - 3 * c, facing], pass_send.at[n], pass_recv.at[n], across)
        for slot in (1, 2, 3):
            plane = fields.at[n, 1 + c, lax.rem(y + slot, 4)]
            send(plane, plane, core_send.at[n, 0], core_recv.at[n, 0], sibling)

    def hand_over(n):
        arrived(fields.at[n, 3 * c, pl.ds(0, 2)], far_recv.at[n])
        arrived(fields.at[n, 3 * c, 0], pass_recv.at[n])
        planes = fields.at[n, 3 * c]
        send(planes, planes, core_send.at[n, 1], core_recv.at[n, 1], sibling)

    def settle(n):
        arrived(fields.at[n, 2 - c, pl.ds(0, 3)], core_recv.at[n, 0])
        arrived(fields.at[n, 3 - 3 * c], core_recv.at[n, 1])

    zero = jnp.zeros((8, 128), F32)
    arrived(maps.at[0, c], map_sib_recv.at[0])
    for r in range(4):
        at = chunk(r)
        first_z(r).wait_recv()
        rhs[:, at] = to_z[0, :, at] + from_z[0, :, at]
        if r % 2 == 1:
            publish(0, r // 2)
    announce(0)
    energy = lax.fori_loop(0, 4, normal, zero)
    reduce_start(0, [0.5 * inner(rhs, rhs), energy])
    extend(0)
    lax.fori_loop(0, 2, gather, 0)
    norm_0, energy_0 = reduce_end(0, 2, lambda: pass_on(0))
    curve_0 = energy_0 + 0.1 * norm_0
    alpha_0 = norm_0 / curve_0
    for h in range(2):
        at = half(h)
        second_z(h).wait_recv()
        quad[:, at] = to_z[1, :, at] + from_z[1, :, at] + 0.1 * rhs[:, at]
        resid[:, at] = rhs[:, at] - alpha_0 * quad[:, at]
        publish(1, h)
    announce(1)
    near_copy(0, 0).wait_recv()
    hand_over(0)
    energy = lax.fori_loop(0, 4, forward, zero)
    reduce_start(1, [0.5 * inner(resid, resid), 0.5 * inner(resid, quad), energy])
    extend(1)
    norm_1, cross, energy_1 = reduce_end(1, 3, lambda: pass_on(1))
    beta = norm_1 / norm_0
    curve_1 = energy_1 + 0.1 * norm_1 + 2.0 * beta * cross + beta * beta * curve_0
    alpha_1 = norm_1 / curve_1
    on_rhs = alpha_0 + alpha_1 * beta
    near_copy(1, 0).wait_recv()

    def iterate(place, line):
        return on_rhs * fields[0, place, line] + alpha_1 * fields[1, place, line]

    def length(gap):
        return jnp.sqrt(gap[0] * gap[0] + gap[1] * gap[1])

    gap = jnp.where(2 * b + c < BINS - 1, iterate(2 + c, y) - iterate(1 + c, y), 0.0)
    reduce_start(2, [fold(length(gap))])

    def differences(line, carry):
        values = [iterate(place, line) for place in range(4)]
        result[line, 0] = values[1]
        result[line, 1] = values[2]
        for n, keep in enumerate((b > 0, None, b < BIN_AXIS - 1)):
            gap = values[n + 1] - values[n]
            if keep is not None:
                gap = jnp.where(keep, gap, 0.0)
            gaps[line, n] = gap
            sizes[line, n] = 1.0 / length(gap)
        return carry

    def prepare():
        hand_over(1)
        settle(0)
        settle(1)
        lax.fori_loop(0, SL, differences, 0)

    (size_sum,) = reduce_end(2, 1, prepare)
    lam = size_sum / COUNT + 1e-06

    def out_copy(line):
        return pltpu.make_async_copy(result.at[line], out.at[:, line], out_sem.at[line])

    def finish(line, carry):
        dual = [
            gaps[line, n] * jnp.minimum(lam * sizes[line, n], 1.0)[None] for n in range(3)
        ]
        for n in range(2):
            result[line, n] = result[line, n] + 0.25 * (dual[n + 1] - dual[n])
        out_copy(line).start()
        return carry

    lax.fori_loop(0, SL, finish, 0)
    for k in range(4):
        sib_copy(k).wait_send()
    departed(slots, map_send)
    departed(turned, turn_send)
    departed(maps.at[0, c], map_sib_send.at[0])
    departed(rest, map_sib_send.at[1])
    departed(to_y, y_send)
    for n in range(2):
        departed(to_z.at[n], z_send.at[n])
        near_copy(n, 0).wait_send()
        near_copy(n, 1).wait_send()
        departed(fields.at[n, 1 + c, pl.ds(0, 3)], along_send.at[n])
        departed(fields.at[n, 3 * c, pl.ds(0, 2)], far_send.at[n])
        departed(fields.at[n, 1 + c, 0], pass_send.at[n])
        departed(fields.at[n, 1 + c, pl.ds(0, 3)], core_send.at[n, 0])
        departed(fields.at[n, 3 * c], core_send.at[n, 1])
    for line in range(SL):
        out_copy(line).wait()


def on_device(kspace, coil_maps, sample_mask):
    dma = pltpu.SemaphoreType.DMA
    whole = pl.BlockSpec(memory_space=pl.ANY)
    return pl.pallas_call(
        kernel,
        out_shape=jax.ShapeDtypeStruct((2, SL) + PLANE, F32),
        in_specs=[whole] * 5,
        out_specs=whole,
        scratch_shapes=[
            pltpu.VMEM((4, 2, 2) + PLANE, F32),
            pltpu.VMEM((2, SL) + PLANE, F32),
            pltpu.VMEM(PLANE, jnp.int32),
            pltpu.VMEM((2, 2, 2 * NY, 2 * NY), BF16),
            pltpu.VMEM((2, 2, 2 * NZ, 2 * NZ), BF16),
            pltpu.VMEM((4, 2, 2) + PLANE, F32),
            pltpu.VMEM(PLANE, F32),
            pltpu.VMEM((2, 16 * HALF, 2 * NY), BF16),
            pltpu.VMEM((2, 16 * HALF, 2 * NY), BF16),
            pltpu.VMEM((4 * NZ, 2 * NY), BF16),
            pltpu.VMEM((4 * NZ, 2 * NY), BF16),
            pltpu.VMEM((16 * HALF, 2 * NY), F32),
            pltpu.VMEM((4, 2) + PLANE, F32),
            pltpu.VMEM((4,) + PLANE, F32),
            pltpu.VMEM((3,) + PLANE, F32),
            pltpu.VMEM((3,) + PLANE, F32),
            pltpu.VMEM((2,) + PLANE, F32),
            pltpu.VMEM((2,) + PLANE, F32),
            pltpu.VMEM((2, 4, SL) + PLANE, F32),
            pltpu.VMEM(PLANE, F32),
            pltpu.VMEM((SL, 3) + PLANE, F32),
            pltpu.VMEM((SL, 3, NZ, NY), F32),
            pltpu.VMEM((SL, 2) + PLANE, F32),
            pltpu.VMEM((3, 2, 1, 128), F32),
            pltpu.VMEM((3, 2, 16, 1, 128), F32),
            dma((5,)), dma((4,)), dma(()),
            dma(()), dma(()), dma(()), dma(()), dma((2,)), dma((2,)),
            dma((4,)), dma((4,)), dma(()), dma((4,)), dma((2,)), dma((6,)),
            dma((2, 2)), dma((2, 2)), dma((2,)), dma((2,)),
            dma((2,)), dma((2,)), dma((2,)), dma((2,)), dma((2, 2)), dma((2, 2)),
            dma((3, 2)), dma((3, 2)), dma((SL,)),
        ],
        compiler_params=pltpu.CompilerParams(
            collective_id=0, has_side_effects=True, vmem_limit_bytes=60 * 1024 * 1024
        ),
        cost_estimate=pl.CostEstimate(flops=20_000_000_000, bytes_accessed=10_000_000, transcendentals=0),
    )(kspace, coil_maps, sample_mask, jnp.asarray(row_tables()), jnp.asarray(col_tables()))


def solution(mesh):
    return jax.shard_map(
        on_device,
        mesh=mesh,
        in_specs=(
            P("bin", "coil", None, None, None, None),
            P("coil", None, None, None, None),
            P("bin", None, None),
        ),
        out_specs=P("bin", None, None, None, None),
        check_vma=False,
    )
```

```python
import math

import jax
import jax.numpy as jnp
import numpy as np
from jax import lax
from jax.experimental import pallas as pl
from jax.experimental.pallas import tpu as pltpu
from jax.sharding import PartitionSpec as P

MESH = pl.DeviceIdType.MESH
F32 = jnp.float32
BF16 = jnp.bfloat16
NZ, NY, SL = 96, 256, 4
BIN_AXIS, COIL_AXIS = 16, 16
BINS = 32
COUNT = (BINS - 1) * SL * NZ * NY
PLANE = (2, NZ, NY)
HALF = NZ // 2
EDGES = (0, 8, 24, 40, 56, 72, 88, 96)
CHUNKS = len(EDGES) - 1


def dft_tables(length):
    index = np.arange(length)
    angle = (index[:, None] * index[None, :] % length) * (2.0 * math.pi / length)
    factor = 1.0 / math.sqrt(length)
    return np.cos(angle) * factor, np.sin(angle) * factor


def halves(table):
    high = table.astype(np.float32).astype(jnp.bfloat16)
    low = (table - high.astype(np.float64)).astype(np.float32).astype(jnp.bfloat16)
    return np.stack([high, low])


def row_tables():
    cos, sin = dft_tables(NY)
    return halves(np.block([[cos, sin], [-sin, cos]]))


def stacked(table, axis):
    high, low = halves(table)
    return np.concatenate([high, high, low], axis=axis)


def parity_tables():
    cos, sin = dft_tables(NY)
    tables = []
    for parity in range(2):
        part = (slice(0, NY // 2), slice(parity, None, 2))
        tables.append(np.block([[cos[part], -sin[part]], [sin[part], cos[part]]]))
    return np.stack([
        np.stack([stacked(table, 0) for table in tables]),
        np.stack([stacked(table.T, 0) for table in tables]),
    ])


def col_tables():
    cos, sin = dft_tables(NZ)
    forward = np.block([[cos, sin], [-sin, cos]])
    return np.stack([stacked(forward, 1), stacked(forward.T, 1)])


def parity_order():
    order = np.concatenate([np.arange(0, NY, 2), np.arange(1, NY, 2)])
    return np.eye(NY)[:, order].astype(jnp.bfloat16)


def split(values):
    high = values.astype(BF16)
    return high, (values - high.astype(F32)).astype(BF16)


def widened(values, axis):
    high, low = split(values)
    return jnp.concatenate([high, low, high], axis=axis)


def dot(left, right):
    return jnp.dot(left, right, preferred_element_type=F32)


def rows(high, low, table):
    return dot(high, table[0]) + dot(low, table[0]) + dot(high, table[1])


def cols(values, table, which):
    return dot(table[which], widened(values, 0))


def by_parity(real, imag):
    return [
        jnp.concatenate([real[:, part], imag[:, part]], axis=1)
        for part in (slice(0, NY // 2), slice(NY // 2, NY))
    ]


def fold(values):
    part = jnp.sum(values.reshape(values.shape[0] // 8, 8, NY), axis=0)
    return part[:, :128] + part[:, 128:]


def total(values):
    return jnp.sum(values, keepdims=True)


def kernel(
    kspace, coil_maps, mask, row_table, col_table, parity_table, order_table, out,
    samples, own_maps, ticks, row, col, half_row, order, maps, weight, lines_high, lines_low, first, lines, wide, mid,
    part, from_sib, to_y, from_y, to_z, from_z,
    fields, quad, gaps, sizes, result, message, sums,
    load_sem, sample_sem, slot_sem,
    map_send, map_recv, turn_send, turn_recv, map_sib_send, map_sib_recv,
    sib_send, sib_recv, y_send, y_recv, z_send, z_recv,
    near_send, near_recv, along_send, along_recv, pass_send, pass_recv, far_send, far_recv, core_send, core_recv,
    sum_send, sum_recv, out_sem,
):
    b = lax.axis_index("bin")
    j = lax.axis_index("coil")
    y, z, c = j // 4, (j // 2) % 2, j % 2
    x = lax.rem(b, 4)
    ring = z * 4 + b // 4

    def at_y(step):
        return (b, lax.rem(y + step, 4) * 4 + z * 2 + c)

    def at_xz(step_x, step_z, core):
        place = lax.rem(ring + step_z + 8, 8)
        return (
            lax.rem(place, 4) * 4 + lax.rem(x + step_x + 4, 4),
            y * 4 + place // 4 * 2 + core,
        )

    rhs = fields.at[0, 1 + c, y]
    resid = fields.at[1, 1 + c, y]
    sibling = (b, j + 1 - 2 * c)
    opposite = (b, j + 2 - 4 * z)
    wraps = jnp.where(c == 1, jnp.where(x == 3, 1, 0), jnp.where(x == 0, -1, 0))
    across = at_xz(2 * c - 1, wraps, 1 - c)
    column_peers = [at_xz(0, step // 2, lax.rem(c + step, 2)) for step in range(1, 16)]
    near_peers = [
        at_xz(0, dz, core) for dz in (0, 1, 2, -1) for core in (c, 1 - c)
    ][1:]
    plane_peers = [
        (b - x + lax.rem(x + step % 4, 4), lax.rem(y + step // 4, 4) * 4 + z * 2 + c) for step in range(1, 16)
    ]

    def remote(source, target, send_sem, recv_sem, device):
        return pltpu.make_async_remote_copy(
            src_ref=source, dst_ref=target, send_sem=send_sem, recv_sem=recv_sem,
            device_id=device, device_id_type=MESH,
        )

    def send(*args):
        copy = remote(*args)
        copy.start()
        return copy

    def arrived(ref, sem):
        remote(ref, ref, sem, sem, sibling).wait_recv()

    def departed(ref, sem):
        remote(ref, ref, sem, sem, sibling).wait_send()

    def load(source, target, sem):
        copy = pltpu.make_async_copy(source, target, sem)
        copy.start()
        return copy

    def sample_copy(k):
        return pltpu.make_async_copy(
            kspace.at[:, :, lax.rem(y + 3 - k, 4)], samples.at[k], sample_sem.at[k]
        )

    barrier = pltpu.get_barrier_semaphore()
    greeted = column_peers + plane_peers + [across]
    for device in greeted:
        pl.semaphore_signal(barrier, inc=1, device_id=device, device_id_type=MESH)
    loads = [load(mask, ticks, load_sem.at[0]), load(row_table, row, load_sem.at[1])]
    sample_copy(0).start()
    loads += [load(col_table, col, load_sem.at[2]), load(coil_maps, own_maps, load_sem.at[3]), load(order_table, order, load_sem.at[5])]
    for k in (1, 2, 3):
        sample_copy(k).start()
    late_load = load(parity_table, half_row, load_sem.at[4])
    slot_copy = load(coil_maps.at[:, y], maps.at[0, c], slot_sem)
    loads[0].wait()
    weight[0] = ticks[0].astype(F32)
    weight[1] = ticks[1].astype(F32)
    for copy in loads[1:]:
        copy.wait()
    weight[2] = dot(weight[c].astype(BF16), order[...])

    def half(h):
        return pl.ds(pl.multiple_of(h * HALF, 16), HALF)

    def sib_copy(k):
        return remote(part.at[k, 1 - c], from_sib.at[k], sib_send.at[k], sib_recv.at[k], sibling)

    def chunk(r):
        return pl.ds(EDGES[r], EDGES[r + 1] - EDGES[r])

    def y_start(r):
        for k in range(3):
            send(to_y.at[k, :, chunk(r)], from_y.at[k, :, chunk(r)], y_send, y_recv.at[r], at_y(3 - k))

    def first_z(r):
        return remote(
            to_z.at[0, :, chunk(r)], from_z.at[0, :, chunk(r)], z_send.at[0], z_recv.at[r], opposite
        )

    def second_z(h):
        return remote(
            to_z.at[1, :, half(h)], from_z.at[1, :, half(h)], z_send.at[1], z_recv.at[CHUNKS + h], opposite
        )

    def adjoint(k, carry):
        s = lax.rem(y + 3 - k, 4)
        sample_copy(k).wait()
        for t in range(4):
            w = weight[t // 2]
            values = jnp.concatenate(
                [samples[k, t // 2, t % 2, 0] * w, samples[k, t // 2, t % 2, 1] * w], axis=1
            )
            lines_high[t * NZ:(t + 1) * NZ], lines_low[t * NZ:(t + 1) * NZ] = split(values)
        first[...] = rows(lines_high[...], lines_low[...], row)
        for bin_ in range(2):
            sum_re, sum_im = 0.0, 0.0
            for coil in range(2):
                at = pl.ds((bin_ * 2 + coil) * NZ, NZ)
                wave = cols(jnp.concatenate([first[at, :NY], first[at, NY:]], axis=0), col, 1)
                sens_re, sens_im = own_maps[coil, s, 0], own_maps[coil, s, 1]
                sum_re += sens_re * wave[:NZ] + sens_im * wave[NZ:]
                sum_im += sens_re * wave[NZ:] - sens_im * wave[:NZ]
            part[k, bin_, 0] = sum_re
            part[k, bin_, 1] = sum_im
        return carry

    lax.fori_loop(0, 4, adjoint, 0)
    pl.semaphore_wait(barrier, len(greeted))
    for k in range(4):
        sib_copy(k).start()
    quarter = pl.ds(pl.multiple_of(x * (NZ // 4), 8), NZ // 4)
    for step in (1, 2, 3):
        send(coil_maps.at[:, lax.rem(y + step, 4), :, quarter], maps.at[4 - step, c, :, :, quarter],
             map_send, map_recv, at_y(step))
    for k in range(3):
        sib_copy(k).wait_recv()
        to_y[k] = part[k, c] + from_sib[k]
    y_start(0)
    y_start(1)
    send(own_maps.at[:, y], maps.at[0, c], map_sib_send.at[0], map_sib_recv.at[0], sibling)
    slots = maps.at[pl.ds(1, 3), c, :, :, quarter]
    sib_copy(3).wait_recv()
    part[3, c] = part[3, c] + from_sib[3]
    arrived(slots, map_recv)
    for step in (1, 2, 3):
        send(slots, slots, turn_send, turn_recv, at_xz(step, 0, c))
    for r in range(CHUNKS):
        at = chunk(r)
        arrived(from_y.at[:, :, at], y_recv.at[r])
        if r + 2 < CHUNKS:
            y_start(r + 2)
        to_z[0, :, at] = part[3, c, :, at] + from_y[0, :, at] + from_y[1, :, at] + from_y[2, :, at]
        first_z(r).start()
    turned = maps.at[pl.ds(1, 3), c, :, :, pl.ds(0, 3 * (NZ // 4))]
    rest = maps.at[pl.ds(1, 3), c]
    slot_copy.wait()
    late_load.wait()

    def pair(n):
        late = n - 2
        slot = jnp.where(n < 2, 0, 1 + lax.rem(late + 3, 3))
        flip = jnp.where(n < 2, n, jnp.where(late < 3, 0, 1))
        return slot, lax.rem(c + flip, 2)

    def spread(field, n):
        for t in range(4):
            slot, core = pair(2 * n + t // 2)
            sens_re, sens_im = maps[slot, core, t % 2, 0], maps[slot, core, t % 2, 1]
            left, right = by_parity(
                sens_re * field[0] - sens_im * field[1], sens_re * field[1] + sens_im * field[0]
            )
            lines[0, t * NZ:(t + 1) * NZ] = widened(left + right, 1)
            lines[1, t * NZ:(t + 1) * NZ] = widened(left - right, 1)
        for parity in range(2):
            mid[parity, :4 * NZ] = dot(lines[parity], half_row[0, parity])

    def masked(t):
        at = pl.ds(t * NZ, NZ)
        even, odd = mid[0, at], mid[1, at]
        mirror = jnp.concatenate([
            jnp.concatenate([even[:, :NY // 2], odd[:, :NY // 2]], axis=1),
            jnp.concatenate([even[:, NY // 2:], odd[:, NY // 2:]], axis=1),
        ], axis=0)
        w = weight[2]
        return cols(mirror, col, 0) * jnp.concatenate([w, w], axis=0)

    def normal(n, energy):
        @pl.when(n == 1)
        def _():
            arrived(turned, turn_recv)
            send(rest, rest, map_sib_send.at[1], map_sib_recv.at[1], sibling)

        @pl.when(n == 2)
        def _():
            arrived(rest, map_sib_recv.at[1])

        spread(rhs, n)
        for t in range(4):
            values = masked(t)
            energy = energy + fold(values * values)
            wave = cols(values, col, 1)
            at = pl.ds(pl.multiple_of((n * 4 + t) * HALF, 16), HALF)
            for parity, part_ in enumerate(by_parity(wave[:NZ], wave[NZ:])):
                for h in range(2):
                    wide[h, parity, at] = widened(part_[h * HALF:(h + 1) * HALF], 1)
        return energy

    def gather(h, carry):
        for parity in range(2):
            mid[parity] = dot(wide[h, parity], half_row[1, parity])
        at = half(h)

        def one(n, sums_):
            sum_re, sum_im = sums_
            for t in range(4):
                place = pl.ds(pl.multiple_of((n * 4 + t) * HALF, 16), HALF)
                slot, core = pair(2 * n + t // 2)
                sens_re, sens_im = maps[slot, core, t % 2, 0, at], maps[slot, core, t % 2, 1, at]
                even, odd = mid[0, place], mid[1, place]
                plus, minus = even + odd, even - odd
                wave_re = jnp.concatenate([plus[:, :NY // 2], minus[:, :NY // 2]], axis=1)
                wave_im = jnp.concatenate([plus[:, NY // 2:], minus[:, NY // 2:]], axis=1)
                sum_re += sens_re * wave_re + sens_im * wave_im
                sum_im += sens_re * wave_im - sens_im * wave_re
            return sum_re, sum_im

        none = jnp.zeros((HALF, NY), F32)
        to_z[1, 0, at], to_z[1, 1, at] = lax.fori_loop(0, 4, one, (none, none))
        second_z(h).start()
        return carry

    def forward(n, energy):
        spread(resid, n)
        for t in range(4):
            values = masked(t)
            energy = energy + fold(values * values)
        return energy

    def inner(left, right):
        return fold(left[0] * right[0] + left[1] * right[1])

    lane = lax.broadcasted_iota(jnp.int32, (1, 128), 1)

    def share(which, stage, peers, me):
        for peer in peers:
            send(message.at[which, stage], sums.at[which, stage, me],
                 sum_send.at[which, stage], sum_recv.at[which, stage], peer)
        sums[which, stage, me] = message[which, stage]

    def collect(which, stage, peers):
        lines = sums.at[which, stage, pl.ds(0, len(peers))]
        arrived(lines, sum_recv.at[which, stage])
        departed(lines, sum_send.at[which, stage])
        return jnp.sum(sums[which, stage, :len(peers) + 1], axis=0)

    def first_group(which):
        if which == 2:
            return near_peers, lax.rem(ring, 4) * 2 + c
        return column_peers, ring * 2 + c

    def reduce_start(which, parts):
        line = jnp.zeros((1, 128), F32)
        for n, value in enumerate(parts):
            line = jnp.where(lane == n, total(value), line)
        message[which, 0] = line
        share(which, 0, *first_group(which))

    def reduce_end(which, count, meanwhile):
        message[which, 1] = collect(which, 0, first_group(which)[0])
        share(which, 1, plane_peers, y * 4 + x)
        meanwhile()
        line = collect(which, 1, plane_peers)
        return [line[:, n:n + 1] for n in range(count)]

    def publish(n, h):
        lines = fields.at[n, 1 + c, y, :, half(h)]
        for step in (1, 2, 3):
            send(lines, lines, along_send.at[n], along_recv.at[n], at_y(step))

    def near_copy(n, which):
        mine = fields.at[n, 1 + c, y]
        target, device = ((mine, sibling), (fields.at[n, 3 - 3 * c, y], across))[which]
        return remote(mine, target, near_send.at[n, which], near_recv.at[n, which], device)

    def announce(n):
        near_copy(n, 0).start()
        near_copy(n, 1).start()

    def extend(n):
        near_copy(n, 1).wait_recv()
        plane = fields.at[n, 3 * c, y]
        for step in (1, 3):
            send(plane, plane, far_send.at[n], far_recv.at[n], at_y(step))

    def pass_on(n):
        arrived(fields.at[n, 1 + c, pl.ds(0, 3)], along_recv.at[n])
        facing = lax.rem(y + 2, 4)
        plane = fields.at[n, 1 + c, facing]
        send(plane, fields.at[n, 3 - 3 * c, facing], pass_send.at[n], pass_recv.at[n], across)
        for slot in (1, 2, 3):
            plane = fields.at[n, 1 + c, lax.rem(y + slot, 4)]
            send(plane, plane, core_send.at[n, 0], core_recv.at[n, 0], sibling)

    def hand_over(n):
        arrived(fields.at[n, 3 * c, pl.ds(0, 2)], far_recv.at[n])
        arrived(fields.at[n, 3 * c, 0], pass_recv.at[n])
        planes = fields.at[n, 3 * c]
        send(planes, planes, core_send.at[n, 1], core_recv.at[n, 1], sibling)

    def settle(n):
        arrived(fields.at[n, 2 - c, pl.ds(0, 3)], core_recv.at[n, 0])
        arrived(fields.at[n, 3 - 3 * c], core_recv.at[n, 1])

    zero = jnp.zeros((8, 128), F32)
    arrived(maps.at[0, c], map_sib_recv.at[0])
    for r in range(CHUNKS):
        at = chunk(r)
        first_z(r).wait_recv()
        rhs[:, at] = to_z[0, :, at] + from_z[0, :, at]
        if r == CHUNKS - 3:
            publish(0, 0)
    publish(0, 1)
    announce(0)
    energy = lax.fori_loop(0, 4, normal, zero)
    reduce_start(0, [0.5 * inner(rhs, rhs), energy])
    extend(0)
    lax.fori_loop(0, 2, gather, 0)
    norm_0, energy_0 = reduce_end(0, 2, lambda: pass_on(0))
    curve_0 = energy_0 + 0.1 * norm_0
    alpha_0 = norm_0 / curve_0
    for h in range(2):
        at = half(h)
        second_z(h).wait_recv()
        quad[:, at] = to_z[1, :, at] + from_z[1, :, at] + 0.1 * rhs[:, at]
        resid[:, at] = rhs[:, at] - alpha_0 * quad[:, at]
        publish(1, h)
    announce(1)
    near_copy(0, 0).wait_recv()
    hand_over(0)
    energy = lax.fori_loop(0, 4, forward, zero)
    reduce_start(1, [0.5 * inner(resid, resid), 0.5 * inner(resid, quad), energy])
    extend(1)
    norm_1, cross, energy_1 = reduce_end(1, 3, lambda: pass_on(1))
    beta = norm_1 / norm_0
    curve_1 = energy_1 + 0.1 * norm_1 + 2.0 * beta * cross + beta * beta * curve_0
    alpha_1 = norm_1 / curve_1
    on_rhs = alpha_0 + alpha_1 * beta
    near_copy(1, 0).wait_recv()

    def iterate(place, line):
        return on_rhs * fields[0, place, line] + alpha_1 * fields[1, place, line]

    def length(gap):
        return jnp.sqrt(gap[0] * gap[0] + gap[1] * gap[1])

    gap = jnp.where(2 * b + c < BINS - 1, iterate(2 + c, y) - iterate(1 + c, y), 0.0)
    reduce_start(2, [fold(length(gap))])

    def differences(line, carry):
        values = [iterate(place, line) for place in range(4)]
        result[line, 0] = values[1]
        result[line, 1] = values[2]
        for n, keep in enumerate((b > 0, None, b < BIN_AXIS - 1)):
            gap = values[n + 1] - values[n]
            if keep is not None:
                gap = jnp.where(keep, gap, 0.0)
            gaps[line, n] = gap
            sizes[line, n] = 1.0 / length(gap)
        return carry

    def prepare():
        hand_over(1)
        settle(0)
        settle(1)
        lax.fori_loop(0, SL, differences, 0)

    (size_sum,) = reduce_end(2, 1, prepare)
    lam = size_sum / COUNT + 1e-06

    def out_copy(line):
        return pltpu.make_async_copy(result.at[line], out.at[:, line], out_sem.at[line])

    def finish(line, carry):
        dual = [
            gaps[line, n] * jnp.minimum(lam * sizes[line, n], 1.0)[None] for n in range(3)
        ]
        for n in range(2):
            result[line, n] = result[line, n] + 0.25 * (dual[n + 1] - dual[n])
        out_copy(line).start()
        return carry

    lax.fori_loop(0, SL, finish, 0)
    for k in range(4):
        sib_copy(k).wait_send()
    departed(slots, map_send)
    departed(turned, turn_send)
    departed(maps.at[0, c], map_sib_send.at[0])
    departed(rest, map_sib_send.at[1])
    departed(to_y, y_send)
    for n in range(2):
        departed(to_z.at[n], z_send.at[n])
        near_copy(n, 0).wait_send()
        near_copy(n, 1).wait_send()
        departed(fields.at[n, 1 + c, pl.ds(0, 3)], along_send.at[n])
        departed(fields.at[n, 3 * c, pl.ds(0, 2)], far_send.at[n])
        departed(fields.at[n, 1 + c, 0], pass_send.at[n])
        departed(fields.at[n, 1 + c, pl.ds(0, 3)], core_send.at[n, 0])
        departed(fields.at[n, 3 * c], core_send.at[n, 1])
    for line in range(SL):
        out_copy(line).wait()


def on_device(kspace, coil_maps, sample_mask):
    dma = pltpu.SemaphoreType.DMA
    whole = pl.BlockSpec(memory_space=pl.ANY)
    return pl.pallas_call(
        kernel,
        out_shape=jax.ShapeDtypeStruct((2, SL) + PLANE, F32),
        in_specs=[whole] * 7,
        out_specs=whole,
        scratch_shapes=[
            pltpu.VMEM((4, 2, 2) + PLANE, F32),
            pltpu.VMEM((2, SL) + PLANE, F32),
            pltpu.VMEM(PLANE, jnp.int32),
            pltpu.VMEM((2, 2 * NY, 2 * NY), BF16),
            pltpu.VMEM((2, 2 * NZ, 6 * NZ), BF16),
            pltpu.VMEM((2, 2, 3 * NY, NY), BF16),
            pltpu.VMEM((NY, NY), BF16),
            pltpu.VMEM((4, 2, 2) + PLANE, F32),
            pltpu.VMEM((3, NZ, NY), F32),
            pltpu.VMEM((4 * NZ, 2 * NY), BF16),
            pltpu.VMEM((4 * NZ, 2 * NY), BF16),
            pltpu.VMEM((4 * NZ, 2 * NY), F32),
            pltpu.VMEM((2, 4 * NZ, 3 * NY), BF16),
            pltpu.VMEM((2, 2, 16 * HALF, 3 * NY), BF16),
            pltpu.VMEM((2, 16 * HALF, NY), F32),
            pltpu.VMEM((4, 2) + PLANE, F32),
            pltpu.VMEM((4,) + PLANE, F32),
            pltpu.VMEM((3,) + PLANE, F32),
            pltpu.VMEM((3,) + PLANE, F32),
            pltpu.VMEM((2,) + PLANE, F32),
            pltpu.VMEM((2,) + PLANE, F32),
            pltpu.VMEM((2, 4, SL) + PLANE, F32),
            pltpu.VMEM(PLANE, F32),
            pltpu.VMEM((SL, 3) + PLANE, F32),
            pltpu.VMEM((SL, 3, NZ, NY), F32),
            pltpu.VMEM((SL, 2) + PLANE, F32),
            pltpu.VMEM((3, 2, 1, 128), F32),
            pltpu.VMEM((3, 2, 16, 1, 128), F32),
            dma((6,)), dma((4,)), dma(()),
            dma(()), dma(()), dma(()), dma(()), dma((2,)), dma((2,)),
            dma((4,)), dma((4,)), dma(()), dma((CHUNKS,)), dma((2,)), dma((CHUNKS + 2,)),
            dma((2, 2)), dma((2, 2)), dma((2,)), dma((2,)),
            dma((2,)), dma((2,)), dma((2,)), dma((2,)), dma((2, 2)), dma((2, 2)),
            dma((3, 2)), dma((3, 2)), dma((SL,)),
        ],
        compiler_params=pltpu.CompilerParams(
            collective_id=0, has_side_effects=True, vmem_limit_bytes=60 * 1024 * 1024
        ),
        cost_estimate=pl.CostEstimate(flops=20_000_000_000, bytes_accessed=10_000_000, transcendentals=0),
    )(
        kspace, coil_maps, sample_mask, jnp.asarray(row_tables()), jnp.asarray(col_tables()),
        jnp.asarray(parity_tables()), jnp.asarray(parity_order()),
    )


def solution(mesh):
    return jax.shard_map(
        on_device,
        mesh=mesh,
        in_specs=(
            P("bin", "coil", None, None, None, None),
            P("coil", None, None, None, None),
            P("bin", None, None),
        ),
        out_specs=P("bin", None, None, None, None),
        check_vma=False,
    )
```

```python
import math

import jax
import jax.numpy as jnp
import numpy as np
from jax import lax
from jax.experimental import pallas as pl
from jax.experimental.pallas import tpu as pltpu
from jax.sharding import PartitionSpec as P

MESH = pl.DeviceIdType.MESH
F32 = jnp.float32
BF16 = jnp.bfloat16
NZ, NY, SL = 96, 256, 4
BIN_AXIS, COIL_AXIS = 16, 16
BINS = 32
COUNT = (BINS - 1) * SL * NZ * NY
PLANE = (2, NZ, NY)
HALF = NZ // 2
EDGES = (0, 32, 64, 96)
CHUNKS = len(EDGES) - 1


def dft_tables(length):
    index = np.arange(length)
    angle = (index[:, None] * index[None, :] % length) * (2.0 * math.pi / length)
    factor = 1.0 / math.sqrt(length)
    return np.cos(angle) * factor, np.sin(angle) * factor


def halves(table):
    high = table.astype(np.float32).astype(jnp.bfloat16)
    low = (table - high.astype(np.float64)).astype(np.float32).astype(jnp.bfloat16)
    return np.stack([high, low])


def row_tables():
    cos, sin = dft_tables(NY)
    return halves(np.block([[cos, sin], [-sin, cos]]))


def stacked(table, axis):
    high, low = halves(table)
    return np.concatenate([high, high, low], axis=axis)


def parity_tables():
    cos, sin = dft_tables(NY)
    tables = []
    for parity in range(2):
        part = (slice(0, NY // 2), slice(parity, None, 2))
        tables.append(np.block([[cos[part], -sin[part]], [sin[part], cos[part]]]))
    return np.stack([
        np.stack([stacked(table, 0) for table in tables]),
        np.stack([stacked(table.T, 0) for table in tables]),
    ])


def col_tables():
    cos, sin = dft_tables(NZ)
    forward = np.block([[cos, sin], [-sin, cos]])
    return np.stack([stacked(forward, 1), stacked(forward.T, 1)])


def parity_order():
    order = np.concatenate([np.arange(0, NY, 2), np.arange(1, NY, 2)])
    return np.eye(NY)[:, order].astype(jnp.bfloat16)


def split(values):
    high = values.astype(BF16)
    return high, (values - high.astype(F32)).astype(BF16)


def widened(values, axis):
    high, low = split(values)
    return jnp.concatenate([high, low, high], axis=axis)


def dot(left, right):
    return jnp.dot(left, right, preferred_element_type=F32)


def rows(high, low, table):
    return dot(high, table[0]) + dot(low, table[0]) + dot(high, table[1])


def cols(values, table, which):
    return dot(table[which], widened(values, 0))


def by_parity(real, imag):
    return [
        jnp.concatenate([real[:, part], imag[:, part]], axis=1)
        for part in (slice(0, NY // 2), slice(NY // 2, NY))
    ]


def fold(values):
    part = jnp.sum(values.reshape(values.shape[0] // 8, 8, NY), axis=0)
    return part[:, :128] + part[:, 128:]


def total(values):
    return jnp.sum(values, keepdims=True)


def kernel(
    kspace, coil_maps, mask, row_table, col_table, parity_table, order_table, out,
    samples, own_maps, ticks, row, col, half_row, order, maps, weight, lines_high, lines_low, first, lines, wide, mid,
    part, from_sib, to_y, from_y, to_z, from_z,
    fields, quad, gaps, sizes, result, message, sums,
    load_sem, sample_sem, slot_sem,
    map_send, map_recv, turn_send, turn_recv, map_sib_send, map_sib_recv,
    sib_send, sib_recv, y_send, y_recv, z_send, z_recv,
    near_send, near_recv, along_send, along_recv, pass_send, pass_recv, far_send, far_recv, core_send, core_recv,
    sum_send, sum_recv, out_sem,
):
    b = lax.axis_index("bin")
    j = lax.axis_index("coil")
    y, z, c = j // 4, (j // 2) % 2, j % 2
    x = lax.rem(b, 4)
    ring = z * 4 + b // 4

    def at_y(step):
        return (b, lax.rem(y + step, 4) * 4 + z * 2 + c)

    def at_xz(step_x, step_z, core):
        place = lax.rem(ring + step_z + 8, 8)
        return (
            lax.rem(place, 4) * 4 + lax.rem(x + step_x + 4, 4),
            y * 4 + place // 4 * 2 + core,
        )

    rhs = fields.at[0, 1 + c, y]
    resid = fields.at[1, 1 + c, y]
    sibling = (b, j + 1 - 2 * c)
    opposite = (b, j + 2 - 4 * z)
    wraps = jnp.where(c == 1, jnp.where(x == 3, 1, 0), jnp.where(x == 0, -1, 0))
    across = at_xz(2 * c - 1, wraps, 1 - c)
    column_peers = [at_xz(0, step // 2, lax.rem(c + step, 2)) for step in range(1, 16)]
    near_peers = [
        at_xz(0, dz, core) for dz in (0, 1, 2, -1) for core in (c, 1 - c)
    ][1:]
    plane_peers = [
        (b - x + lax.rem(x + step % 4, 4), lax.rem(y + step // 4, 4) * 4 + z * 2 + c) for step in range(1, 16)
    ]

    def remote(source, target, send_sem, recv_sem, device):
        return pltpu.make_async_remote_copy(
            src_ref=source, dst_ref=target, send_sem=send_sem, recv_sem=recv_sem,
            device_id=device, device_id_type=MESH,
        )

    def send(*args):
        copy = remote(*args)
        copy.start()
        return copy

    def arrived(ref, sem):
        remote(ref, ref, sem, sem, sibling).wait_recv()

    def departed(ref, sem):
        remote(ref, ref, sem, sem, sibling).wait_send()

    def load(source, target, sem):
        copy = pltpu.make_async_copy(source, target, sem)
        copy.start()
        return copy

    def sample_copy(k):
        return pltpu.make_async_copy(
            kspace.at[:, :, lax.rem(y + 3 - k, 4)], samples.at[k], sample_sem.at[k]
        )

    barrier = pltpu.get_barrier_semaphore()
    greeted = column_peers + plane_peers + [across]
    for device in greeted:
        pl.semaphore_signal(barrier, inc=1, device_id=device, device_id_type=MESH)
    loads = [load(mask, ticks, load_sem.at[0]), load(row_table, row, load_sem.at[1])]
    sample_copy(0).start()
    loads += [load(col_table, col, load_sem.at[2]), load(coil_maps, own_maps, load_sem.at[3]), load(order_table, order, load_sem.at[5])]
    for k in (1, 2, 3):
        sample_copy(k).start()
    late_load = load(parity_table, half_row, load_sem.at[4])
    slot_copy = load(coil_maps.at[:, y], maps.at[0, c], slot_sem)
    loads[0].wait()
    weight[0] = ticks[0].astype(F32)
    weight[1] = ticks[1].astype(F32)
    for copy in loads[1:]:
        copy.wait()
    weight[2] = dot(weight[c].astype(BF16), order[...])

    def half(h):
        return pl.ds(pl.multiple_of(h * HALF, 16), HALF)

    def sib_copy(k):
        return remote(part.at[k, 1 - c], from_sib.at[k], sib_send.at[k], sib_recv.at[k], sibling)

    def chunk(r):
        return pl.ds(EDGES[r], EDGES[r + 1] - EDGES[r])

    def y_start(r):
        for k in range(3):
            send(to_y.at[k, :, chunk(r)], from_y.at[k, :, chunk(r)], y_send, y_recv.at[r], at_y(3 - k))

    def first_z(r):
        return remote(
            to_z.at[0, :, chunk(r)], from_z.at[0, :, chunk(r)], z_send.at[0], z_recv.at[r], opposite
        )

    def second_z(h):
        return remote(
            to_z.at[1, :, half(h)], from_z.at[1, :, half(h)], z_send.at[1], z_recv.at[CHUNKS + h], opposite
        )

    def adjoint(k, carry):
        s = lax.rem(y + 3 - k, 4)
        sample_copy(k).wait()
        for t in range(4):
            w = weight[t // 2]
            values = jnp.concatenate(
                [samples[k, t // 2, t % 2, 0] * w, samples[k, t // 2, t % 2, 1] * w], axis=1
            )
            lines_high[t * NZ:(t + 1) * NZ], lines_low[t * NZ:(t + 1) * NZ] = split(values)
        first[...] = rows(lines_high[...], lines_low[...], row)
        for bin_ in range(2):
            sum_re, sum_im = 0.0, 0.0
            for coil in range(2):
                at = pl.ds((bin_ * 2 + coil) * NZ, NZ)
                wave = cols(jnp.concatenate([first[at, :NY], first[at, NY:]], axis=0), col, 1)
                sens_re, sens_im = own_maps[coil, s, 0], own_maps[coil, s, 1]
                sum_re += sens_re * wave[:NZ] + sens_im * wave[NZ:]
                sum_im += sens_re * wave[NZ:] - sens_im * wave[:NZ]
            part[k, bin_, 0] = sum_re
            part[k, bin_, 1] = sum_im
        return carry

    lax.fori_loop(0, 4, adjoint, 0)
    pl.semaphore_wait(barrier, len(greeted))
    for k in range(4):
        sib_copy(k).start()
    quarter = pl.ds(pl.multiple_of(x * (NZ // 4), 8), NZ // 4)
    for step in (1, 2, 3):
        send(coil_maps.at[:, lax.rem(y + step, 4), :, quarter], maps.at[4 - step, c, :, :, quarter],
             map_send, map_recv, at_y(step))
    for k in range(3):
        sib_copy(k).wait_recv()
        to_y[k] = part[k, c] + from_sib[k]
    y_start(0)
    send(own_maps.at[:, y], maps.at[0, c], map_sib_send.at[0], map_sib_recv.at[0], sibling)
    slots = maps.at[pl.ds(1, 3), c, :, :, quarter]
    sib_copy(3).wait_recv()
    part[3, c] = part[3, c] + from_sib[3]
    arrived(slots, map_recv)
    for step in (1, 2, 3):
        send(slots, slots, turn_send, turn_recv, at_xz(step, 0, c))
    y_start(1)
    for r in range(CHUNKS):
        at = chunk(r)
        arrived(from_y.at[:, :, at], y_recv.at[r])
        if r + 2 < CHUNKS:
            y_start(r + 2)
        to_z[0, :, at] = part[3, c, :, at] + from_y[0, :, at] + from_y[1, :, at] + from_y[2, :, at]
        first_z(r).start()
    turned = maps.at[pl.ds(1, 3), c, :, :, pl.ds(0, 3 * (NZ // 4))]
    rest = maps.at[pl.ds(1, 3), c]
    slot_copy.wait()
    late_load.wait()

    def pair(n):
        late = n - 2
        slot = jnp.where(n < 2, 0, 1 + lax.rem(late + 3, 3))
        flip = jnp.where(n < 2, n, jnp.where(late < 3, 0, 1))
        return slot, lax.rem(c + flip, 2)

    def spread(field, n):
        for t in range(4):
            slot, core = pair(2 * n + t // 2)
            sens_re, sens_im = maps[slot, core, t % 2, 0], maps[slot, core, t % 2, 1]
            left, right = by_parity(
                sens_re * field[0] - sens_im * field[1], sens_re * field[1] + sens_im * field[0]
            )
            lines[0, t * NZ:(t + 1) * NZ] = widened(left + right, 1)
            lines[1, t * NZ:(t + 1) * NZ] = widened(left - right, 1)
        for parity in range(2):
            mid[parity, :4 * NZ] = dot(lines[parity], half_row[0, parity])

    def masked(t):
        at = pl.ds(t * NZ, NZ)
        even, odd = mid[0, at], mid[1, at]
        mirror = jnp.concatenate([
            jnp.concatenate([even[:, :NY // 2], odd[:, :NY // 2]], axis=1),
            jnp.concatenate([even[:, NY // 2:], odd[:, NY // 2:]], axis=1),
        ], axis=0)
        w = weight[2]
        return cols(mirror, col, 0) * jnp.concatenate([w, w], axis=0)

    def publish(n):
        plane = fields.at[n, 1 + c, y]
        for step in (1, 2, 3):
            send(plane, plane, along_send.at[n], along_recv.at[n], at_y(step))

    def near_copy(n, which):
        mine = fields.at[n, 1 + c, y]
        target, device = ((mine, sibling), (fields.at[n, 3 - 3 * c, y], across))[which]
        return remote(mine, target, near_send.at[n, which], near_recv.at[n, which], device)

    def normal(n, energy):
        @pl.when(n == 1)
        def _():
            publish(0)
            near_copy(0, 0).start()
            near_copy(0, 1).start()
            arrived(turned, turn_recv)
            send(rest, rest, map_sib_send.at[1], map_sib_recv.at[1], sibling)

        @pl.when(n == 2)
        def _():
            arrived(rest, map_sib_recv.at[1])

        spread(rhs, n)
        for t in range(4):
            values = masked(t)
            energy = energy + fold(values * values)
            wave = cols(values, col, 1)
            at = pl.ds(pl.multiple_of((n * 4 + t) * HALF, 16), HALF)
            for parity, part_ in enumerate(by_parity(wave[:NZ], wave[NZ:])):
                for h in range(2):
                    wide[h, parity, at] = widened(part_[h * HALF:(h + 1) * HALF], 1)
        return energy

    def gather(h, carry):
        for parity in range(2):
            mid[parity] = dot(wide[h, parity], half_row[1, parity])
        at = half(h)

        def one(n, sums_):
            sum_re, sum_im = sums_
            for t in range(4):
                place = pl.ds(pl.multiple_of((n * 4 + t) * HALF, 16), HALF)
                slot, core = pair(2 * n + t // 2)
                sens_re, sens_im = maps[slot, core, t % 2, 0, at], maps[slot, core, t % 2, 1, at]
                even, odd = mid[0, place], mid[1, place]
                plus, minus = even + odd, even - odd
                wave_re = jnp.concatenate([plus[:, :NY // 2], minus[:, :NY // 2]], axis=1)
                wave_im = jnp.concatenate([plus[:, NY // 2:], minus[:, NY // 2:]], axis=1)
                sum_re += sens_re * wave_re + sens_im * wave_im
                sum_im += sens_re * wave_im - sens_im * wave_re
            return sum_re, sum_im

        none = jnp.zeros((HALF, NY), F32)
        to_z[1, 0, at], to_z[1, 1, at] = lax.fori_loop(0, 4, one, (none, none))
        second_z(h).start()
        return carry

    def forward(n, energy):
        spread(resid, n)
        for t in range(4):
            values = masked(t)
            energy = energy + fold(values * values)
        return energy

    def inner(left, right):
        return fold(left[0] * right[0] + left[1] * right[1])

    lane = lax.broadcasted_iota(jnp.int32, (1, 128), 1)

    def share(which, stage, peers, me):
        for peer in peers:
            send(message.at[which, stage], sums.at[which, stage, me],
                 sum_send.at[which, stage], sum_recv.at[which, stage], peer)
        sums[which, stage, me] = message[which, stage]

    def collect(which, stage, peers):
        lines = sums.at[which, stage, pl.ds(0, len(peers))]
        arrived(lines, sum_recv.at[which, stage])
        departed(lines, sum_send.at[which, stage])
        return jnp.sum(sums[which, stage, :len(peers) + 1], axis=0)

    def first_group(which):
        if which == 2:
            return near_peers, lax.rem(ring, 4) * 2 + c
        return column_peers, ring * 2 + c

    def reduce_start(which, parts):
        line = jnp.zeros((1, 128), F32)
        for n, value in enumerate(parts):
            line = jnp.where(lane == n, total(value), line)
        message[which, 0] = line
        share(which, 0, *first_group(which))

    def reduce_end(which, count, early, meanwhile):
        early()
        message[which, 1] = collect(which, 0, first_group(which)[0])
        share(which, 1, plane_peers, y * 4 + x)
        meanwhile()
        line = collect(which, 1, plane_peers)
        return [line[:, n:n + 1] for n in range(count)]

    def extend(n):
        near_copy(n, 1).wait_recv()
        plane = fields.at[n, 3 * c, y]
        for step in (1, 3):
            send(plane, plane, far_send.at[n], far_recv.at[n], at_y(step))

    def pass_on(n):
        arrived(fields.at[n, 1 + c, pl.ds(0, 3)], along_recv.at[n])
        facing = lax.rem(y + 2, 4)
        plane = fields.at[n, 1 + c, facing]
        send(plane, fields.at[n, 3 - 3 * c, facing], pass_send.at[n], pass_recv.at[n], across)
        for slot in (1, 2, 3):
            plane = fields.at[n, 1 + c, lax.rem(y + slot, 4)]
            send(plane, plane, core_send.at[n, 0], core_recv.at[n, 0], sibling)

    def hand_over(n):
        arrived(fields.at[n, 3 * c, pl.ds(0, 2)], far_recv.at[n])
        arrived(fields.at[n, 3 * c, 0], pass_recv.at[n])
        planes = fields.at[n, 3 * c]
        send(planes, planes, core_send.at[n, 1], core_recv.at[n, 1], sibling)

    def settle(n):
        arrived(fields.at[n, 2 - c, pl.ds(0, 3)], core_recv.at[n, 0])
        arrived(fields.at[n, 3 - 3 * c], core_recv.at[n, 1])

    def idle():
        pass

    def first_window():
        near_copy(1, 0).start()
        near_copy(0, 0).wait_recv()
        hand_over(0)

    def second_window():
        extend(1)
        pass_on(1)

    zero = jnp.zeros((8, 128), F32)
    arrived(maps.at[0, c], map_sib_recv.at[0])
    for r in range(CHUNKS):
        at = chunk(r)
        first_z(r).wait_recv()
        rhs[:, at] = to_z[0, :, at] + from_z[0, :, at]
    energy = lax.fori_loop(0, 4, normal, zero)
    reduce_start(0, [0.5 * inner(rhs, rhs), energy])
    lax.fori_loop(0, 2, gather, 0)
    norm_0, energy_0 = reduce_end(0, 2, idle, idle)
    extend(0)
    pass_on(0)
    curve_0 = energy_0 + 0.1 * norm_0
    alpha_0 = norm_0 / curve_0
    for h in range(2):
        at = half(h)
        second_z(h).wait_recv()
        quad[:, at] = to_z[1, :, at] + from_z[1, :, at] + 0.1 * rhs[:, at]
        resid[:, at] = rhs[:, at] - alpha_0 * quad[:, at]
    publish(1)
    near_copy(1, 1).start()
    energy = lax.fori_loop(0, 4, forward, zero)
    reduce_start(1, [0.5 * inner(resid, resid), 0.5 * inner(resid, quad), energy])
    norm_1, cross, energy_1 = reduce_end(1, 3, first_window, second_window)
    beta = norm_1 / norm_0
    curve_1 = energy_1 + 0.1 * norm_1 + 2.0 * beta * cross + beta * beta * curve_0
    alpha_1 = norm_1 / curve_1
    on_rhs = alpha_0 + alpha_1 * beta
    near_copy(1, 0).wait_recv()

    def iterate(place, line):
        return on_rhs * fields[0, place, line] + alpha_1 * fields[1, place, line]

    def length(gap):
        return jnp.sqrt(gap[0] * gap[0] + gap[1] * gap[1])

    gap = jnp.where(2 * b + c < BINS - 1, iterate(2 + c, y) - iterate(1 + c, y), 0.0)
    reduce_start(2, [fold(length(gap))])

    def differences(line, carry):
        values = [iterate(place, line) for place in range(4)]
        result[line, 0] = values[1]
        result[line, 1] = values[2]
        for n, keep in enumerate((b > 0, None, b < BIN_AXIS - 1)):
            gap = values[n + 1] - values[n]
            if keep is not None:
                gap = jnp.where(keep, gap, 0.0)
            gaps[line, n] = gap
            sizes[line, n] = 1.0 / length(gap)
        return carry

    def prepare():
        settle(0)
        settle(1)
        lax.fori_loop(0, SL, differences, 0)

    (size_sum,) = reduce_end(2, 1, lambda: hand_over(1), prepare)
    lam = size_sum / COUNT + 1e-06

    def out_copy(line):
        return pltpu.make_async_copy(result.at[line], out.at[:, line], out_sem.at[line])

    def finish(line, carry):
        dual = [
            gaps[line, n] * jnp.minimum(lam * sizes[line, n], 1.0)[None] for n in range(3)
        ]
        for n in range(2):
            result[line, n] = result[line, n] + 0.25 * (dual[n + 1] - dual[n])
        out_copy(line).start()
        return carry

    lax.fori_loop(0, SL, finish, 0)
    for k in range(4):
        sib_copy(k).wait_send()
    departed(slots, map_send)
    departed(turned, turn_send)
    departed(maps.at[0, c], map_sib_send.at[0])
    departed(rest, map_sib_send.at[1])
    departed(to_y, y_send)
    for n in range(2):
        departed(to_z.at[n], z_send.at[n])
        near_copy(n, 0).wait_send()
        near_copy(n, 1).wait_send()
        departed(fields.at[n, 1 + c, pl.ds(0, 3)], along_send.at[n])
        departed(fields.at[n, 3 * c, pl.ds(0, 2)], far_send.at[n])
        departed(fields.at[n, 1 + c, 0], pass_send.at[n])
        departed(fields.at[n, 1 + c, pl.ds(0, 3)], core_send.at[n, 0])
        departed(fields.at[n, 3 * c], core_send.at[n, 1])
    for line in range(SL):
        out_copy(line).wait()


def on_device(kspace, coil_maps, sample_mask):
    dma = pltpu.SemaphoreType.DMA
    whole = pl.BlockSpec(memory_space=pl.ANY)
    return pl.pallas_call(
        kernel,
        out_shape=jax.ShapeDtypeStruct((2, SL) + PLANE, F32),
        in_specs=[whole] * 7,
        out_specs=whole,
        scratch_shapes=[
            pltpu.VMEM((4, 2, 2) + PLANE, F32),
            pltpu.VMEM((2, SL) + PLANE, F32),
            pltpu.VMEM(PLANE, jnp.int32),
            pltpu.VMEM((2, 2 * NY, 2 * NY), BF16),
            pltpu.VMEM((2, 2 * NZ, 6 * NZ), BF16),
            pltpu.VMEM((2, 2, 3 * NY, NY), BF16),
            pltpu.VMEM((NY, NY), BF16),
            pltpu.VMEM((4, 2, 2) + PLANE, F32),
            pltpu.VMEM((3, NZ, NY), F32),
            pltpu.VMEM((4 * NZ, 2 * NY), BF16),
            pltpu.VMEM((4 * NZ, 2 * NY), BF16),
            pltpu.VMEM((4 * NZ, 2 * NY), F32),
            pltpu.VMEM((2, 4 * NZ, 3 * NY), BF16),
            pltpu.VMEM((2, 2, 16 * HALF, 3 * NY), BF16),
            pltpu.VMEM((2, 16 * HALF, NY), F32),
            pltpu.VMEM((4, 2) + PLANE, F32),
            pltpu.VMEM((4,) + PLANE, F32),
            pltpu.VMEM((3,) + PLANE, F32),
            pltpu.VMEM((3,) + PLANE, F32),
            pltpu.VMEM((2,) + PLANE, F32),
            pltpu.VMEM((2,) + PLANE, F32),
            pltpu.VMEM((2, 4, SL) + PLANE, F32),
            pltpu.VMEM(PLANE, F32),
            pltpu.VMEM((SL, 3) + PLANE, F32),
            pltpu.VMEM((SL, 3, NZ, NY), F32),
            pltpu.VMEM((SL, 2) + PLANE, F32),
            pltpu.VMEM((3, 2, 1, 128), F32),
            pltpu.VMEM((3, 2, 16, 1, 128), F32),
            dma((6,)), dma((4,)), dma(()),
            dma(()), dma(()), dma(()), dma(()), dma((2,)), dma((2,)),
            dma((4,)), dma((4,)), dma(()), dma((CHUNKS,)), dma((2,)), dma((CHUNKS + 2,)),
            dma((2, 2)), dma((2, 2)), dma((2,)), dma((2,)),
            dma((2,)), dma((2,)), dma((2,)), dma((2,)), dma((2, 2)), dma((2, 2)),
            dma((3, 2)), dma((3, 2)), dma((SL,)),
        ],
        compiler_params=pltpu.CompilerParams(
            collective_id=0, has_side_effects=True, vmem_limit_bytes=60 * 1024 * 1024
        ),
        cost_estimate=pl.CostEstimate(flops=20_000_000_000, bytes_accessed=10_000_000, transcendentals=0),
    )(
        kspace, coil_maps, sample_mask, jnp.asarray(row_tables()), jnp.asarray(col_tables()),
        jnp.asarray(parity_tables()), jnp.asarray(parity_order()),
    )


def solution(mesh):
    return jax.shard_map(
        on_device,
        mesh=mesh,
        in_specs=(
            P("bin", "coil", None, None, None, None),
            P("coil", None, None, None, None),
            P("bin", None, None),
        ),
        out_specs=P("bin", None, None, None, None),
        check_vma=False,
    )
```

```python
import math

import jax
import jax.numpy as jnp
import numpy as np
from jax import lax
from jax.experimental import pallas as pl
from jax.experimental.pallas import tpu as pltpu
from jax.sharding import PartitionSpec as P

MESH = pl.DeviceIdType.MESH
F32 = jnp.float32
BF16 = jnp.bfloat16
NZ, NY, SL = 96, 256, 4
BIN_AXIS, COIL_AXIS = 16, 16
BINS = 32
COUNT = (BINS - 1) * SL * NZ * NY
PLANE = (2, NZ, NY)
HALF = NZ // 2
EDGES = (0, 32, 64, 96)
CHUNKS = len(EDGES) - 1
RING_HOPS = (0, 1, 2, 1)


def dft_tables(length):
    index = np.arange(length)
    angle = (index[:, None] * index[None, :] % length) * (2.0 * math.pi / length)
    factor = 1.0 / math.sqrt(length)
    return np.cos(angle) * factor, np.sin(angle) * factor


def halves(table):
    high = table.astype(np.float32).astype(jnp.bfloat16)
    low = (table - high.astype(np.float64)).astype(np.float32).astype(jnp.bfloat16)
    return np.stack([high, low])


def row_tables():
    cos, sin = dft_tables(NY)
    return halves(np.block([[cos, sin], [-sin, cos]]))


def stacked(table, axis):
    high, low = halves(table)
    return np.concatenate([high, high, low], axis=axis)


def parity_tables():
    cos, sin = dft_tables(NY)
    tables = []
    for parity in range(2):
        part = (slice(0, NY // 2), slice(parity, None, 2))
        tables.append(np.block([[cos[part], -sin[part]], [sin[part], cos[part]]]))
    return np.stack([
        np.stack([stacked(table, 0) for table in tables]),
        np.stack([stacked(table.T, 0) for table in tables]),
    ])


def col_tables():
    cos, sin = dft_tables(NZ)
    forward = np.block([[cos, sin], [-sin, cos]])
    return np.stack([stacked(forward, 1), stacked(forward.T, 1)])


def parity_order():
    order = np.concatenate([np.arange(0, NY, 2), np.arange(1, NY, 2)])
    return np.eye(NY)[:, order].astype(jnp.bfloat16)


def split(values):
    high = values.astype(BF16)
    return high, (values - high.astype(F32)).astype(BF16)


def widened(values, axis):
    high, low = split(values)
    return jnp.concatenate([high, low, high], axis=axis)


def dot(left, right):
    return jnp.dot(left, right, preferred_element_type=F32)


def rows(high, low, table):
    return dot(high, table[0]) + dot(low, table[0]) + dot(high, table[1])


def cols(values, table, which):
    return dot(table[which], widened(values, 0))


def by_parity(real, imag):
    return [
        jnp.concatenate([real[:, part], imag[:, part]], axis=1)
        for part in (slice(0, NY // 2), slice(NY // 2, NY))
    ]


def fold(values):
    part = jnp.sum(values.reshape(values.shape[0] // 8, 8, NY), axis=0)
    return part[:, :128] + part[:, 128:]


def total(values):
    return jnp.sum(values, keepdims=True)


def kernel(
    kspace, coil_maps, mask, row_table, col_table, parity_table, order_table, out,
    samples, own_maps, ticks, row, col, half_row, order, maps, weight, lines_high, lines_low, first, lines, wide, mid,
    part, from_sib, to_y, from_y, to_z, from_z,
    fields, quad, gaps, sizes, result, message, sums,
    load_sem, sample_sem, slot_sem,
    map_send, map_recv, turn_send, turn_recv, map_sib_send, map_sib_recv,
    sib_send, sib_recv, y_send, y_recv, z_send, z_recv,
    near_send, near_recv, along_send, along_recv, pass_send, pass_recv, far_send, far_recv, core_send, core_recv,
    sum_send, sum_recv, out_sem,
):
    b = lax.axis_index("bin")
    j = lax.axis_index("coil")
    y, z, c = j // 4, (j // 2) % 2, j % 2
    x = lax.rem(b, 4)
    ring = z * 4 + b // 4

    def at_y(step):
        return (b, lax.rem(y + step, 4) * 4 + z * 2 + c)

    def at_xz(step_x, step_z, core):
        place = lax.rem(ring + step_z + 8, 8)
        return (
            lax.rem(place, 4) * 4 + lax.rem(x + step_x + 4, 4),
            y * 4 + place // 4 * 2 + core,
        )

    rhs = fields.at[0, 1 + c, y]
    resid = fields.at[1, 1 + c, y]
    sibling = (b, j + 1 - 2 * c)
    opposite = (b, j + 2 - 4 * z)
    wraps = jnp.where(c == 1, jnp.where(x == 3, 1, 0), jnp.where(x == 0, -1, 0))
    across = at_xz(2 * c - 1, wraps, 1 - c)
    column_peers = [
        at_xz(0, dz, core) for dz in (4, 3, 5, 2, 6, 1, 7, 0) for core in (1 - c, c)
    ][:-1]
    near_peers = [at_xz(0, dz, core) for dz in (2, 1, -1, 0) for core in (1 - c, c)][:-1]
    turns = sorted(range(1, 16), key=lambda step: -RING_HOPS[step % 4] - RING_HOPS[step // 4])
    plane_peers = [
        (b - x + lax.rem(x + step % 4, 4), lax.rem(y + step // 4, 4) * 4 + z * 2 + c) for step in turns
    ]

    def remote(source, target, send_sem, recv_sem, device):
        return pltpu.make_async_remote_copy(
            src_ref=source, dst_ref=target, send_sem=send_sem, recv_sem=recv_sem,
            device_id=device, device_id_type=MESH,
        )

    def send(*args):
        copy = remote(*args)
        copy.start()
        return copy

    def arrived(ref, sem):
        remote(ref, ref, sem, sem, sibling).wait_recv()

    def departed(ref, sem):
        remote(ref, ref, sem, sem, sibling).wait_send()

    def load(source, target, sem):
        copy = pltpu.make_async_copy(source, target, sem)
        copy.start()
        return copy

    def sample_copy(k):
        return pltpu.make_async_copy(
            kspace.at[:, :, lax.rem(y + 3 - k, 4)], samples.at[k], sample_sem.at[k]
        )

    barrier = pltpu.get_barrier_semaphore()
    greeted = column_peers + plane_peers + [across]
    for device in greeted:
        pl.semaphore_signal(barrier, inc=1, device_id=device, device_id_type=MESH)
    loads = [load(mask, ticks, load_sem.at[0]), load(row_table, row, load_sem.at[1])]
    sample_copy(0).start()
    loads += [load(col_table, col, load_sem.at[2]), load(coil_maps, own_maps, load_sem.at[3]), load(order_table, order, load_sem.at[5])]
    for k in (1, 2, 3):
        sample_copy(k).start()
    late_load = load(parity_table, half_row, load_sem.at[4])
    slot_copy = load(coil_maps.at[:, y], maps.at[0, c], slot_sem)
    loads[0].wait()
    weight[0] = ticks[0].astype(F32)
    weight[1] = ticks[1].astype(F32)
    for copy in loads[1:]:
        copy.wait()
    weight[2] = dot(weight[c].astype(BF16), order[...])

    def half(h):
        return pl.ds(pl.multiple_of(h * HALF, 16), HALF)

    def sib_copy(k):
        return remote(part.at[k, 1 - c], from_sib.at[k], sib_send.at[k], sib_recv.at[k], sibling)

    def chunk(r):
        return pl.ds(EDGES[r], EDGES[r + 1] - EDGES[r])

    def y_start(r):
        for k in range(3):
            send(to_y.at[k, :, chunk(r)], from_y.at[k, :, chunk(r)], y_send, y_recv.at[r], at_y(3 - k))

    def first_z(r):
        return remote(
            to_z.at[0, :, chunk(r)], from_z.at[0, :, chunk(r)], z_send.at[0], z_recv.at[r], opposite
        )

    def second_z(h):
        return remote(
            to_z.at[1, :, half(h)], from_z.at[1, :, half(h)], z_send.at[1], z_recv.at[CHUNKS + h], opposite
        )

    def adjoint(k, carry):
        s = lax.rem(y + 3 - k, 4)
        sample_copy(k).wait()
        for t in range(4):
            w = weight[t // 2]
            values = jnp.concatenate(
                [samples[k, t // 2, t % 2, 0] * w, samples[k, t // 2, t % 2, 1] * w], axis=1
            )
            lines_high[t * NZ:(t + 1) * NZ], lines_low[t * NZ:(t + 1) * NZ] = split(values)
        first[...] = rows(lines_high[...], lines_low[...], row)
        for bin_ in range(2):
            sum_re, sum_im = 0.0, 0.0
            for coil in range(2):
                at = pl.ds((bin_ * 2 + coil) * NZ, NZ)
                wave = cols(jnp.concatenate([first[at, :NY], first[at, NY:]], axis=0), col, 1)
                sens_re, sens_im = own_maps[coil, s, 0], own_maps[coil, s, 1]
                sum_re += sens_re * wave[:NZ] + sens_im * wave[NZ:]
                sum_im += sens_re * wave[NZ:] - sens_im * wave[:NZ]
            part[k, bin_, 0] = sum_re
            part[k, bin_, 1] = sum_im
        return carry

    lax.fori_loop(0, 4, adjoint, 0)
    pl.semaphore_wait(barrier, len(greeted))
    for k in range(4):
        sib_copy(k).start()
    quarter = pl.ds(pl.multiple_of(x * (NZ // 4), 8), NZ // 4)
    for step in (1, 2, 3):
        send(coil_maps.at[:, lax.rem(y + step, 4), :, quarter], maps.at[4 - step, c, :, :, quarter],
             map_send, map_recv, at_y(step))
    for k in range(3):
        sib_copy(k).wait_recv()
        to_y[k] = part[k, c] + from_sib[k]
    y_start(0)
    send(own_maps.at[:, y], maps.at[0, c], map_sib_send.at[0], map_sib_recv.at[0], sibling)
    slots = maps.at[pl.ds(1, 3), c, :, :, quarter]
    sib_copy(3).wait_recv()
    part[3, c] = part[3, c] + from_sib[3]
    arrived(slots, map_recv)
    for step in (1, 2, 3):
        send(slots, slots, turn_send, turn_recv, at_xz(step, 0, c))
    y_start(1)
    for r in range(CHUNKS):
        at = chunk(r)
        arrived(from_y.at[:, :, at], y_recv.at[r])
        if r + 2 < CHUNKS:
            y_start(r + 2)
        to_z[0, :, at] = part[3, c, :, at] + from_y[0, :, at] + from_y[1, :, at] + from_y[2, :, at]
        first_z(r).start()
    turned = maps.at[pl.ds(1, 3), c, :, :, pl.ds(0, 3 * (NZ // 4))]
    rest = maps.at[pl.ds(1, 3), c]
    slot_copy.wait()
    late_load.wait()

    def pair(n):
        late = n - 2
        slot = jnp.where(n < 2, 0, 1 + lax.rem(late + 3, 3))
        flip = jnp.where(n < 2, n, jnp.where(late < 3, 0, 1))
        return slot, lax.rem(c + flip, 2)

    def spread(field, n):
        for t in range(4):
            slot, core = pair(2 * n + t // 2)
            sens_re, sens_im = maps[slot, core, t % 2, 0], maps[slot, core, t % 2, 1]
            left, right = by_parity(
                sens_re * field[0] - sens_im * field[1], sens_re * field[1] + sens_im * field[0]
            )
            lines[0, t * NZ:(t + 1) * NZ] = widened(left + right, 1)
            lines[1, t * NZ:(t + 1) * NZ] = widened(left - right, 1)
        for parity in range(2):
            mid[parity, :4 * NZ] = dot(lines[parity], half_row[0, parity])

    def masked(t):
        at = pl.ds(t * NZ, NZ)
        even, odd = mid[0, at], mid[1, at]
        mirror = jnp.concatenate([
            jnp.concatenate([even[:, :NY // 2], odd[:, :NY // 2]], axis=1),
            jnp.concatenate([even[:, NY // 2:], odd[:, NY // 2:]], axis=1),
        ], axis=0)
        w = weight[2]
        return cols(mirror, col, 0) * jnp.concatenate([w, w], axis=0)

    def publish(n):
        plane = fields.at[n, 1 + c, y]
        for step in (1, 2, 3):
            send(plane, plane, along_send.at[n], along_recv.at[n], at_y(step))

    def near_copy(n, which):
        mine = fields.at[n, 1 + c, y]
        target, device = ((mine, sibling), (fields.at[n, 3 - 3 * c, y], across))[which]
        return remote(mine, target, near_send.at[n, which], near_recv.at[n, which], device)

    def normal(n, energy):
        @pl.when(n == 1)
        def _():
            publish(0)
            near_copy(0, 0).start()
            near_copy(0, 1).start()
            arrived(turned, turn_recv)
            send(rest, rest, map_sib_send.at[1], map_sib_recv.at[1], sibling)

        @pl.when(n == 2)
        def _():
            arrived(rest, map_sib_recv.at[1])

        spread(rhs, n)
        for t in range(4):
            values = masked(t)
            energy = energy + fold(values * values)
            wave = cols(values, col, 1)
            at = pl.ds(pl.multiple_of((n * 4 + t) * HALF, 16), HALF)
            for parity, part_ in enumerate(by_parity(wave[:NZ], wave[NZ:])):
                for h in range(2):
                    wide[h, parity, at] = widened(part_[h * HALF:(h + 1) * HALF], 1)
        return energy

    def gather(h, carry):
        for parity in range(2):
            mid[parity] = dot(wide[h, parity], half_row[1, parity])
        at = half(h)

        def one(n, sums_):
            sum_re, sum_im = sums_
            for t in range(4):
                place = pl.ds(pl.multiple_of((n * 4 + t) * HALF, 16), HALF)
                slot, core = pair(2 * n + t // 2)
                sens_re, sens_im = maps[slot, core, t % 2, 0, at], maps[slot, core, t % 2, 1, at]
                even, odd = mid[0, place], mid[1, place]
                plus, minus = even + odd, even - odd
                wave_re = jnp.concatenate([plus[:, :NY // 2], minus[:, :NY // 2]], axis=1)
                wave_im = jnp.concatenate([plus[:, NY // 2:], minus[:, NY // 2:]], axis=1)
                sum_re += sens_re * wave_re + sens_im * wave_im
                sum_im += sens_re * wave_im - sens_im * wave_re
            return sum_re, sum_im

        none = jnp.zeros((HALF, NY), F32)
        to_z[1, 0, at], to_z[1, 1, at] = lax.fori_loop(0, 4, one, (none, none))
        second_z(h).start()
        return carry

    def forward(n, energy):
        spread(resid, n)
        for t in range(4):
            values = masked(t)
            energy = energy + fold(values * values)
        return energy

    def inner(left, right):
        return fold(left[0] * right[0] + left[1] * right[1])

    lane = lax.broadcasted_iota(jnp.int32, (1, 128), 1)

    def share(which, stage, peers, me):
        for peer in peers:
            send(message.at[which, stage], sums.at[which, stage, me],
                 sum_send.at[which, stage], sum_recv.at[which, stage], peer)
        sums[which, stage, me] = message[which, stage]

    def collect(which, stage, peers):
        lines = sums.at[which, stage, pl.ds(0, len(peers))]
        arrived(lines, sum_recv.at[which, stage])
        departed(lines, sum_send.at[which, stage])
        return jnp.sum(sums[which, stage, :len(peers) + 1], axis=0)

    def first_group(which):
        if which == 2:
            return near_peers, lax.rem(ring, 4) * 2 + c
        return column_peers, ring * 2 + c

    def reduce_start(which, parts):
        line = jnp.zeros((1, 128), F32)
        for n, value in enumerate(parts):
            line = jnp.where(lane == n, total(value), line)
        message[which, 0] = line
        share(which, 0, *first_group(which))

    def reduce_end(which, count, early, meanwhile):
        early()
        message[which, 1] = collect(which, 0, first_group(which)[0])
        share(which, 1, plane_peers, y * 4 + x)
        meanwhile()
        line = collect(which, 1, plane_peers)
        return [line[:, n:n + 1] for n in range(count)]

    def extend(n):
        near_copy(n, 1).wait_recv()
        plane = fields.at[n, 3 * c, y]
        for step in (1, 3):
            send(plane, plane, far_send.at[n], far_recv.at[n], at_y(step))

    def pass_on(n):
        arrived(fields.at[n, 1 + c, pl.ds(0, 3)], along_recv.at[n])
        facing = lax.rem(y + 2, 4)
        plane = fields.at[n, 1 + c, facing]
        send(plane, fields.at[n, 3 - 3 * c, facing], pass_send.at[n], pass_recv.at[n], across)
        for slot in (1, 2, 3):
            plane = fields.at[n, 1 + c, lax.rem(y + slot, 4)]
            send(plane, plane, core_send.at[n, 0], core_recv.at[n, 0], sibling)

    def hand_over(n):
        arrived(fields.at[n, 3 * c, pl.ds(0, 2)], far_recv.at[n])
        arrived(fields.at[n, 3 * c, 0], pass_recv.at[n])
        planes = fields.at[n, 3 * c]
        send(planes, planes, core_send.at[n, 1], core_recv.at[n, 1], sibling)

    def settle(n):
        arrived(fields.at[n, 2 - c, pl.ds(0, 3)], core_recv.at[n, 0])
        arrived(fields.at[n, 3 - 3 * c], core_recv.at[n, 1])

    def idle():
        pass

    def first_window():
        near_copy(1, 0).start()
        near_copy(0, 0).wait_recv()
        hand_over(0)

    def second_window():
        extend(1)
        pass_on(1)

    zero = jnp.zeros((8, 128), F32)
    arrived(maps.at[0, c], map_sib_recv.at[0])
    for r in range(CHUNKS):
        at = chunk(r)
        first_z(r).wait_recv()
        rhs[:, at] = to_z[0, :, at] + from_z[0, :, at]
    energy = lax.fori_loop(0, 4, normal, zero)
    lax.fori_loop(0, 2, gather, 0)
    reduce_start(0, [0.5 * inner(rhs, rhs), energy])
    norm_0, energy_0 = reduce_end(0, 2, idle, idle)
    extend(0)
    pass_on(0)
    curve_0 = energy_0 + 0.1 * norm_0
    alpha_0 = norm_0 / curve_0
    for h in range(2):
        at = half(h)
        second_z(h).wait_recv()
        quad[:, at] = to_z[1, :, at] + from_z[1, :, at] + 0.1 * rhs[:, at]
        resid[:, at] = rhs[:, at] - alpha_0 * quad[:, at]
    publish(1)
    near_copy(1, 1).start()
    energy = lax.fori_loop(0, 4, forward, zero)
    reduce_start(1, [0.5 * inner(resid, resid), 0.5 * inner(resid, quad), energy])
    norm_1, cross, energy_1 = reduce_end(1, 3, first_window, second_window)
    beta = norm_1 / norm_0
    curve_1 = energy_1 + 0.1 * norm_1 + 2.0 * beta * cross + beta * beta * curve_0
    alpha_1 = norm_1 / curve_1
    on_rhs = alpha_0 + alpha_1 * beta
    near_copy(1, 0).wait_recv()

    def iterate(place, line):
        return on_rhs * fields[0, place, line] + alpha_1 * fields[1, place, line]

    def length(gap):
        return jnp.sqrt(gap[0] * gap[0] + gap[1] * gap[1])

    gap = jnp.where(2 * b + c < BINS - 1, iterate(2 + c, y) - iterate(1 + c, y), 0.0)
    reduce_start(2, [fold(length(gap))])

    def differences(line, carry):
        values = [iterate(place, line) for place in range(4)]
        result[line, 0] = values[1]
        result[line, 1] = values[2]
        for n, keep in enumerate((b > 0, None, b < BIN_AXIS - 1)):
            gap = values[n + 1] - values[n]
            if keep is not None:
                gap = jnp.where(keep, gap, 0.0)
            gaps[line, n] = gap
            sizes[line, n] = 1.0 / length(gap)
        return carry

    def prepare():
        settle(0)
        settle(1)
        lax.fori_loop(0, SL, differences, 0)

    (size_sum,) = reduce_end(2, 1, lambda: hand_over(1), prepare)
    lam = size_sum / COUNT + 1e-06

    def out_copy(line):
        return pltpu.make_async_copy(result.at[line], out.at[:, line], out_sem.at[line])

    def finish(line, carry):
        dual = [
            gaps[line, n] * jnp.minimum(lam * sizes[line, n], 1.0)[None] for n in range(3)
        ]
        for n in range(2):
            result[line, n] = result[line, n] + 0.25 * (dual[n + 1] - dual[n])
        out_copy(line).start()
        return carry

    lax.fori_loop(0, SL, finish, 0)
    for k in range(4):
        sib_copy(k).wait_send()
    departed(slots, map_send)
    departed(turned, turn_send)
    departed(maps.at[0, c], map_sib_send.at[0])
    departed(rest, map_sib_send.at[1])
    departed(to_y, y_send)
    for n in range(2):
        departed(to_z.at[n], z_send.at[n])
        near_copy(n, 0).wait_send()
        near_copy(n, 1).wait_send()
        departed(fields.at[n, 1 + c, pl.ds(0, 3)], along_send.at[n])
        departed(fields.at[n, 3 * c, pl.ds(0, 2)], far_send.at[n])
        departed(fields.at[n, 1 + c, 0], pass_send.at[n])
        departed(fields.at[n, 1 + c, pl.ds(0, 3)], core_send.at[n, 0])
        departed(fields.at[n, 3 * c], core_send.at[n, 1])
    for line in range(SL):
        out_copy(line).wait()


def on_device(kspace, coil_maps, sample_mask):
    dma = pltpu.SemaphoreType.DMA
    whole = pl.BlockSpec(memory_space=pl.ANY)
    return pl.pallas_call(
        kernel,
        out_shape=jax.ShapeDtypeStruct((2, SL) + PLANE, F32),
        in_specs=[whole] * 7,
        out_specs=whole,
        scratch_shapes=[
            pltpu.VMEM((4, 2, 2) + PLANE, F32),
            pltpu.VMEM((2, SL) + PLANE, F32),
            pltpu.VMEM(PLANE, jnp.int32),
            pltpu.VMEM((2, 2 * NY, 2 * NY), BF16),
            pltpu.VMEM((2, 2 * NZ, 6 * NZ), BF16),
            pltpu.VMEM((2, 2, 3 * NY, NY), BF16),
            pltpu.VMEM((NY, NY), BF16),
            pltpu.VMEM((4, 2, 2) + PLANE, F32),
            pltpu.VMEM((3, NZ, NY), F32),
            pltpu.VMEM((4 * NZ, 2 * NY), BF16),
            pltpu.VMEM((4 * NZ, 2 * NY), BF16),
            pltpu.VMEM((4 * NZ, 2 * NY), F32),
            pltpu.VMEM((2, 4 * NZ, 3 * NY), BF16),
            pltpu.VMEM((2, 2, 16 * HALF, 3 * NY), BF16),
            pltpu.VMEM((2, 16 * HALF, NY), F32),
            pltpu.VMEM((4, 2) + PLANE, F32),
            pltpu.VMEM((4,) + PLANE, F32),
            pltpu.VMEM((3,) + PLANE, F32),
            pltpu.VMEM((3,) + PLANE, F32),
            pltpu.VMEM((2,) + PLANE, F32),
            pltpu.VMEM((2,) + PLANE, F32),
            pltpu.VMEM((2, 4, SL) + PLANE, F32),
            pltpu.VMEM(PLANE, F32),
            pltpu.VMEM((SL, 3) + PLANE, F32),
            pltpu.VMEM((SL, 3, NZ, NY), F32),
            pltpu.VMEM((SL, 2) + PLANE, F32),
            pltpu.VMEM((3, 2, 1, 128), F32),
            pltpu.VMEM((3, 2, 16, 1, 128), F32),
            dma((6,)), dma((4,)), dma(()),
            dma(()), dma(()), dma(()), dma(()), dma((2,)), dma((2,)),
            dma((4,)), dma((4,)), dma(()), dma((CHUNKS,)), dma((2,)), dma((CHUNKS + 2,)),
            dma((2, 2)), dma((2, 2)), dma((2,)), dma((2,)),
            dma((2,)), dma((2,)), dma((2,)), dma((2,)), dma((2, 2)), dma((2, 2)),
            dma((3, 2)), dma((3, 2)), dma((SL,)),
        ],
        compiler_params=pltpu.CompilerParams(
            collective_id=0, has_side_effects=True, vmem_limit_bytes=60 * 1024 * 1024
        ),
        cost_estimate=pl.CostEstimate(flops=20_000_000_000, bytes_accessed=10_000_000, transcendentals=0),
    )(
        kspace, coil_maps, sample_mask, jnp.asarray(row_tables()), jnp.asarray(col_tables()),
        jnp.asarray(parity_tables()), jnp.asarray(parity_order()),
    )


def solution(mesh):
    return jax.shard_map(
        on_device,
        mesh=mesh,
        in_specs=(
            P("bin", "coil", None, None, None, None),
            P("coil", None, None, None, None),
            P("bin", None, None),
        ),
        out_specs=P("bin", None, None, None, None),
        check_vma=False,
    )
```

```python
import math

import jax
import jax.numpy as jnp
import numpy as np
from jax import lax
from jax.experimental import pallas as pl
from jax.experimental.pallas import tpu as pltpu
from jax.sharding import PartitionSpec as P

MESH = pl.DeviceIdType.MESH
F32 = jnp.float32
BF16 = jnp.bfloat16
NZ, NY, SL = 96, 256, 4
BIN_AXIS, COIL_AXIS = 16, 16
BINS = 32
COUNT = (BINS - 1) * SL * NZ * NY
PLANE = (2, NZ, NY)
HALF = NZ // 2
EDGES = (0, 32, 64, 96)
CHUNKS = len(EDGES) - 1
RING_HOPS = (0, 1, 2, 1)


def dft_tables(length):
    index = np.arange(length)
    angle = (index[:, None] * index[None, :] % length) * (2.0 * math.pi / length)
    factor = 1.0 / math.sqrt(length)
    return np.cos(angle) * factor, np.sin(angle) * factor


def halves(table):
    high = table.astype(np.float32).astype(jnp.bfloat16)
    low = (table - high.astype(np.float64)).astype(np.float32).astype(jnp.bfloat16)
    return np.stack([high, low])


def row_tables():
    cos, sin = dft_tables(NY)
    return halves(np.block([[cos, sin], [-sin, cos]]))


def stacked(table, axis):
    high, low = halves(table)
    return np.concatenate([high, high, low], axis=axis)


def parity_tables():
    cos, sin = dft_tables(NY)
    tables = []
    for parity in range(2):
        part = (slice(0, NY // 2), slice(parity, None, 2))
        tables.append(np.block([[cos[part], -sin[part]], [sin[part], cos[part]]]))
    return np.stack([
        np.stack([stacked(table, 0) for table in tables]),
        np.stack([stacked(table.T, 0) for table in tables]),
    ])


def col_tables():
    cos, sin = dft_tables(NZ)
    forward = np.block([[cos, sin], [-sin, cos]])
    return np.stack([stacked(forward, 1), stacked(forward.T, 1)])


def parity_order():
    order = np.concatenate([np.arange(0, NY, 2), np.arange(1, NY, 2)])
    return np.eye(NY)[:, order].astype(jnp.bfloat16)


def split(values):
    high = values.astype(BF16)
    return high, (values - high.astype(F32)).astype(BF16)


def widened(values, axis):
    high, low = split(values)
    return jnp.concatenate([high, low, high], axis=axis)


def dot(left, right):
    return jnp.dot(left, right, preferred_element_type=F32)


def rows(high, low, table):
    return dot(high, table[0]) + dot(low, table[0]) + dot(high, table[1])


def cols(values, table, which):
    return dot(table[which], widened(values, 0))


def by_parity(real, imag):
    return [
        jnp.concatenate([real[:, part], imag[:, part]], axis=1)
        for part in (slice(0, NY // 2), slice(NY // 2, NY))
    ]


def fold(values):
    part = jnp.sum(values.reshape(values.shape[0] // 8, 8, NY), axis=0)
    return part[:, :128] + part[:, 128:]


def total(values):
    return jnp.sum(values, keepdims=True)


def kernel(
    kspace, coil_maps, mask, row_table, col_table, parity_table, order_table, out,
    samples, own_maps, ticks, row, col, half_row, order, maps, weight, lines_high, lines_low, first, lines, wide, mid,
    part, from_sib, to_y, from_y, to_z, from_z,
    fields, quad, gaps, sizes, result, message, sums,
    load_sem, sample_sem, slot_sem,
    map_send, map_recv, turn_send, turn_recv, map_sib_send, map_sib_recv,
    sib_send, sib_recv, y_send, y_recv, z_send, z_recv,
    near_send, near_recv, along_send, along_recv, pass_send, pass_recv, far_send, far_recv, core_send, core_recv,
    sum_send, sum_recv, out_sem,
):
    b = lax.axis_index("bin")
    j = lax.axis_index("coil")
    y, z, c = j // 4, (j // 2) % 2, j % 2
    x = lax.rem(b, 4)
    ring = z * 4 + b // 4

    def at_y(step):
        return (b, lax.rem(y + step, 4) * 4 + z * 2 + c)

    def at_xz(step_x, step_z, core):
        place = lax.rem(ring + step_z + 8, 8)
        return (
            lax.rem(place, 4) * 4 + lax.rem(x + step_x + 4, 4),
            y * 4 + place // 4 * 2 + core,
        )

    rhs = fields.at[0, 1 + c, y]
    resid = fields.at[1, 1 + c, y]
    sibling = (b, j + 1 - 2 * c)
    opposite = (b, j + 2 - 4 * z)
    wraps = jnp.where(c == 1, jnp.where(x == 3, 1, 0), jnp.where(x == 0, -1, 0))
    across = at_xz(2 * c - 1, wraps, 1 - c)
    column_peers = [
        at_xz(0, dz, core) for dz in (4, 3, 5, 2, 6, 1, 7, 0) for core in (1 - c, c)
    ][:-1]
    near_peers = [at_xz(0, dz, core) for dz in (2, 1, -1, 0) for core in (1 - c, c)][:-1]
    turns = sorted(range(1, 16), key=lambda step: -RING_HOPS[step % 4] - RING_HOPS[step // 4])
    plane_peers = [
        (b - x + lax.rem(x + step % 4, 4), lax.rem(y + step // 4, 4) * 4 + z * 2 + c) for step in turns
    ]

    def remote(source, target, send_sem, recv_sem, device):
        return pltpu.make_async_remote_copy(
            src_ref=source, dst_ref=target, send_sem=send_sem, recv_sem=recv_sem,
            device_id=device, device_id_type=MESH,
        )

    def send(*args):
        copy = remote(*args)
        copy.start()
        return copy

    def arrived(ref, sem):
        remote(ref, ref, sem, sem, sibling).wait_recv()

    def departed(ref, sem):
        remote(ref, ref, sem, sem, sibling).wait_send()

    def load(source, target, sem):
        copy = pltpu.make_async_copy(source, target, sem)
        copy.start()
        return copy

    def sample_copy(k):
        return pltpu.make_async_copy(
            kspace.at[:, :, lax.rem(y + 3 - k, 4)], samples.at[k], sample_sem.at[k]
        )

    barrier = pltpu.get_barrier_semaphore()
    greeted = column_peers + plane_peers + [across]
    for device in greeted:
        pl.semaphore_signal(barrier, inc=1, device_id=device, device_id_type=MESH)
    loads = [load(mask, ticks, load_sem.at[0]), load(row_table, row, load_sem.at[1])]
    sample_copy(0).start()
    loads += [load(col_table, col, load_sem.at[2]), load(coil_maps, own_maps, load_sem.at[3]), load(order_table, order, load_sem.at[5])]
    for k in (1, 2, 3):
        sample_copy(k).start()
    late_load = load(parity_table, half_row, load_sem.at[4])
    slot_copy = load(coil_maps.at[:, y], maps.at[0, c], slot_sem)
    loads[0].wait()
    weight[0] = ticks[0].astype(F32)
    weight[1] = ticks[1].astype(F32)
    for copy in loads[1:]:
        copy.wait()
    weight[2] = dot(weight[c].astype(BF16), order[...])

    def half(h):
        return pl.ds(pl.multiple_of(h * HALF, 16), HALF)

    def sib_copy(k):
        return remote(part.at[k, 1 - c], from_sib.at[k], sib_send.at[k], sib_recv.at[k], sibling)

    def chunk(r):
        return pl.ds(EDGES[r], EDGES[r + 1] - EDGES[r])

    def y_start(r):
        for k in range(3):
            send(to_y.at[k, :, chunk(r)], from_y.at[k, :, chunk(r)], y_send, y_recv.at[r], at_y(3 - k))

    def first_z(r):
        return remote(
            to_z.at[0, :, chunk(r)], from_z.at[0, :, chunk(r)], z_send.at[0], z_recv.at[r], opposite
        )

    def second_z(h):
        return remote(
            to_z.at[1, :, half(h)], from_z.at[1, :, half(h)], z_send.at[1], z_recv.at[CHUNKS + h], opposite
        )

    def adjoint(k, carry):
        s = lax.rem(y + 3 - k, 4)
        sample_copy(k).wait()
        for t in range(4):
            w = weight[t // 2]
            values = jnp.concatenate(
                [samples[k, t // 2, t % 2, 0] * w, samples[k, t // 2, t % 2, 1] * w], axis=1
            )
            lines_high[t * NZ:(t + 1) * NZ], lines_low[t * NZ:(t + 1) * NZ] = split(values)
        first[...] = rows(lines_high[...], lines_low[...], row)
        for bin_ in range(2):
            sum_re, sum_im = 0.0, 0.0
            for coil in range(2):
                at = pl.ds((bin_ * 2 + coil) * NZ, NZ)
                wave = cols(jnp.concatenate([first[at, :NY], first[at, NY:]], axis=0), col, 1)
                sens_re, sens_im = own_maps[coil, s, 0], own_maps[coil, s, 1]
                sum_re += sens_re * wave[:NZ] + sens_im * wave[NZ:]
                sum_im += sens_re * wave[NZ:] - sens_im * wave[:NZ]
            part[k, bin_, 0] = sum_re
            part[k, bin_, 1] = sum_im
        return carry

    lax.fori_loop(0, 4, adjoint, 0)
    pl.semaphore_wait(barrier, len(greeted))
    for k in range(4):
        sib_copy(k).start()
    quarter = pl.ds(pl.multiple_of(x * (NZ // 4), 8), NZ // 4)
    for step in (1, 2, 3):
        send(coil_maps.at[:, lax.rem(y + step, 4), :, quarter], maps.at[4 - step, c, :, :, quarter],
             map_send, map_recv, at_y(step))
    for k in range(3):
        sib_copy(k).wait_recv()
        to_y[k] = part[k, c] + from_sib[k]
    y_start(0)
    send(own_maps.at[:, y], maps.at[0, c], map_sib_send.at[0], map_sib_recv.at[0], sibling)
    slots = maps.at[pl.ds(1, 3), c, :, :, quarter]
    sib_copy(3).wait_recv()
    part[3, c] = part[3, c] + from_sib[3]
    arrived(slots, map_recv)
    for step in (1, 2, 3):
        send(slots, slots, turn_send, turn_recv, at_xz(step, 0, c))
    y_start(1)
    for r in range(CHUNKS):
        at = chunk(r)
        arrived(from_y.at[:, :, at], y_recv.at[r])
        if r + 2 < CHUNKS:
            y_start(r + 2)
        to_z[0, :, at] = part[3, c, :, at] + from_y[0, :, at] + from_y[1, :, at] + from_y[2, :, at]
        first_z(r).start()
    turned = maps.at[pl.ds(1, 3), c, :, :, pl.ds(0, 3 * (NZ // 4))]
    rest = maps.at[pl.ds(1, 3), c]
    slot_copy.wait()
    late_load.wait()

    def pair(n):
        late = n - 2
        slot = jnp.where(n < 2, 0, 1 + lax.rem(late + 3, 3))
        flip = jnp.where(n < 2, n, jnp.where(late < 3, 0, 1))
        return slot, lax.rem(c + flip, 2)

    def spread(field, n):
        for t in range(4):
            slot, core = pair(2 * n + t // 2)
            sens_re, sens_im = maps[slot, core, t % 2, 0], maps[slot, core, t % 2, 1]
            left, right = by_parity(
                sens_re * field[0] - sens_im * field[1], sens_re * field[1] + sens_im * field[0]
            )
            lines[0, t * NZ:(t + 1) * NZ] = widened(left + right, 1)
            lines[1, t * NZ:(t + 1) * NZ] = widened(left - right, 1)
        for parity in range(2):
            mid[parity, :4 * NZ] = dot(lines[parity], half_row[0, parity])

    def masked(t):
        at = pl.ds(t * NZ, NZ)
        even, odd = mid[0, at], mid[1, at]
        mirror = jnp.concatenate([
            jnp.concatenate([even[:, :NY // 2], odd[:, :NY // 2]], axis=1),
            jnp.concatenate([even[:, NY // 2:], odd[:, NY // 2:]], axis=1),
        ], axis=0)
        w = weight[2]
        return cols(mirror, col, 0) * jnp.concatenate([w, w], axis=0)

    def publish(n):
        plane = fields.at[n, 1 + c, y]
        for step in (1, 2, 3):
            send(plane, plane, along_send.at[n], along_recv.at[n], at_y(step))

    def near_copy(n, which):
        mine = fields.at[n, 1 + c, y]
        target, device = ((mine, sibling), (fields.at[n, 3 - 3 * c, y], across))[which]
        return remote(mine, target, near_send.at[n, which], near_recv.at[n, which], device)

    def normal(n, energy):
        @pl.when(n == 1)
        def _():
            publish(0)
            near_copy(0, 0).start()
            near_copy(0, 1).start()
            arrived(turned, turn_recv)
            send(rest, rest, map_sib_send.at[1], map_sib_recv.at[1], sibling)

        @pl.when(n == 2)
        def _():
            arrived(rest, map_sib_recv.at[1])

        spread(rhs, n)
        for t in range(4):
            values = masked(t)
            energy = energy + fold(values * values)
            wave = cols(values, col, 1)
            at = pl.ds(pl.multiple_of((n * 4 + t) * HALF, 16), HALF)
            for parity, part_ in enumerate(by_parity(wave[:NZ], wave[NZ:])):
                for h in range(2):
                    wide[h, parity, at] = widened(part_[h * HALF:(h + 1) * HALF], 1)
        return energy

    def gather(h, carry):
        for parity in range(2):
            mid[parity] = dot(wide[h, parity], half_row[1, parity])
        at = half(h)

        def one(n, sums_):
            sum_re, sum_im = sums_
            for t in range(4):
                place = pl.ds(pl.multiple_of((n * 4 + t) * HALF, 16), HALF)
                slot, core = pair(2 * n + t // 2)
                sens_re, sens_im = maps[slot, core, t % 2, 0, at], maps[slot, core, t % 2, 1, at]
                even, odd = mid[0, place], mid[1, place]
                plus, minus = even + odd, even - odd
                wave_re = jnp.concatenate([plus[:, :NY // 2], minus[:, :NY // 2]], axis=1)
                wave_im = jnp.concatenate([plus[:, NY // 2:], minus[:, NY // 2:]], axis=1)
                sum_re += sens_re * wave_re + sens_im * wave_im
                sum_im += sens_re * wave_im - sens_im * wave_re
            return sum_re, sum_im

        none = jnp.zeros((HALF, NY), F32)
        to_z[1, 0, at], to_z[1, 1, at] = lax.fori_loop(0, 4, one, (none, none))
        second_z(h).start()
        return carry

    def forward(n, energy):
        spread(resid, n)
        for t in range(4):
            values = masked(t)
            energy = energy + fold(values * values)
        return energy

    def inner(left, right):
        return fold(left[0] * right[0] + left[1] * right[1])

    lane = lax.broadcasted_iota(jnp.int32, (1, 128), 1)

    def share(which, stage, peers, me):
        for peer in peers:
            send(message.at[which, stage], sums.at[which, stage, me],
                 sum_send.at[which, stage], sum_recv.at[which, stage], peer)
        sums[which, stage, me] = message[which, stage]

    def collect(which, stage, peers):
        lines = sums.at[which, stage, pl.ds(0, len(peers))]
        arrived(lines, sum_recv.at[which, stage])
        departed(lines, sum_send.at[which, stage])
        return jnp.sum(sums[which, stage, :len(peers) + 1], axis=0)

    def first_group(which):
        if which == 2:
            return near_peers, lax.rem(ring, 4) * 2 + c
        return column_peers, ring * 2 + c

    def reduce_start(which, parts):
        line = jnp.zeros((1, 128), F32)
        for n, value in enumerate(parts):
            line = jnp.where(lane == n, total(value), line)
        message[which, 0] = line
        share(which, 0, *first_group(which))

    def reduce_end(which, count, early, meanwhile):
        early()
        message[which, 1] = collect(which, 0, first_group(which)[0])
        share(which, 1, plane_peers, y * 4 + x)
        meanwhile()
        line = collect(which, 1, plane_peers)
        return [line[:, n:n + 1] for n in range(count)]

    def extend(n):
        near_copy(n, 1).wait_recv()
        plane = fields.at[n, 3 * c, y]
        for step in (1, 3):
            send(plane, plane, far_send.at[n], far_recv.at[n], at_y(step))

    def pass_on(n):
        arrived(fields.at[n, 1 + c, pl.ds(0, 3)], along_recv.at[n])
        facing = lax.rem(y + 2, 4)
        plane = fields.at[n, 1 + c, facing]
        send(plane, fields.at[n, 3 - 3 * c, facing], pass_send.at[n], pass_recv.at[n], across)
        for slot in (1, 2, 3):
            plane = fields.at[n, 1 + c, lax.rem(y + slot, 4)]
            send(plane, plane, core_send.at[n, 0], core_recv.at[n, 0], sibling)

    def hand_over(n):
        arrived(fields.at[n, 3 * c, pl.ds(0, 2)], far_recv.at[n])
        arrived(fields.at[n, 3 * c, 0], pass_recv.at[n])
        planes = fields.at[n, 3 * c]
        send(planes, planes, core_send.at[n, 1], core_recv.at[n, 1], sibling)

    def settle(n):
        arrived(fields.at[n, 2 - c, pl.ds(0, 3)], core_recv.at[n, 0])
        arrived(fields.at[n, 3 - 3 * c], core_recv.at[n, 1])

    def idle():
        pass

    def first_window():
        near_copy(1, 0).start()
        near_copy(0, 0).wait_recv()
        hand_over(0)

    def second_window():
        extend(1)
        pass_on(1)

    zero = jnp.zeros((8, 128), F32)
    arrived(maps.at[0, c], map_sib_recv.at[0])
    for r in range(CHUNKS):
        at = chunk(r)
        first_z(r).wait_recv()
        rhs[:, at] = to_z[0, :, at] + from_z[0, :, at]
    energy = lax.fori_loop(0, 4, normal, zero)
    reduce_start(0, [0.5 * inner(rhs, rhs), energy])
    lax.fori_loop(0, 2, gather, 0)
    norm_0, energy_0 = reduce_end(0, 2, idle, idle)
    extend(0)
    pass_on(0)
    curve_0 = energy_0 + 0.1 * norm_0
    alpha_0 = norm_0 / curve_0
    for h in range(2):
        at = half(h)
        second_z(h).wait_recv()
        quad[:, at] = to_z[1, :, at] + from_z[1, :, at] + 0.1 * rhs[:, at]
        resid[:, at] = rhs[:, at] - alpha_0 * quad[:, at]
    publish(1)
    near_copy(1, 1).start()
    energy = lax.fori_loop(0, 4, forward, zero)
    reduce_start(1, [0.5 * inner(resid, resid), 0.5 * inner(resid, quad), energy])
    norm_1, cross, energy_1 = reduce_end(1, 3, first_window, second_window)
    beta = norm_1 / norm_0
    curve_1 = energy_1 + 0.1 * norm_1 + 2.0 * beta * cross + beta * beta * curve_0
    alpha_1 = norm_1 / curve_1
    on_rhs = alpha_0 + alpha_1 * beta
    near_copy(1, 0).wait_recv()

    def iterate(place, line):
        return on_rhs * fields[0, place, line] + alpha_1 * fields[1, place, line]

    def length(gap):
        return jnp.sqrt(gap[0] * gap[0] + gap[1] * gap[1])

    gap = jnp.where(2 * b + c < BINS - 1, iterate(2 + c, y) - iterate(1 + c, y), 0.0)
    reduce_start(2, [fold(length(gap))])

    def differences(line, carry):
        values = [iterate(place, line) for place in range(4)]
        result[line, 0] = values[1]
        result[line, 1] = values[2]
        for n, keep in enumerate((b > 0, None, b < BIN_AXIS - 1)):
            gap = values[n + 1] - values[n]
            if keep is not None:
                gap = jnp.where(keep, gap, 0.0)
            gaps[line, n] = gap
            sizes[line, n] = 1.0 / length(gap)
        return carry

    def prepare():
        settle(0)
        settle(1)
        lax.fori_loop(0, SL, differences, 0)

    (size_sum,) = reduce_end(2, 1, lambda: hand_over(1), prepare)
    lam = size_sum / COUNT + 1e-06

    def out_copy(line):
        return pltpu.make_async_copy(result.at[line], out.at[:, line], out_sem.at[line])

    def finish(line, carry):
        dual = [
            gaps[line, n] * jnp.minimum(lam * sizes[line, n], 1.0)[None] for n in range(3)
        ]
        for n in range(2):
            result[line, n] = result[line, n] + 0.25 * (dual[n + 1] - dual[n])
        out_copy(line).start()
        return carry

    lax.fori_loop(0, SL, finish, 0)
    for k in range(4):
        sib_copy(k).wait_send()
    departed(slots, map_send)
    departed(turned, turn_send)
    departed(maps.at[0, c], map_sib_send.at[0])
    departed(rest, map_sib_send.at[1])
    departed(to_y, y_send)
    for n in range(2):
        departed(to_z.at[n], z_send.at[n])
        near_copy(n, 0).wait_send()
        near_copy(n, 1).wait_send()
        departed(fields.at[n, 1 + c, pl.ds(0, 3)], along_send.at[n])
        departed(fields.at[n, 3 * c, pl.ds(0, 2)], far_send.at[n])
        departed(fields.at[n, 1 + c, 0], pass_send.at[n])
        departed(fields.at[n, 1 + c, pl.ds(0, 3)], core_send.at[n, 0])
        departed(fields.at[n, 3 * c], core_send.at[n, 1])
    for line in range(SL):
        out_copy(line).wait()


def on_device(kspace, coil_maps, sample_mask):
    dma = pltpu.SemaphoreType.DMA
    whole = pl.BlockSpec(memory_space=pl.ANY)
    return pl.pallas_call(
        kernel,
        out_shape=jax.ShapeDtypeStruct((2, SL) + PLANE, F32),
        in_specs=[whole] * 7,
        out_specs=whole,
        scratch_shapes=[
            pltpu.VMEM((4, 2, 2) + PLANE, F32),
            pltpu.VMEM((2, SL) + PLANE, F32),
            pltpu.VMEM(PLANE, jnp.int32),
            pltpu.VMEM((2, 2 * NY, 2 * NY), BF16),
            pltpu.VMEM((2, 2 * NZ, 6 * NZ), BF16),
            pltpu.VMEM((2, 2, 3 * NY, NY), BF16),
            pltpu.VMEM((NY, NY), BF16),
            pltpu.VMEM((4, 2, 2) + PLANE, F32),
            pltpu.VMEM((3, NZ, NY), F32),
            pltpu.VMEM((4 * NZ, 2 * NY), BF16),
            pltpu.VMEM((4 * NZ, 2 * NY), BF16),
            pltpu.VMEM((4 * NZ, 2 * NY), F32),
            pltpu.VMEM((2, 4 * NZ, 3 * NY), BF16),
            pltpu.VMEM((2, 2, 16 * HALF, 3 * NY), BF16),
            pltpu.VMEM((2, 16 * HALF, NY), F32),
            pltpu.VMEM((4, 2) + PLANE, F32),
            pltpu.VMEM((4,) + PLANE, F32),
            pltpu.VMEM((3,) + PLANE, F32),
            pltpu.VMEM((3,) + PLANE, F32),
            pltpu.VMEM((2,) + PLANE, F32),
            pltpu.VMEM((2,) + PLANE, F32),
            pltpu.VMEM((2, 4, SL) + PLANE, F32),
            pltpu.VMEM(PLANE, F32),
            pltpu.VMEM((SL, 3) + PLANE, F32),
            pltpu.VMEM((SL, 3, NZ, NY), F32),
            pltpu.VMEM((SL, 2) + PLANE, F32),
            pltpu.VMEM((3, 2, 1, 128), F32),
            pltpu.VMEM((3, 2, 16, 1, 128), F32),
            dma((6,)), dma((4,)), dma(()),
            dma(()), dma(()), dma(()), dma(()), dma((2,)), dma((2,)),
            dma((4,)), dma((4,)), dma(()), dma((CHUNKS,)), dma((2,)), dma((CHUNKS + 2,)),
            dma((2, 2)), dma((2, 2)), dma((2,)), dma((2,)),
            dma((2,)), dma((2,)), dma((2,)), dma((2,)), dma((2, 2)), dma((2, 2)),
            dma((3, 2)), dma((3, 2)), dma((SL,)),
        ],
        compiler_params=pltpu.CompilerParams(
            collective_id=0, has_side_effects=True, vmem_limit_bytes=60 * 1024 * 1024
        ),
        cost_estimate=pl.CostEstimate(flops=20_000_000_000, bytes_accessed=10_000_000, transcendentals=0),
    )(
        kspace, coil_maps, sample_mask, jnp.asarray(row_tables()), jnp.asarray(col_tables()),
        jnp.asarray(parity_tables()), jnp.asarray(parity_order()),
    )


def solution(mesh):
    return jax.shard_map(
        on_device,
        mesh=mesh,
        in_specs=(
            P("bin", "coil", None, None, None, None),
            P("coil", None, None, None, None),
            P("bin", None, None),
        ),
        out_specs=P("bin", None, None, None, None),
        check_vma=False,
    )
```

```python
import math

import jax
import jax.numpy as jnp
import numpy as np
from jax import lax
from jax.experimental import pallas as pl
from jax.experimental.pallas import tpu as pltpu
from jax.sharding import PartitionSpec as P

MESH = pl.DeviceIdType.MESH
F32 = jnp.float32
BF16 = jnp.bfloat16
NZ, NY, SL = 96, 256, 4
BIN_AXIS, COIL_AXIS = 16, 16
BINS = 32
COUNT = (BINS - 1) * SL * NZ * NY
PLANE = (2, NZ, NY)
HALF = NZ // 2
EDGES = (0, 32, 64, 96)
CHUNKS = len(EDGES) - 1


def dft_tables(length):
    index = np.arange(length)
    angle = (index[:, None] * index[None, :] % length) * (2.0 * math.pi / length)
    factor = 1.0 / math.sqrt(length)
    return np.cos(angle) * factor, np.sin(angle) * factor


def halves(table):
    high = table.astype(np.float32).astype(jnp.bfloat16)
    low = (table - high.astype(np.float64)).astype(np.float32).astype(jnp.bfloat16)
    return np.stack([high, low])


def row_tables():
    cos, sin = dft_tables(NY)
    return halves(np.block([[cos, sin], [-sin, cos]]))


def stacked(table, axis):
    high, low = halves(table)
    return np.concatenate([high, high, low], axis=axis)


def parity_tables():
    cos, sin = dft_tables(NY)
    tables = []
    for parity in range(2):
        part = (slice(0, NY // 2), slice(parity, None, 2))
        tables.append(np.block([[cos[part], -sin[part]], [sin[part], cos[part]]]))
    return np.stack([
        np.stack([stacked(table, 0) for table in tables]),
        np.stack([stacked(table.T, 0) for table in tables]),
    ])


def col_tables():
    cos, sin = dft_tables(NZ)
    forward = np.block([[cos, sin], [-sin, cos]])
    return np.stack([stacked(forward, 1), stacked(forward.T, 1)])


def parity_order():
    order = np.concatenate([np.arange(0, NY, 2), np.arange(1, NY, 2)])
    return np.eye(NY)[:, order].astype(jnp.bfloat16)


def split(values):
    high = values.astype(BF16)
    return high, (values - high.astype(F32)).astype(BF16)


def widened(values, axis):
    high, low = split(values)
    return jnp.concatenate([high, low, high], axis=axis)


def dot(left, right):
    return jnp.dot(left, right, preferred_element_type=F32)


def rows(high, low, table):
    return dot(high, table[0]) + dot(low, table[0]) + dot(high, table[1])


def cols(values, table, which):
    return dot(table[which], widened(values, 0))


def by_parity(real, imag):
    return [
        jnp.concatenate([real[:, part], imag[:, part]], axis=1)
        for part in (slice(0, NY // 2), slice(NY // 2, NY))
    ]


def fold(values):
    part = jnp.sum(values.reshape(values.shape[0] // 8, 8, NY), axis=0)
    return part[:, :128] + part[:, 128:]


def total(values):
    return jnp.sum(values, keepdims=True)


def kernel(
    kspace, coil_maps, mask, row_table, col_table, parity_table, order_table, out,
    samples, own_maps, ticks, row, col, half_row, order, maps, weight, lines_high, lines_low, first, lines, spectra, wide, mid,
    part, from_sib, to_y, from_y, to_z, from_z,
    fields, quad, gaps, sizes, result, message, sums,
    load_sem, sample_sem, slot_sem,
    map_send, map_recv, turn_send, turn_recv, map_sib_send, map_sib_recv,
    sib_send, sib_recv, y_send, y_recv, z_send, z_recv,
    near_send, near_recv, along_send, along_recv, pass_send, pass_recv, far_send, far_recv, core_send, core_recv,
    sum_send, sum_recv, out_sem,
):
    b = lax.axis_index("bin")
    j = lax.axis_index("coil")
    y, z, c = j // 4, (j // 2) % 2, j % 2
    x = lax.rem(b, 4)
    ring = z * 4 + b // 4

    def at_y(step):
        return (b, lax.rem(y + step, 4) * 4 + z * 2 + c)

    def at_xz(step_x, step_z, core):
        place = lax.rem(ring + step_z + 8, 8)
        return (
            lax.rem(place, 4) * 4 + lax.rem(x + step_x + 4, 4),
            y * 4 + place // 4 * 2 + core,
        )

    rhs = fields.at[0, 1 + c, y]
    resid = fields.at[1, 1 + c, y]
    sibling = (b, j + 1 - 2 * c)
    opposite = (b, j + 2 - 4 * z)
    wraps = jnp.where(c == 1, jnp.where(x == 3, 1, 0), jnp.where(x == 0, -1, 0))
    across = at_xz(2 * c - 1, wraps, 1 - c)
    column_peers = [at_xz(0, step // 2, lax.rem(c + step, 2)) for step in range(1, 16)]
    near_peers = [
        at_xz(0, dz, core) for dz in (0, 1, 2, -1) for core in (c, 1 - c)
    ][1:]
    plane_peers = [
        (b - x + lax.rem(x + step % 4, 4), lax.rem(y + step // 4, 4) * 4 + z * 2 + c) for step in range(1, 16)
    ]

    def remote(source, target, send_sem, recv_sem, device):
        return pltpu.make_async_remote_copy(
            src_ref=source, dst_ref=target, send_sem=send_sem, recv_sem=recv_sem,
            device_id=device, device_id_type=MESH,
        )

    def send(*args):
        copy = remote(*args)
        copy.start()
        return copy

    def arrived(ref, sem):
        remote(ref, ref, sem, sem, sibling).wait_recv()

    def departed(ref, sem):
        remote(ref, ref, sem, sem, sibling).wait_send()

    def load(source, target, sem):
        copy = pltpu.make_async_copy(source, target, sem)
        copy.start()
        return copy

    def sample_copy(k):
        return pltpu.make_async_copy(
            kspace.at[:, :, lax.rem(y + 3 - k, 4)], samples.at[k], sample_sem.at[k]
        )

    barrier = pltpu.get_barrier_semaphore()
    greeted = column_peers + plane_peers + [across]
    for device in greeted:
        pl.semaphore_signal(barrier, inc=1, device_id=device, device_id_type=MESH)
    loads = [load(mask, ticks, load_sem.at[0]), load(row_table, row, load_sem.at[1])]
    sample_copy(0).start()
    loads += [load(col_table, col, load_sem.at[2]), load(coil_maps, own_maps, load_sem.at[3]), load(order_table, order, load_sem.at[5])]
    for k in (1, 2, 3):
        sample_copy(k).start()
    late_load = load(parity_table, half_row, load_sem.at[4])
    slot_copy = load(coil_maps.at[:, y], maps.at[0, c], slot_sem)
    loads[0].wait()
    weight[0] = ticks[0].astype(F32)
    weight[1] = ticks[1].astype(F32)
    for copy in loads[1:]:
        copy.wait()
    weight[2] = dot(weight[c].astype(BF16), order[...])

    def half(h):
        return pl.ds(pl.multiple_of(h * HALF, 16), HALF)

    def sib_copy(k):
        return remote(part.at[k, 1 - c], from_sib.at[k], sib_send.at[k], sib_recv.at[k], sibling)

    def chunk(r):
        return pl.ds(EDGES[r], EDGES[r + 1] - EDGES[r])

    def y_start(r):
        for k in range(3):
            send(to_y.at[k, :, chunk(r)], from_y.at[k, :, chunk(r)], y_send, y_recv.at[r], at_y(3 - k))

    def first_z(r):
        return remote(
            to_z.at[0, :, chunk(r)], from_z.at[0, :, chunk(r)], z_send.at[0], z_recv.at[r], opposite
        )

    def second_z(h):
        return remote(
            to_z.at[1, :, half(h)], from_z.at[1, :, half(h)], z_send.at[1], z_recv.at[CHUNKS + h], opposite
        )

    def adjoint(k, carry):
        s = lax.rem(y + 3 - k, 4)
        sample_copy(k).wait()
        for t in range(4):
            w = weight[t // 2]
            values = jnp.concatenate(
                [samples[k, t // 2, t % 2, 0] * w, samples[k, t // 2, t % 2, 1] * w], axis=1
            )
            lines_high[t * NZ:(t + 1) * NZ], lines_low[t * NZ:(t + 1) * NZ] = split(values)
        first[...] = rows(lines_high[...], lines_low[...], row)
        for bin_ in range(2):
            sum_re, sum_im = 0.0, 0.0
            for coil in range(2):
                at = pl.ds((bin_ * 2 + coil) * NZ, NZ)
                wave = cols(jnp.concatenate([first[at, :NY], first[at, NY:]], axis=0), col, 1)
                sens_re, sens_im = own_maps[coil, s, 0], own_maps[coil, s, 1]
                sum_re += sens_re * wave[:NZ] + sens_im * wave[NZ:]
                sum_im += sens_re * wave[NZ:] - sens_im * wave[:NZ]
            part[k, bin_, 0] = sum_re
            part[k, bin_, 1] = sum_im
        return carry

    lax.fori_loop(0, 4, adjoint, 0)
    pl.semaphore_wait(barrier, len(greeted))
    for k in range(4):
        sib_copy(k).start()
    quarter = pl.ds(pl.multiple_of(x * (NZ // 4), 8), NZ // 4)
    for step in (1, 2, 3):
        send(coil_maps.at[:, lax.rem(y + step, 4), :, quarter], maps.at[4 - step, c, :, :, quarter],
             map_send, map_recv, at_y(step))
    for k in range(3):
        sib_copy(k).wait_recv()
        to_y[k] = part[k, c] + from_sib[k]
    y_start(0)
    send(own_maps.at[:, y], maps.at[0, c], map_sib_send.at[0], map_sib_recv.at[0], sibling)
    slots = maps.at[pl.ds(1, 3), c, :, :, quarter]
    sib_copy(3).wait_recv()
    part[3, c] = part[3, c] + from_sib[3]
    arrived(slots, map_recv)
    for step in (1, 2, 3):
        send(slots, slots, turn_send, turn_recv, at_xz(step, 0, c))
    y_start(1)
    for r in range(CHUNKS):
        at = chunk(r)
        arrived(from_y.at[:, :, at], y_recv.at[r])
        if r + 2 < CHUNKS:
            y_start(r + 2)
        to_z[0, :, at] = part[3, c, :, at] + from_y[0, :, at] + from_y[1, :, at] + from_y[2, :, at]
        first_z(r).start()
    turned = maps.at[pl.ds(1, 3), c, :, :, pl.ds(0, 3 * (NZ // 4))]
    rest = maps.at[pl.ds(1, 3), c]
    slot_copy.wait()
    late_load.wait()

    def pair(n):
        late = n - 2
        slot = jnp.where(n < 2, 0, 1 + lax.rem(late + 3, 3))
        flip = jnp.where(n < 2, n, jnp.where(late < 3, 0, 1))
        return slot, lax.rem(c + flip, 2)

    def spread(field, n):
        for t in range(4):
            slot, core = pair(2 * n + t // 2)
            sens_re, sens_im = maps[slot, core, t % 2, 0], maps[slot, core, t % 2, 1]
            left, right = by_parity(
                sens_re * field[0] - sens_im * field[1], sens_re * field[1] + sens_im * field[0]
            )
            lines[0, t * NZ:(t + 1) * NZ] = widened(left + right, 1)
            lines[1, t * NZ:(t + 1) * NZ] = widened(left - right, 1)
        for parity in range(2):
            mid[parity, :4 * NZ] = dot(lines[parity], half_row[0, parity])

    def masked(t):
        at = pl.ds(t * NZ, NZ)
        even, odd = mid[0, at], mid[1, at]
        mirror = jnp.concatenate([
            jnp.concatenate([even[:, :NY // 2], odd[:, :NY // 2]], axis=1),
            jnp.concatenate([even[:, NY // 2:], odd[:, NY // 2:]], axis=1),
        ], axis=0)
        w = weight[2]
        return cols(mirror, col, 0) * jnp.concatenate([w, w], axis=0)

    def publish(n):
        plane = fields.at[n, 1 + c, y]
        for step in (1, 2, 3):
            send(plane, plane, along_send.at[n], along_recv.at[n], at_y(step))

    def near_copy(n, which):
        mine = fields.at[n, 1 + c, y]
        target, device = ((mine, sibling), (fields.at[n, 3 - 3 * c, y], across))[which]
        return remote(mine, target, near_send.at[n, which], near_recv.at[n, which], device)

    def normal(n, energy):
        @pl.when(n == 1)
        def _():
            publish(0)
            near_copy(0, 0).start()
            near_copy(0, 1).start()
            arrived(turned, turn_recv)
            send(rest, rest, map_sib_send.at[1], map_sib_recv.at[1], sibling)

        @pl.when(n == 2)
        def _():
            arrived(rest, map_sib_recv.at[1])

        spread(rhs, n)
        for t in range(4):
            values = masked(t)
            energy = energy + fold(values * values)
            spectra[n * 4 + t] = values
        return energy

    def back(n, carry):
        for t in range(4):
            wave = cols(spectra[n * 4 + t], col, 1)
            at = pl.ds(pl.multiple_of((n * 4 + t) * HALF, 16), HALF)
            for parity, part_ in enumerate(by_parity(wave[:NZ], wave[NZ:])):
                for h in range(2):
                    wide[h, parity, at] = widened(part_[h * HALF:(h + 1) * HALF], 1)
        return carry

    def gather(h, carry):
        for parity in range(2):
            mid[parity] = dot(wide[h, parity], half_row[1, parity])
        at = half(h)

        def one(n, sums_):
            sum_re, sum_im = sums_
            for t in range(4):
                place = pl.ds(pl.multiple_of((n * 4 + t) * HALF, 16), HALF)
                slot, core = pair(2 * n + t // 2)
                sens_re, sens_im = maps[slot, core, t % 2, 0, at], maps[slot, core, t % 2, 1, at]
                even, odd = mid[0, place], mid[1, place]
                plus, minus = even + odd, even - odd
                wave_re = jnp.concatenate([plus[:, :NY // 2], minus[:, :NY // 2]], axis=1)
                wave_im = jnp.concatenate([plus[:, NY // 2:], minus[:, NY // 2:]], axis=1)
                sum_re += sens_re * wave_re + sens_im * wave_im
                sum_im += sens_re * wave_im - sens_im * wave_re
            return sum_re, sum_im

        none = jnp.zeros((HALF, NY), F32)
        to_z[1, 0, at], to_z[1, 1, at] = lax.fori_loop(0, 4, one, (none, none))
        second_z(h).start()
        return carry

    def forward(n, energy):
        spread(resid, n)
        for t in range(4):
            values = masked(t)
            energy = energy + fold(values * values)
        return energy

    def inner(left, right):
        return fold(left[0] * right[0] + left[1] * right[1])

    lane = lax.broadcasted_iota(jnp.int32, (1, 128), 1)

    def share(which, stage, peers, me):
        for peer in peers:
            send(message.at[which, stage], sums.at[which, stage, me],
                 sum_send.at[which, stage], sum_recv.at[which, stage], peer)
        sums[which, stage, me] = message[which, stage]

    def collect(which, stage, peers):
        lines = sums.at[which, stage, pl.ds(0, len(peers))]
        arrived(lines, sum_recv.at[which, stage])
        departed(lines, sum_send.at[which, stage])
        return jnp.sum(sums[which, stage, :len(peers) + 1], axis=0)

    def first_group(which):
        if which == 2:
            return near_peers, lax.rem(ring, 4) * 2 + c
        return column_peers, ring * 2 + c

    def reduce_start(which, parts):
        line = jnp.zeros((1, 128), F32)
        for n, value in enumerate(parts):
            line = jnp.where(lane == n, total(value), line)
        message[which, 0] = line
        share(which, 0, *first_group(which))

    def reduce_end(which, count, early, meanwhile):
        early()
        message[which, 1] = collect(which, 0, first_group(which)[0])
        share(which, 1, plane_peers, y * 4 + x)
        meanwhile()
        line = collect(which, 1, plane_peers)
        return [line[:, n:n + 1] for n in range(count)]

    def extend(n):
        near_copy(n, 1).wait_recv()
        plane = fields.at[n, 3 * c, y]
        for step in (1, 3):
            send(plane, plane, far_send.at[n], far_recv.at[n], at_y(step))

    def pass_on(n):
        arrived(fields.at[n, 1 + c, pl.ds(0, 3)], along_recv.at[n])
        facing = lax.rem(y + 2, 4)
        plane = fields.at[n, 1 + c, facing]
        send(plane, fields.at[n, 3 - 3 * c, facing], pass_send.at[n], pass_recv.at[n], across)
        for slot in (1, 2, 3):
            plane = fields.at[n, 1 + c, lax.rem(y + slot, 4)]
            send(plane, plane, core_send.at[n, 0], core_recv.at[n, 0], sibling)

    def hand_over(n):
        arrived(fields.at[n, 3 * c, pl.ds(0, 2)], far_recv.at[n])
        arrived(fields.at[n, 3 * c, 0], pass_recv.at[n])
        planes = fields.at[n, 3 * c]
        send(planes, planes, core_send.at[n, 1], core_recv.at[n, 1], sibling)

    def settle(n):
        arrived(fields.at[n, 2 - c, pl.ds(0, 3)], core_recv.at[n, 0])
        arrived(fields.at[n, 3 - 3 * c], core_recv.at[n, 1])

    def idle():
        pass

    def first_window():
        near_copy(1, 0).start()
        near_copy(0, 0).wait_recv()
        hand_over(0)

    def second_window():
        extend(1)
        pass_on(1)

    zero = jnp.zeros((8, 128), F32)
    arrived(maps.at[0, c], map_sib_recv.at[0])
    for r in range(CHUNKS):
        at = chunk(r)
        first_z(r).wait_recv()
        rhs[:, at] = to_z[0, :, at] + from_z[0, :, at]
    energy = lax.fori_loop(0, 4, normal, zero)
    reduce_start(0, [0.5 * inner(rhs, rhs), energy])
    lax.fori_loop(0, 4, back, 0)
    lax.fori_loop(0, 2, gather, 0)
    norm_0, energy_0 = reduce_end(0, 2, idle, idle)
    extend(0)
    pass_on(0)
    curve_0 = energy_0 + 0.1 * norm_0
    alpha_0 = norm_0 / curve_0
    for h in range(2):
        at = half(h)
        second_z(h).wait_recv()
        quad[:, at] = to_z[1, :, at] + from_z[1, :, at] + 0.1 * rhs[:, at]
        resid[:, at] = rhs[:, at] - alpha_0 * quad[:, at]
    publish(1)
    near_copy(1, 1).start()
    energy = lax.fori_loop(0, 4, forward, zero)
    reduce_start(1, [0.5 * inner(resid, resid), 0.5 * inner(resid, quad), energy])
    norm_1, cross, energy_1 = reduce_end(1, 3, first_window, second_window)
    beta = norm_1 / norm_0
    curve_1 = energy_1 + 0.1 * norm_1 + 2.0 * beta * cross + beta * beta * curve_0
    alpha_1 = norm_1 / curve_1
    on_rhs = alpha_0 + alpha_1 * beta
    near_copy(1, 0).wait_recv()

    def iterate(place, line):
        return on_rhs * fields[0, place, line] + alpha_1 * fields[1, place, line]

    def length(gap):
        return jnp.sqrt(gap[0] * gap[0] + gap[1] * gap[1])

    gap = jnp.where(2 * b + c < BINS - 1, iterate(2 + c, y) - iterate(1 + c, y), 0.0)
    reduce_start(2, [fold(length(gap))])

    def differences(line, carry):
        values = [iterate(place, line) for place in range(4)]
        result[line, 0] = values[1]
        result[line, 1] = values[2]
        for n, keep in enumerate((b > 0, None, b < BIN_AXIS - 1)):
            gap = values[n + 1] - values[n]
            if keep is not None:
                gap = jnp.where(keep, gap, 0.0)
            gaps[line, n] = gap
            sizes[line, n] = 1.0 / length(gap)
        return carry

    def prepare():
        settle(0)
        settle(1)
        lax.fori_loop(0, SL, differences, 0)

    (size_sum,) = reduce_end(2, 1, lambda: hand_over(1), prepare)
    lam = size_sum / COUNT + 1e-06

    def out_copy(line):
        return pltpu.make_async_copy(result.at[line], out.at[:, line], out_sem.at[line])

    def finish(line, carry):
        dual = [
            gaps[line, n] * jnp.minimum(lam * sizes[line, n], 1.0)[None] for n in range(3)
        ]
        for n in range(2):
            result[line, n] = result[line, n] + 0.25 * (dual[n + 1] - dual[n])
        out_copy(line).start()
        return carry

    lax.fori_loop(0, SL, finish, 0)
    for k in range(4):
        sib_copy(k).wait_send()
    departed(slots, map_send)
    departed(turned, turn_send)
    departed(maps.at[0, c], map_sib_send.at[0])
    departed(rest, map_sib_send.at[1])
    departed(to_y, y_send)
    for n in range(2):
        departed(to_z.at[n], z_send.at[n])
        near_copy(n, 0).wait_send()
        near_copy(n, 1).wait_send()
        departed(fields.at[n, 1 + c, pl.ds(0, 3)], along_send.at[n])
        departed(fields.at[n, 3 * c, pl.ds(0, 2)], far_send.at[n])
        departed(fields.at[n, 1 + c, 0], pass_send.at[n])
        departed(fields.at[n, 1 + c, pl.ds(0, 3)], core_send.at[n, 0])
        departed(fields.at[n, 3 * c], core_send.at[n, 1])
    for line in range(SL):
        out_copy(line).wait()


def on_device(kspace, coil_maps, sample_mask):
    dma = pltpu.SemaphoreType.DMA
    whole = pl.BlockSpec(memory_space=pl.ANY)
    return pl.pallas_call(
        kernel,
        out_shape=jax.ShapeDtypeStruct((2, SL) + PLANE, F32),
        in_specs=[whole] * 7,
        out_specs=whole,
        scratch_shapes=[
            pltpu.VMEM((4, 2, 2) + PLANE, F32),
            pltpu.VMEM((2, SL) + PLANE, F32),
            pltpu.VMEM(PLANE, jnp.int32),
            pltpu.VMEM((2, 2 * NY, 2 * NY), BF16),
            pltpu.VMEM((2, 2 * NZ, 6 * NZ), BF16),
            pltpu.VMEM((2, 2, 3 * NY, NY), BF16),
            pltpu.VMEM((NY, NY), BF16),
            pltpu.VMEM((4, 2, 2) + PLANE, F32),
            pltpu.VMEM((3, NZ, NY), F32),
            pltpu.VMEM((4 * NZ, 2 * NY), BF16),
            pltpu.VMEM((4 * NZ, 2 * NY), BF16),
            pltpu.VMEM((4 * NZ, 2 * NY), F32),
            pltpu.VMEM((2, 4 * NZ, 3 * NY), BF16),
            pltpu.VMEM((16, 2 * NZ, NY), F32),
            pltpu.VMEM((2, 2, 16 * HALF, 3 * NY), BF16),
            pltpu.VMEM((2, 16 * HALF, NY), F32),
            pltpu.VMEM((4, 2) + PLANE, F32),
            pltpu.VMEM((4,) + PLANE, F32),
            pltpu.VMEM((3,) + PLANE, F32),
            pltpu.VMEM((3,) + PLANE, F32),
            pltpu.VMEM((2,) + PLANE, F32),
            pltpu.VMEM((2,) + PLANE, F32),
            pltpu.VMEM((2, 4, SL) + PLANE, F32),
            pltpu.VMEM(PLANE, F32),
            pltpu.VMEM((SL, 3) + PLANE, F32),
            pltpu.VMEM((SL, 3, NZ, NY), F32),
            pltpu.VMEM((SL, 2) + PLANE, F32),
            pltpu.VMEM((3, 2, 1, 128), F32),
            pltpu.VMEM((3, 2, 16, 1, 128), F32),
            dma((6,)), dma((4,)), dma(()),
            dma(()), dma(()), dma(()), dma(()), dma((2,)), dma((2,)),
            dma((4,)), dma((4,)), dma(()), dma((CHUNKS,)), dma((2,)), dma((CHUNKS + 2,)),
            dma((2, 2)), dma((2, 2)), dma((2,)), dma((2,)),
            dma((2,)), dma((2,)), dma((2,)), dma((2,)), dma((2, 2)), dma((2, 2)),
            dma((3, 2)), dma((3, 2)), dma((SL,)),
        ],
        compiler_params=pltpu.CompilerParams(
            collective_id=0, has_side_effects=True, vmem_limit_bytes=60 * 1024 * 1024
        ),
        cost_estimate=pl.CostEstimate(flops=20_000_000_000, bytes_accessed=10_000_000, transcendentals=0),
    )(
        kspace, coil_maps, sample_mask, jnp.asarray(row_tables()), jnp.asarray(col_tables()),
        jnp.asarray(parity_tables()), jnp.asarray(parity_order()),
    )


def solution(mesh):
    return jax.shard_map(
        on_device,
        mesh=mesh,
        in_specs=(
            P("bin", "coil", None, None, None, None),
            P("coil", None, None, None, None),
            P("bin", None, None),
        ),
        out_specs=P("bin", None, None, None, None),
        check_vma=False,
    )
```

```python
import math

import jax
import jax.numpy as jnp
import numpy as np
from jax import lax
from jax.experimental import pallas as pl
from jax.experimental.pallas import tpu as pltpu
from jax.sharding import PartitionSpec as P

MESH = pl.DeviceIdType.MESH
F32 = jnp.float32
BF16 = jnp.bfloat16
NZ, NY, SL = 96, 256, 4
BIN_AXIS, COIL_AXIS = 16, 16
BINS = 32
COUNT = (BINS - 1) * SL * NZ * NY
PLANE = (2, NZ, NY)
HALF = NZ // 2
EDGES = (0, 32, 64, 96)
CHUNKS = len(EDGES) - 1


def dft_tables(length):
    index = np.arange(length)
    angle = (index[:, None] * index[None, :] % length) * (2.0 * math.pi / length)
    factor = 1.0 / math.sqrt(length)
    return np.cos(angle) * factor, np.sin(angle) * factor


def halves(table):
    high = table.astype(np.float32).astype(jnp.bfloat16)
    low = (table - high.astype(np.float64)).astype(np.float32).astype(jnp.bfloat16)
    return np.stack([high, low])


def row_tables():
    cos, sin = dft_tables(NY)
    return halves(np.block([[cos, sin], [-sin, cos]]))


def stacked(table, axis):
    high, low = halves(table)
    return np.concatenate([high, high, low], axis=axis)


def parity_tables():
    cos, sin = dft_tables(NY)
    tables = []
    for parity in range(2):
        part = (slice(0, NY // 2), slice(parity, None, 2))
        tables.append(np.block([[cos[part], -sin[part]], [sin[part], cos[part]]]))
    return np.stack([
        np.stack([stacked(table, 0) for table in tables]),
        np.stack([stacked(table.T, 0) for table in tables]),
    ])


def col_tables():
    cos, sin = dft_tables(NZ)
    forward = np.block([[cos, sin], [-sin, cos]])
    return np.stack([stacked(forward, 1), stacked(forward.T, 1)])


def parity_order():
    order = np.concatenate([np.arange(0, NY, 2), np.arange(1, NY, 2)])
    return np.eye(NY)[:, order].astype(jnp.bfloat16)


def split(values):
    high = values.astype(BF16)
    return high, (values - high.astype(F32)).astype(BF16)


def widened(values, axis):
    high, low = split(values)
    return jnp.concatenate([high, low, high], axis=axis)


def dot(left, right):
    return jnp.dot(left, right, preferred_element_type=F32)


def rows(high, low, table):
    return dot(high, table[0]) + dot(low, table[0]) + dot(high, table[1])


def cols(values, table, which):
    return dot(table[which], widened(values, 0))


def by_parity(real, imag):
    return [
        jnp.concatenate([real[:, part], imag[:, part]], axis=1)
        for part in (slice(0, NY // 2), slice(NY // 2, NY))
    ]


def fold(values):
    part = jnp.sum(values.reshape(values.shape[0] // 8, 8, NY), axis=0)
    return part[:, :128] + part[:, 128:]


def total(values):
    return jnp.sum(values, keepdims=True)


def kernel(
    kspace, coil_maps, mask, row_table, col_table, parity_table, order_table, out,
    samples, own_maps, ticks, row, col, half_row, order, maps, weight, lines_high, lines_low, first, lines, wide, mid,
    part, from_sib, to_y, from_y, to_z, from_z,
    fields, quad, gaps, sizes, result, message, sums,
    load_sem, sample_sem, slot_sem,
    map_send, map_recv, turn_send, turn_recv, map_sib_send, map_sib_recv,
    sib_send, sib_recv, y_send, y_recv, z_send, z_recv,
    near_send, near_recv, along_send, along_recv, pass_send, pass_recv, far_send, far_recv, core_send, core_recv,
    sum_send, sum_recv, out_sem,
):
    b = lax.axis_index("bin")
    j = lax.axis_index("coil")
    y, z, c = j // 4, (j // 2) % 2, j % 2
    x = lax.rem(b, 4)
    ring = z * 4 + b // 4

    def at_y(step):
        return (b, lax.rem(y + step, 4) * 4 + z * 2 + c)

    def at_xz(step_x, step_z, core):
        place = lax.rem(ring + step_z + 8, 8)
        return (
            lax.rem(place, 4) * 4 + lax.rem(x + step_x + 4, 4),
            y * 4 + place // 4 * 2 + core,
        )

    rhs = fields.at[0, 1 + c, y]
    resid = fields.at[1, 1 + c, y]
    sibling = (b, j + 1 - 2 * c)
    opposite = (b, j + 2 - 4 * z)
    wraps = jnp.where(c == 1, jnp.where(x == 3, 1, 0), jnp.where(x == 0, -1, 0))
    across = at_xz(2 * c - 1, wraps, 1 - c)
    column_peers = [at_xz(0, step // 2, lax.rem(c + step, 2)) for step in range(1, 16)]
    near_peers = [
        at_xz(0, dz, core) for dz in (0, 1, 2, -1) for core in (c, 1 - c)
    ][1:]
    plane_peers = [
        (b - x + lax.rem(x + step % 4, 4), lax.rem(y + step // 4, 4) * 4 + z * 2 + c) for step in range(1, 16)
    ]

    def remote(source, target, send_sem, recv_sem, device):
        return pltpu.make_async_remote_copy(
            src_ref=source, dst_ref=target, send_sem=send_sem, recv_sem=recv_sem,
            device_id=device, device_id_type=MESH,
        )

    def send(*args):
        copy = remote(*args)
        copy.start()
        return copy

    def arrived(ref, sem):
        remote(ref, ref, sem, sem, sibling).wait_recv()

    def departed(ref, sem):
        remote(ref, ref, sem, sem, sibling).wait_send()

    def load(source, target, sem):
        copy = pltpu.make_async_copy(source, target, sem)
        copy.start()
        return copy

    def sample_copy(k):
        return pltpu.make_async_copy(
            kspace.at[:, :, lax.rem(y + 3 - k, 4)], samples.at[k], sample_sem.at[k]
        )

    barrier = pltpu.get_barrier_semaphore()
    greeted = column_peers + plane_peers + [across]
    for device in greeted:
        pl.semaphore_signal(barrier, inc=1, device_id=device, device_id_type=MESH)
    loads = [load(mask, ticks, load_sem.at[0]), load(row_table, row, load_sem.at[1])]
    sample_copy(0).start()
    loads += [load(col_table, col, load_sem.at[2]), load(coil_maps, own_maps, load_sem.at[3]), load(order_table, order, load_sem.at[5])]
    for k in (1, 2, 3):
        sample_copy(k).start()
    late_load = load(parity_table, half_row, load_sem.at[4])
    slot_copy = load(coil_maps.at[:, y], maps.at[0, c], slot_sem)
    loads[0].wait()
    weight[0] = ticks[0].astype(F32)
    weight[1] = ticks[1].astype(F32)
    for copy in loads[1:]:
        copy.wait()
    weight[2] = dot(weight[c].astype(BF16), order[...])

    def half(h):
        return pl.ds(pl.multiple_of(h * HALF, 16), HALF)

    def sib_copy(k):
        return remote(part.at[k, 1 - c], from_sib.at[k], sib_send.at[k], sib_recv.at[k], sibling)

    def chunk(r):
        return pl.ds(EDGES[r], EDGES[r + 1] - EDGES[r])

    def y_start(r):
        for k in range(3):
            send(to_y.at[k, :, chunk(r)], from_y.at[k, :, chunk(r)], y_send, y_recv.at[r], at_y(3 - k))

    def first_z(r):
        return remote(
            to_z.at[0, :, chunk(r)], from_z.at[0, :, chunk(r)], z_send.at[0], z_recv.at[r], opposite
        )

    def second_z(h):
        return remote(
            to_z.at[1, :, half(h)], from_z.at[1, :, half(h)], z_send.at[1], z_recv.at[CHUNKS + h], opposite
        )

    def adjoint(k, carry):
        s = lax.rem(y + 3 - k, 4)
        sample_copy(k).wait()
        for t in range(4):
            w = weight[t // 2]
            values = jnp.concatenate(
                [samples[k, t // 2, t % 2, 0] * w, samples[k, t // 2, t % 2, 1] * w], axis=1
            )
            lines_high[t * NZ:(t + 1) * NZ], lines_low[t * NZ:(t + 1) * NZ] = split(values)
        first[...] = rows(lines_high[...], lines_low[...], row)
        for bin_ in range(2):
            sum_re, sum_im = 0.0, 0.0
            for coil in range(2):
                at = pl.ds((bin_ * 2 + coil) * NZ, NZ)
                wave = cols(jnp.concatenate([first[at, :NY], first[at, NY:]], axis=0), col, 1)
                sens_re, sens_im = own_maps[coil, s, 0], own_maps[coil, s, 1]
                sum_re += sens_re * wave[:NZ] + sens_im * wave[NZ:]
                sum_im += sens_re * wave[NZ:] - sens_im * wave[:NZ]
            part[k, bin_, 0] = sum_re
            part[k, bin_, 1] = sum_im
        return carry

    lax.fori_loop(0, 4, adjoint, 0)
    pl.semaphore_wait(barrier, len(greeted))
    for k in range(4):
        sib_copy(k).start()
    quarter = pl.ds(pl.multiple_of(x * (NZ // 4), 8), NZ // 4)
    for step in (1, 2, 3):
        send(coil_maps.at[:, lax.rem(y + step, 4), :, quarter], maps.at[4 - step, c, :, :, quarter],
             map_send, map_recv, at_y(step))
    for k in range(3):
        sib_copy(k).wait_recv()
        to_y[k] = part[k, c] + from_sib[k]
    y_start(0)
    send(own_maps.at[:, y], maps.at[0, c], map_sib_send.at[0], map_sib_recv.at[0], sibling)
    slots = maps.at[pl.ds(1, 3), c, :, :, quarter]
    sib_copy(3).wait_recv()
    part[3, c] = part[3, c] + from_sib[3]
    arrived(slots, map_recv)
    for step in (1, 2, 3):
        send(slots, slots, turn_send, turn_recv, at_xz(step, 0, c))
    y_start(1)
    for r in range(CHUNKS):
        at = chunk(r)
        arrived(from_y.at[:, :, at], y_recv.at[r])
        if r + 2 < CHUNKS:
            y_start(r + 2)
        to_z[0, :, at] = part[3, c, :, at] + from_y[0, :, at] + from_y[1, :, at] + from_y[2, :, at]
        first_z(r).start()
    turned = maps.at[pl.ds(1, 3), c, :, :, pl.ds(0, 3 * (NZ // 4))]
    rest = maps.at[pl.ds(1, 3), c]
    slot_copy.wait()
    late_load.wait()

    def pair(n):
        late = n - 2
        slot = jnp.where(n < 2, 0, 1 + lax.rem(late + 3, 3))
        flip = jnp.where(n < 2, n, jnp.where(late < 3, 0, 1))
        return slot, lax.rem(c + flip, 2)

    def spread(field, n):
        for t in range(4):
            slot, core = pair(2 * n + t // 2)
            sens_re, sens_im = maps[slot, core, t % 2, 0], maps[slot, core, t % 2, 1]
            left, right = by_parity(
                sens_re * field[0] - sens_im * field[1], sens_re * field[1] + sens_im * field[0]
            )
            lines[0, t * NZ:(t + 1) * NZ] = widened(left + right, 1)
            lines[1, t * NZ:(t + 1) * NZ] = widened(left - right, 1)
        for parity in range(2):
            mid[parity, :4 * NZ] = dot(lines[parity], half_row[0, parity])

    def masked(t):
        at = pl.ds(t * NZ, NZ)
        even, odd = mid[0, at], mid[1, at]
        mirror = jnp.concatenate([
            jnp.concatenate([even[:, :NY // 2], odd[:, :NY // 2]], axis=1),
            jnp.concatenate([even[:, NY // 2:], odd[:, NY // 2:]], axis=1),
        ], axis=0)
        w = weight[2]
        return cols(mirror, col, 0) * jnp.concatenate([w, w], axis=0)

    def publish(n):
        plane = fields.at[n, 1 + c, y]
        for step in (1, 2, 3):
            send(plane, plane, along_send.at[n], along_recv.at[n], at_y(step))

    def near_copy(n, which):
        mine = fields.at[n, 1 + c, y]
        target, device = ((mine, sibling), (fields.at[n, 3 - 3 * c, y], across))[which]
        return remote(mine, target, near_send.at[n, which], near_recv.at[n, which], device)

    def normal(n, energy):
        @pl.when(n == 1)
        def _():
            publish(0)
            near_copy(0, 0).start()
            near_copy(0, 1).start()
            arrived(turned, turn_recv)
            send(rest, rest, map_sib_send.at[1], map_sib_recv.at[1], sibling)

        @pl.when(n == 2)
        def _():
            arrived(rest, map_sib_recv.at[1])

        spread(rhs, n)
        for t in range(4):
            values = masked(t)
            energy = energy + fold(values * values)
            wave = cols(values, col, 1)
            at = pl.ds(pl.multiple_of((n * 4 + t) * HALF, 16), HALF)
            for parity, part_ in enumerate(by_parity(wave[:NZ], wave[NZ:])):
                for h in range(2):
                    wide[h, parity, at] = widened(part_[h * HALF:(h + 1) * HALF], 1)
        return energy

    def gather(h, carry):
        for parity in range(2):
            mid[parity] = dot(wide[h, parity], half_row[1, parity])
        at = half(h)

        def one(n, sums_):
            sum_re, sum_im = sums_
            for t in range(4):
                place = pl.ds(pl.multiple_of((n * 4 + t) * HALF, 16), HALF)
                slot, core = pair(2 * n + t // 2)
                sens_re, sens_im = maps[slot, core, t % 2, 0, at], maps[slot, core, t % 2, 1, at]
                even, odd = mid[0, place], mid[1, place]
                plus, minus = even + odd, even - odd
                wave_re = jnp.concatenate([plus[:, :NY // 2], minus[:, :NY // 2]], axis=1)
                wave_im = jnp.concatenate([plus[:, NY // 2:], minus[:, NY // 2:]], axis=1)
                sum_re += sens_re * wave_re + sens_im * wave_im
                sum_im += sens_re * wave_im - sens_im * wave_re
            return sum_re, sum_im

        none = jnp.zeros((HALF, NY), F32)
        to_z[1, 0, at], to_z[1, 1, at] = lax.fori_loop(0, 4, one, (none, none))
        second_z(h).start()
        return carry

    def forward(n, energy):
        spread(resid, n)
        for t in range(4):
            values = masked(t)
            energy = energy + fold(values * values)
        return energy

    def inner(left, right):
        return fold(left[0] * right[0] + left[1] * right[1])

    lane = lax.broadcasted_iota(jnp.int32, (1, 128), 1)

    def share(which, stage, peers, me):
        for peer in peers:
            send(message.at[which, stage], sums.at[which, stage, me],
                 sum_send.at[which, stage], sum_recv.at[which, stage], peer)
        sums[which, stage, me] = message[which, stage]

    def collect(which, stage, peers):
        lines = sums.at[which, stage, pl.ds(0, len(peers))]
        arrived(lines, sum_recv.at[which, stage])
        departed(lines, sum_send.at[which, stage])
        return jnp.sum(sums[which, stage, :len(peers) + 1], axis=0)

    def first_group(which):
        if which == 2:
            return near_peers, lax.rem(ring, 4) * 2 + c
        return column_peers, ring * 2 + c

    def reduce_start(which, parts):
        line = jnp.zeros((1, 128), F32)
        for n, value in enumerate(parts):
            line = jnp.where(lane == n, total(value), line)
        message[which, 0] = line
        share(which, 0, *first_group(which))

    def reduce_end(which, count, early, meanwhile):
        early()
        message[which, 1] = collect(which, 0, first_group(which)[0])
        share(which, 1, plane_peers, y * 4 + x)
        meanwhile()
        line = collect(which, 1, plane_peers)
        return [line[:, n:n + 1] for n in range(count)]

    def extend(n):
        near_copy(n, 1).wait_recv()
        plane = fields.at[n, 3 * c, y]
        for step in (1, 3):
            send(plane, plane, far_send.at[n], far_recv.at[n], at_y(step))

    def pass_on(n):
        arrived(fields.at[n, 1 + c, pl.ds(0, 3)], along_recv.at[n])
        facing = lax.rem(y + 2, 4)
        plane = fields.at[n, 1 + c, facing]
        send(plane, fields.at[n, 3 - 3 * c, facing], pass_send.at[n], pass_recv.at[n], across)
        for slot in (1, 2, 3):
            plane = fields.at[n, 1 + c, lax.rem(y + slot, 4)]
            send(plane, plane, core_send.at[n, 0], core_recv.at[n, 0], sibling)

    def hand_over(n):
        arrived(fields.at[n, 3 * c, pl.ds(0, 2)], far_recv.at[n])
        arrived(fields.at[n, 3 * c, 0], pass_recv.at[n])
        planes = fields.at[n, 3 * c]
        send(planes, planes, core_send.at[n, 1], core_recv.at[n, 1], sibling)

    def settle(n):
        arrived(fields.at[n, 2 - c, pl.ds(0, 3)], core_recv.at[n, 0])
        arrived(fields.at[n, 3 - 3 * c], core_recv.at[n, 1])

    def idle():
        pass

    def first_window():
        near_copy(1, 0).start()
        near_copy(0, 0).wait_recv()
        hand_over(0)

    def second_window():
        extend(1)
        pass_on(1)

    zero = jnp.zeros((8, 128), F32)
    arrived(maps.at[0, c], map_sib_recv.at[0])
    for r in range(CHUNKS):
        at = chunk(r)
        first_z(r).wait_recv()
        rhs[:, at] = to_z[0, :, at] + from_z[0, :, at]
    energy = lax.fori_loop(0, 4, normal, zero)
    reduce_start(0, [0.5 * inner(rhs, rhs), energy])
    lax.fori_loop(0, 2, gather, 0)
    norm_0, energy_0 = reduce_end(0, 2, idle, idle)
    extend(0)
    pass_on(0)
    curve_0 = energy_0 + 0.1 * norm_0
    alpha_0 = norm_0 / curve_0
    for h in range(2):
        at = half(h)
        second_z(h).wait_recv()
        quad[:, at] = to_z[1, :, at] + from_z[1, :, at] + 0.1 * rhs[:, at]
        resid[:, at] = rhs[:, at] - alpha_0 * quad[:, at]
    publish(1)
    near_copy(1, 1).start()
    energy = lax.fori_loop(0, 4, forward, zero)
    reduce_start(1, [0.5 * inner(resid, resid), 0.5 * inner(resid, quad), energy])
    norm_1, cross, energy_1 = reduce_end(1, 3, first_window, second_window)
    beta = norm_1 / norm_0
    curve_1 = energy_1 + 0.1 * norm_1 + 2.0 * beta * cross + beta * beta * curve_0
    alpha_1 = norm_1 / curve_1
    on_rhs = alpha_0 + alpha_1 * beta
    near_copy(1, 0).wait_recv()

    def iterate(place, line):
        return on_rhs * fields[0, place, line] + alpha_1 * fields[1, place, line]

    def length(gap):
        return jnp.sqrt(gap[0] * gap[0] + gap[1] * gap[1])

    gap = jnp.where(2 * b + c < BINS - 1, iterate(2 + c, y) - iterate(1 + c, y), 0.0)
    reduce_start(2, [fold(length(gap))])

    def differences(line, carry):
        values = [iterate(place, line) for place in range(4)]
        result[line, 0] = values[1]
        result[line, 1] = values[2]
        for n, keep in enumerate((b > 0, None, b < BIN_AXIS - 1)):
            gap = values[n + 1] - values[n]
            if keep is not None:
                gap = jnp.where(keep, gap, 0.0)
            gaps[line, n] = gap
            sizes[line, n] = 1.0 / length(gap)
        return carry

    def drain_first():
        for k in range(4):
            sib_copy(k).wait_send()
        departed(slots, map_send)
        departed(turned, turn_send)
        departed(maps.at[0, c], map_sib_send.at[0])
        departed(rest, map_sib_send.at[1])
        departed(to_y, y_send)

    def drain(n):
        departed(to_z.at[n], z_send.at[n])
        near_copy(n, 0).wait_send()
        near_copy(n, 1).wait_send()
        departed(fields.at[n, 1 + c, pl.ds(0, 3)], along_send.at[n])
        departed(fields.at[n, 3 * c, pl.ds(0, 2)], far_send.at[n])
        departed(fields.at[n, 1 + c, 0], pass_send.at[n])
        departed(fields.at[n, 1 + c, pl.ds(0, 3)], core_send.at[n, 0])
        departed(fields.at[n, 3 * c], core_send.at[n, 1])

    def third_window():
        hand_over(1)
        drain_first()
        drain(0)

    def prepare():
        settle(0)
        settle(1)
        lax.fori_loop(0, SL, differences, 0)

    (size_sum,) = reduce_end(2, 1, third_window, prepare)
    lam = size_sum / COUNT + 1e-06

    def out_copy(line):
        return pltpu.make_async_copy(result.at[line], out.at[:, line], out_sem.at[line])

    def finish(line, carry):
        dual = [
            gaps[line, n] * jnp.minimum(lam * sizes[line, n], 1.0)[None] for n in range(3)
        ]
        for n in range(2):
            result[line, n] = result[line, n] + 0.25 * (dual[n + 1] - dual[n])
        out_copy(line).start()
        return carry

    lax.fori_loop(0, SL, finish, 0)
    drain(1)
    for line in range(SL):
        out_copy(line).wait()


def on_device(kspace, coil_maps, sample_mask):
    dma = pltpu.SemaphoreType.DMA
    whole = pl.BlockSpec(memory_space=pl.ANY)
    return pl.pallas_call(
        kernel,
        out_shape=jax.ShapeDtypeStruct((2, SL) + PLANE, F32),
        in_specs=[whole] * 7,
        out_specs=whole,
        scratch_shapes=[
            pltpu.VMEM((4, 2, 2) + PLANE, F32),
            pltpu.VMEM((2, SL) + PLANE, F32),
            pltpu.VMEM(PLANE, jnp.int32),
            pltpu.VMEM((2, 2 * NY, 2 * NY), BF16),
            pltpu.VMEM((2, 2 * NZ, 6 * NZ), BF16),
            pltpu.VMEM((2, 2, 3 * NY, NY), BF16),
            pltpu.VMEM((NY, NY), BF16),
            pltpu.VMEM((4, 2, 2) + PLANE, F32),
            pltpu.VMEM((3, NZ, NY), F32),
            pltpu.VMEM((4 * NZ, 2 * NY), BF16),
            pltpu.VMEM((4 * NZ, 2 * NY), BF16),
            pltpu.VMEM((4 * NZ, 2 * NY), F32),
            pltpu.VMEM((2, 4 * NZ, 3 * NY), BF16),
            pltpu.VMEM((2, 2, 16 * HALF, 3 * NY), BF16),
            pltpu.VMEM((2, 16 * HALF, NY), F32),
            pltpu.VMEM((4, 2) + PLANE, F32),
            pltpu.VMEM((4,) + PLANE, F32),
            pltpu.VMEM((3,) + PLANE, F32),
            pltpu.VMEM((3,) + PLANE, F32),
            pltpu.VMEM((2,) + PLANE, F32),
            pltpu.VMEM((2,) + PLANE, F32),
            pltpu.VMEM((2, 4, SL) + PLANE, F32),
            pltpu.VMEM(PLANE, F32),
            pltpu.VMEM((SL, 3) + PLANE, F32),
            pltpu.VMEM((SL, 3, NZ, NY), F32),
            pltpu.VMEM((SL, 2) + PLANE, F32),
            pltpu.VMEM((3, 2, 1, 128), F32),
            pltpu.VMEM((3, 2, 16, 1, 128), F32),
            dma((6,)), dma((4,)), dma(()),
            dma(()), dma(()), dma(()), dma(()), dma((2,)), dma((2,)),
            dma((4,)), dma((4,)), dma(()), dma((CHUNKS,)), dma((2,)), dma((CHUNKS + 2,)),
            dma((2, 2)), dma((2, 2)), dma((2,)), dma((2,)),
            dma((2,)), dma((2,)), dma((2,)), dma((2,)), dma((2, 2)), dma((2, 2)),
            dma((3, 2)), dma((3, 2)), dma((SL,)),
        ],
        compiler_params=pltpu.CompilerParams(
            collective_id=0, has_side_effects=True, vmem_limit_bytes=60 * 1024 * 1024
        ),
        cost_estimate=pl.CostEstimate(flops=20_000_000_000, bytes_accessed=10_000_000, transcendentals=0),
    )(
        kspace, coil_maps, sample_mask, jnp.asarray(row_tables()), jnp.asarray(col_tables()),
        jnp.asarray(parity_tables()), jnp.asarray(parity_order()),
    )


def solution(mesh):
    return jax.shard_map(
        on_device,
        mesh=mesh,
        in_specs=(
            P("bin", "coil", None, None, None, None),
            P("coil", None, None, None, None),
            P("bin", None, None),
        ),
        out_specs=P("bin", None, None, None, None),
        check_vma=False,
    )
```
